128 devices in a mesh: scene: 4 (over y), tile: 32 (over x, z, core).
Axes of the slice: x: 4, y: 4, z: 4, core: 2. Of those that a mesh axis runs over, the one named last changes fastest.
Arguments:
- features: bfloat16 [128, 32, 64, 768], P(('scene', 'tile')), parts along dimension 0, may hold values from -120 to 120
- dw_kernel: bfloat16 [3, 3, 3, 768], replicated, may hold values from -2 to 2
- se_reduce: bfloat16 [3, 768, 192], replicated, may hold values from -0.21875 to 0.21875
- se_expand: bfloat16 [3, 192, 768], replicated, may hold values from -0.4375 to 0.4375
- mix_weight: bfloat16 [3, 768, 768], replicated, may hold values from -0.21875 to 0.21875
- norm_gain: float32 [768], replicated, may hold values from 0.5 to 2
- kv_weight: bfloat16 [768, 1536], replicated, may hold values from -0.21875 to 0.21875
- kv_bias: float32 [1536], replicated, may hold values from -3 to 3
- proj_weight: bfloat16 [768, 768], replicated, may hold values from -0.21875 to 0.21875
- proj_bias: float32 [768], replicated, may hold values from -3 to 3
Outputs:
- blocked: bfloat16 [128, 32, 64, 768], P(('scene', 'tile')), parts along dimension 0
The draws below stay inside these ranges and needn't reach their ends.
There are 4 independent parts, one for each index of `scene`. The reference program is written for one: setup_inputs(seed, part) draws one part's arguments, and reference() takes and returns one part's arrays. A program takes and returns all parts, laid end to end along the dimension named above; an argument that names none is the same for every part. Nothing has to cross between parts.
All inputs are finite; a program needn't handle non-finite values.
Results may differ from the reference program's by a relative error of at most 0.008.
The reference program's roundings to bfloat16 on the way count: a program that leaves them out, or rounds other values in their place, can miss the bound.
Values may be sent and summed in bfloat16 or wider, within the bound.
No kernel may reach another device: no remote copies, remote signals or barrier semaphores. Data moves between devices by JAX's collectives and lax.ppermute only.
A program may use at most 128 MiB of HBM per device.

```python
import math
import jax
import jax.numpy as jnp
from jax import lax

D = 768
HEADS = 24
HEAD_DIM = 32
SE_DIM = 192
WIN = 32
LEVELS = 3
TILE_COLS = 4
MAP = 256
TILE_ROWS = 8
TH = 32
TW = 64
N_TILE = 32


def draw_features(key, part):
    key = jax.random.fold_in(key, 17)
    keys_list = jax.random.split(key, 6)
    shape_all = (N_TILE, TH, TW, D)
    tile_rows = jnp.arange(N_TILE) // TILE_COLS
    tile_cols = jnp.arange(N_TILE) % TILE_COLS
    row_index = tile_rows[:, None] * TH + jnp.arange(TH)[None, :]
    col_index = tile_cols[:, None] * TW + jnp.arange(TW)[None, :]
    rising = jnp.exp(math.log(3.0) * (row_index.astype(jnp.float32) / MAP - 0.5))
    across = jnp.exp(math.log(3.0) * (col_index.astype(jnp.float32) / MAP - 0.5))
    block_side = MAP // 4
    block_table = jnp.exp(jax.random.uniform(keys_list[5], (4, 4), minval=0.0, maxval=math.log(2.0)) - 0.5 * math.log(2.0))
    block_scale = block_table[(row_index // block_side)[:, :, None], (col_index // block_side)[:, None, :]]
    token_scale = jnp.exp(jax.random.uniform(keys_list[0], (N_TILE, TH, TW), minval=0.0, maxval=math.log(10.0)))
    channel_scale = jnp.exp(jax.random.uniform(keys_list[1], (D,), minval=0.0, maxval=math.log(10.0))) / 3.0
    offset = 0.5 * jnp.clip(jax.random.normal(keys_list[2], (D,)), -3.0, 3.0)
    base_part = jnp.clip(jax.random.normal(keys_list[3], shape_all), -4.0, 4.0)
    cell_scale = token_scale * block_scale * rising[:, :, None] * across[:, None, :]
    values = (base_part * channel_scale + offset) * cell_scale[..., None] / 5.5
    return values.astype(jnp.bfloat16)


def centred(key, dims, deviation, most, dtype=jnp.bfloat16):
    values = deviation * jax.random.normal(key, dims, jnp.float32)
    return jnp.clip(values, min=-most, max=most).astype(dtype)


def setup_inputs(seed: int = 0, part: int = 0) -> dict:
    arg_keys = jax.random.split(jax.random.key(seed), 11)
    own_keys = jax.random.split(jax.random.fold_in(arg_keys[10], part), 11)
    features = draw_features(jax.random.fold_in(jax.random.fold_in(arg_keys[10], part), 71), part)
    dw_kernel = centred(arg_keys[1], (LEVELS, 3, 3, D), 9 ** -0.5, 2.0)
    se_reduce = centred(arg_keys[2], (LEVELS, D, SE_DIM), D ** -0.5, 0.21875)
    se_expand = centred(arg_keys[3], (LEVELS, SE_DIM, D), SE_DIM ** -0.5, 0.4375)
    mix_weight = centred(arg_keys[4], (LEVELS, D, D), D ** -0.5, 0.21875)
    norm_gain = jnp.clip(jnp.exp(jax.random.uniform(arg_keys[5], (D,), jnp.float32, math.log(0.5), math.log(2.0))), 0.5, 2.0)
    kv_weight = centred(arg_keys[6], (D, 2 * D), D ** -0.5, 0.21875)
    kv_bias = centred(arg_keys[7], (2 * D,), 0.5, 3.0, jnp.float32)
    proj_weight = centred(arg_keys[8], (D, D), D ** -0.5, 0.21875)
    proj_bias = centred(arg_keys[9], (D,), 0.5, 3.0, jnp.float32)
    return {"features": features, "dw_kernel": dw_kernel, "se_reduce": se_reduce, "se_expand": se_expand, "mix_weight": mix_weight, "norm_gain": norm_gain, "kv_weight": kv_weight, "kv_bias": kv_bias, "proj_weight": proj_weight, "proj_bias": proj_bias}


def build_map(tiles):
    arranged = tiles.reshape(TILE_ROWS, TILE_COLS, TH, TW, D)
    return arranged.transpose(0, 2, 1, 3, 4).reshape(MAP, MAP, D)

def depthwise(inputs, kernel):
    height, breadth = (inputs.shape[0], inputs.shape[1])
    padded = jnp.pad(inputs, ((1, 1), (1, 1), (0, 0)))
    summed = jnp.zeros(inputs.shape, jnp.float32)
    for shift_row in range(3):
        for shift_col in range(3):
            window_part = padded[shift_row:shift_row + height, shift_col:shift_col + breadth]
            summed = summed + window_part.astype(jnp.float32) * kernel[shift_row, shift_col].astype(jnp.float32)
    return summed

def squeeze_gate(channel_mean, reduce_matrix, expand_matrix):
    inner = jax.nn.gelu(jnp.dot(channel_mean, reduce_matrix.astype(jnp.float32), precision=lax.Precision.HIGHEST), approximate=False)
    return jax.nn.sigmoid(jnp.dot(inner, expand_matrix.astype(jnp.float32), precision=lax.Precision.HIGHEST))

def pool_half(padded):
    height = padded.shape[0] - 1
    breadth = padded.shape[1] - 1
    paired = padded[:height].reshape(height // 2, 2, breadth + 1, padded.shape[2])
    rowmax = jnp.maximum(lax.optimization_barrier(jnp.max(paired, axis=1)), padded[2::2])
    paired = rowmax[:, :breadth].reshape(height // 2, breadth // 2, 2, padded.shape[2])
    return jnp.maximum(lax.optimization_barrier(jnp.max(paired, axis=2)), rowmax[:, 2::2])

def level_step(inputs, kernel, reduce_matrix, expand_matrix, mix_matrix):
    response = jax.nn.gelu(depthwise(inputs, kernel), approximate=False)
    channel_mean = lax.optimization_barrier(jnp.mean(response, axis=(0, 1)))
    gate_values = squeeze_gate(channel_mean, reduce_matrix, expand_matrix)
    scaled = (response * gate_values).astype(jnp.bfloat16)
    channels = inputs.shape[2]
    product = jnp.dot(scaled.reshape(-1, channels), mix_matrix, preferred_element_type=jnp.float32).reshape(inputs.shape)
    mixed_map = (inputs.astype(jnp.float32) + product).astype(jnp.bfloat16)
    padded = jnp.pad(mixed_map, ((1, 0), (1, 0), (0, 0)), constant_values=-jnp.inf)
    return pool_half(padded)

def window_attention(window_tokens, query_tokens, norm_gain, kv_weight, kv_bias, proj_weight, proj_bias):
    length = window_tokens.shape[0]
    flat_tokens = window_tokens.astype(jnp.float32)
    centre = lax.optimization_barrier(jnp.mean(flat_tokens, axis=-1, keepdims=True))
    spread = lax.optimization_barrier(jnp.mean(jnp.square(flat_tokens - centre), axis=-1, keepdims=True))
    normed = ((flat_tokens - centre) * lax.rsqrt(spread + 1e-05) * norm_gain).astype(jnp.bfloat16)
    keyval = (jnp.dot(normed, kv_weight, preferred_element_type=jnp.float32) + kv_bias).astype(jnp.bfloat16)
    key_heads = keyval[:, :D].reshape(length, HEADS, HEAD_DIM)
    value_heads = keyval[:, D:].reshape(length, HEADS, HEAD_DIM)
    query_heads = query_tokens.reshape(length, HEADS, HEAD_DIM)
    scores = jnp.einsum('qhd,khd->hqk', query_heads.astype(jnp.float32), key_heads.astype(jnp.float32)) * HEAD_DIM ** (-0.5)
    weights = jax.nn.softmax(scores, axis=-1).astype(jnp.bfloat16)
    attended = jnp.einsum('hqk,khd->qhd', weights.astype(jnp.float32), value_heads.astype(jnp.float32)).astype(jnp.bfloat16)
    attended = attended.reshape(length, D)
    output_rows = flat_tokens + jnp.dot(attended, proj_weight, preferred_element_type=jnp.float32) + proj_bias
    return output_rows.astype(jnp.bfloat16)

def reference(features, dw_kernel, se_reduce, se_expand, mix_weight, norm_gain, kv_weight, kv_bias, proj_weight, proj_bias):
    scene_map = build_map(features)
    coarse = scene_map
    for level_index in range(LEVELS):
        coarse = level_step(coarse, dw_kernel[level_index], se_reduce[level_index], se_expand[level_index], mix_weight[level_index])
    query_tokens = coarse.reshape(WIN * WIN, D)
    side_count = MAP // WIN
    windows = scene_map.reshape(side_count, WIN, side_count, WIN, D).transpose(0, 2, 1, 3, 4).reshape(-1, WIN * WIN, D)
    outputs = lax.map(lambda tokens_in: window_attention(tokens_in, query_tokens, norm_gain, kv_weight, kv_bias, proj_weight, proj_bias), windows)
    restored = outputs.reshape(side_count, side_count, WIN, WIN, D).transpose(0, 2, 1, 3, 4).reshape(MAP, MAP, D)
    return restored.reshape(TILE_ROWS, TH, TILE_COLS, TW, D).transpose(0, 2, 1, 3, 4).reshape(N_TILE, TH, TW, D)
```

```python
import jax
import jax.numpy as jnp
from jax import lax
from jax.experimental import pallas as pl
from jax.experimental.pallas import tpu as pltpu
from jax.sharding import PartitionSpec as P

HEADS = 24
TILE_COLS = 4
EPSILON = 1e-05
BF = jnp.bfloat16
F32 = jnp.float32
VM = pl.BlockSpec(memory_space=pltpu.VMEM)
LOG2E = 1.4426950408889634
QB = 256
KC = 512
UNROLL = 8


def kv_kernel(x_ref, gain_ref, w_ref, b_ref, kt_ref, vt_ref):
    dim = x_ref.shape[-1]
    tokens = x_ref.shape[0] * x_ref.shape[1]
    x = x_ref[...].reshape(tokens, dim).astype(F32)
    centre = jnp.mean(x, axis=1, keepdims=True)
    moved = x - centre
    spread = jnp.mean(jnp.square(moved), axis=1, keepdims=True)
    normed = (moved * lax.rsqrt(spread + EPSILON) * gain_ref[...]).astype(BF)
    keys = (jnp.dot(normed, w_ref[:, :dim], preferred_element_type=F32) + b_ref[:, :dim]).astype(BF)
    for group in range(dim // 128):
        kt_ref[group] = keys[:, 128 * group : 128 * group + 128]
    vals = jnp.dot(normed, w_ref[:, dim:], preferred_element_type=F32) + b_ref[:, dim:]
    vt_ref[...] = vals.T.astype(BF)


def keys_values(tile_map, gain, weight, bias):
    rows, cols, dim = tile_map.shape
    win = rows
    step = 8
    tokens = step * win
    windows = cols // win
    per = rows // step
    return pl.pallas_call(
        kv_kernel,
        grid=(windows, per),
        in_specs=[
            pl.BlockSpec((step, win, dim), lambda w, i: (i, w, 0)),
            pl.BlockSpec((1, dim), lambda w, i: (0, 0)),
            pl.BlockSpec((dim, 2 * dim), lambda w, i: (0, 0)),
            pl.BlockSpec((1, 2 * dim), lambda w, i: (0, 0)),
        ],
        out_specs=[
            pl.BlockSpec((dim // 128, tokens, 128), lambda w, i: (0, w * per + i, 0)),
            pl.BlockSpec((dim, tokens), lambda w, i: (0, w * per + i)),
        ],
        out_shape=[
            jax.ShapeDtypeStruct((dim // 128, rows * cols, 128), BF),
            jax.ShapeDtypeStruct((dim, rows * cols), BF),
        ],
        compiler_params=pltpu.CompilerParams(vmem_limit_bytes=32 * 2**20),
        cost_estimate=pl.CostEstimate(
            flops=4 * rows * cols * dim * dim, bytes_accessed=12 * 2**20, transcendentals=0
        ),
        name="keys_values",
    )(tile_map, gain.reshape(1, dim), weight, bias.reshape(1, 2 * dim))


def attention_kernel(q_ref, kt_ref, vt_ref, x_ref, wp_ref, bp_ref, out_ref, qa, sb, mb, ot):
    count, dim = q_ref.shape
    length = kt_ref.shape[1] // 2
    blocks = count // QB
    units = HEADS * blocks
    scale = (dim // HEADS) ** (-0.5) * LOG2E
    lane = lax.broadcasted_iota(jnp.int32, (1, 128), 1)
    for group in range(dim // 128):
        q = q_ref[:, 128 * group : 128 * group + 128]
        for part in range(4):
            qa[4 * group + part] = jnp.where(lane // 32 == part, q, jnp.zeros_like(q))
    ones = jnp.ones((16, KC), BF)

    def score(unit, slot, start):
        head = unit // blocks
        rows = pl.ds(pl.multiple_of(unit % blocks * QB, QB), QB)
        s = lax.dot_general(
            kt_ref[head // 4, pl.ds(start, KC), :],
            qa[head, rows, :],
            (((1,), (1,)), ((), ())),
            preferred_element_type=F32,
        )
        sb[slot, pl.ds(start, KC), :] = s
        return jnp.max(s.reshape(KC // 8, 8, QB), axis=0)

    def step(unit, slot, following):
        if unit is not None:
            head = unit // blocks
            rows = pl.ds(pl.multiple_of(head * 32, 32), 32)
            cols = pl.ds(pl.multiple_of(unit % blocks * QB, QB), QB)
        for w in range(2):
            top = total = None
            if unit is not None:
                peak = jnp.max(mb[slot, w], axis=0, keepdims=True)
            for start in range(length * w, length * w + length, KC):
                high = score(following, 1 - slot, start)
                top = high if top is None else jnp.maximum(top, high)
                if unit is not None:
                    p = jnp.exp2((sb[slot, pl.ds(start, KC), :] - peak) * scale).astype(BF)
                    v = jnp.concatenate([vt_ref[rows, pl.ds(start, KC)], ones], axis=0)
                    o = jnp.dot(v, p, preferred_element_type=F32)
                    total = o if total is None else total + o
            mb[1 - slot, w] = top
            if unit is not None:
                ot[w, rows, cols] = (total[:32] / total[32:33]).astype(BF)

    step(None, 1, 0)

    def body(turn, _):
        for j in range(UNROLL):
            unit = UNROLL * turn + j
            step(unit, j % 2, jnp.minimum(unit + 1, units - 1))
        return 0

    lax.fori_loop(0, units // UNROLL, body, 0)

    win = out_ref.shape[1] // 2
    lines = QB // win
    for w in range(2):
        for part in range(blocks):
            o = ot[w, :, part * QB : part * QB + QB]
            y = lax.dot_general(o, wp_ref[...], (((0,), (0,)), ((), ())), preferred_element_type=F32)
            r = slice(part * lines, part * lines + lines)
            x = x_ref[r, w * win : w * win + win, :].reshape(QB, dim).astype(F32)
            y = x + y + bp_ref[...]
            out_ref[r, w * win : w * win + win, :] = y.astype(BF).reshape(lines, win, dim)


def attention(q, kt, vt, tile_map, wp, bp):
    rows, cols, dim = tile_map.shape
    count = q.shape[0]
    return pl.pallas_call(
        attention_kernel,
        in_specs=[VM] * 6,
        out_specs=VM,
        out_shape=jax.ShapeDtypeStruct((count // 32, cols, dim), BF),
        scratch_shapes=[
            pltpu.VMEM((HEADS, count, 128), BF),
            pltpu.VMEM((2, rows * cols, QB), F32),
            pltpu.VMEM((2, 2, 8, QB), F32),
            pltpu.VMEM((2, dim, count), BF),
        ],
        compiler_params=pltpu.CompilerParams(vmem_limit_bytes=56 * 2**20),
        cost_estimate=pl.CostEstimate(
            flops=8 * count * 1024 * dim,
            bytes_accessed=16 * 2**20,
            transcendentals=48 * count * 1024,
        ),
        name="attention",
    )(q, kt, vt, tile_map, wp, bp.reshape(1, dim))


def shifted(value, axis, steps):
    count = lax.axis_size(axis)
    initial, last = (max(0, -steps), min(count, count - steps))
    return lax.ppermute(value, axis, [(source, source + steps) for source in range(initial, last)])


def mark_fill(piece, missing, fill_value):
    return jnp.where(missing, jnp.full_like(piece, fill_value), piece)


def strip_rims(inputs, grid_row, grid_col, grid_rows, fill_value, both_sides):
    if both_sides:
        move_list = ((TILE_COLS, True), (-TILE_COLS, False))
    else:
        move_list = ((TILE_COLS, True),)
    received = []
    for stride, from_above in move_list:
        edge_part = inputs[-1:] if from_above else inputs[:1]
        arrived = shifted(edge_part, "tile", stride)
        missing = grid_row == 0 if from_above else grid_row == grid_rows - 1
        received.append(mark_fill(arrived, missing, fill_value))
    stacked = jnp.concatenate([received[0], inputs] + received[1:], axis=0)
    received = []
    for stride, from_left in ((1, True), (-1, False))[: len(move_list)]:
        edge_part = stacked[:, -1:] if from_left else stacked[:, :1]
        arrived = shifted(edge_part, "tile", stride)
        missing = grid_col == 0 if from_left else grid_col == TILE_COLS - 1
        received.append(mark_fill(arrived, missing, fill_value))
    return jnp.concatenate([received[0], stacked] + received[1:], axis=1)


def squeeze_gate(channel_mean, reduce_matrix, expand_matrix):
    inner = jax.nn.gelu(
        jnp.dot(channel_mean, reduce_matrix.astype(jnp.float32), precision=lax.Precision.HIGHEST),
        approximate=False,
    )
    return jax.nn.sigmoid(
        jnp.dot(inner, expand_matrix.astype(jnp.float32), precision=lax.Precision.HIGHEST)
    )


def pool_half(padded):
    height = padded.shape[0] - 1
    breadth = padded.shape[1] - 1
    paired = padded[:height].reshape(height // 2, 2, breadth + 1, padded.shape[2])
    rowmax = jnp.maximum(jnp.max(paired, axis=1), padded[2::2])
    paired = rowmax[:, :breadth].reshape(height // 2, breadth // 2, 2, padded.shape[2])
    return jnp.maximum(jnp.max(paired, axis=2), rowmax[:, 2::2])


def level_step(
    inputs, kernel, reduce_matrix, expand_matrix, mix_matrix, rim_rule, sum_rule, cell_count
):
    height, breadth, channels = inputs.shape
    padded = rim_rule(inputs, 0.0, True)
    summed = jnp.zeros(inputs.shape, jnp.float32)
    for shift_row in range(3):
        for shift_col in range(3):
            window_part = padded[shift_row : shift_row + height, shift_col : shift_col + breadth]
            summed = summed + window_part.astype(jnp.float32) * kernel[shift_row, shift_col].astype(
                jnp.float32
            )
    response = jax.nn.gelu(summed, approximate=False)
    channel_mean = sum_rule(jnp.sum(response, axis=(0, 1))) / cell_count
    gate_values = squeeze_gate(channel_mean, reduce_matrix, expand_matrix)
    scaled = (response * gate_values).astype(jnp.bfloat16)
    product = jnp.dot(
        scaled.reshape(-1, channels), mix_matrix, preferred_element_type=jnp.float32
    ).reshape(inputs.shape)
    mixed_map = (inputs.astype(jnp.float32) + product).astype(jnp.bfloat16)
    return pool_half(rim_rule(mixed_map, -jnp.inf, False))


def assemble(collected, grid_rows):
    tile_count, tile_high, tile_wide, channels = collected.shape
    arranged = collected.reshape(grid_rows, tile_count // grid_rows, tile_high, tile_wide, channels)
    return arranged.transpose(0, 2, 1, 3, 4).reshape(
        grid_rows * tile_high, tile_count // grid_rows * tile_wide, channels
    )


def body(
    features,
    dw_kernel,
    se_reduce,
    se_expand,
    mix_weight,
    norm_gain,
    kv_weight,
    kv_bias,
    proj_weight,
    proj_bias,
):
    tile_map = features[0]
    grid_size = lax.axis_size("tile")
    grid_rows = grid_size // TILE_COLS
    position = lax.axis_index("tile")
    grid_row = position // TILE_COLS
    grid_col = position % TILE_COLS
    level_count = dw_kernel.shape[0]

    def spread_rim(inputs, fill_value, both_sides):
        return strip_rims(inputs, grid_row, grid_col, grid_rows, fill_value, both_sides)

    def scene_sum(partial_sum):
        count = lax.axis_size("tile")
        copies = jnp.broadcast_to(partial_sum[None], (count,) + partial_sum.shape)
        return jnp.sum(lax.all_to_all(copies, "tile", 0, 0, tiled=True), axis=0)

    coarse = tile_map
    for level_index in range(level_count):
        coarse = level_step(
            coarse,
            dw_kernel[level_index],
            se_reduce[level_index],
            se_expand[level_index],
            mix_weight[level_index],
            spread_rim,
            scene_sum,
            coarse.shape[0] * coarse.shape[1] * grid_size,
        )
    collected = lax.all_gather(coarse[None], "tile", axis=0, tiled=True)
    query_map = assemble(collected, grid_rows)
    channels = tile_map.shape[-1]
    query_tokens = query_map.reshape(-1, channels)
    kt, vt = keys_values(tile_map, norm_gain, kv_weight, kv_bias)
    return attention(query_tokens, kt, vt, tile_map, proj_weight, proj_bias)[None]


def solution(mesh):
    in_specs = (P(("scene", "tile"), None, None, None), P(), P(), P(), P(), P(), P(), P(), P(), P())
    out_specs = P(("scene", "tile"), None, None, None)
    return jax.shard_map(body, mesh=mesh, in_specs=in_specs, out_specs=out_specs, check_vma=False)
```

```python
import functools

import jax
import jax.numpy as jnp
from jax import lax
from jax.experimental import pallas as pl
from jax.experimental.pallas import tpu as pltpu
from jax.sharding import PartitionSpec as P

HEADS = 24
TILE_COLS = 4
EPSILON = 1e-05
BF = jnp.bfloat16
F32 = jnp.float32
VM = pl.BlockSpec(memory_space=pltpu.VMEM)
LOG2E = 1.4426950408889634
QB = 256
KC = 512
UNROLL = 8


def kv_kernel(x_ref, gain_ref, w_ref, b_ref, kt_ref, vt_ref):
    dim = x_ref.shape[-1]
    tokens = x_ref.shape[0] * x_ref.shape[1]
    x = x_ref[...].reshape(tokens, dim).astype(F32)
    centre = jnp.mean(x, axis=1, keepdims=True)
    moved = x - centre
    spread = jnp.mean(jnp.square(moved), axis=1, keepdims=True)
    normed = (moved * lax.rsqrt(spread + EPSILON) * gain_ref[...]).astype(BF)
    keys = (jnp.dot(normed, w_ref[:, :dim], preferred_element_type=F32) + b_ref[:, :dim]).astype(BF)
    for group in range(dim // 128):
        kt_ref[group] = keys[:, 128 * group : 128 * group + 128]
    vals = jnp.dot(normed, w_ref[:, dim:], preferred_element_type=F32) + b_ref[:, dim:]
    vt_ref[...] = vals.T.astype(BF)


def keys_values(tile_map, gain, weight, bias, window):
    win, _, dim = tile_map.shape
    step = 8
    tokens = step * win
    return pl.pallas_call(
        kv_kernel,
        grid=(win // step,),
        in_specs=[
            pl.BlockSpec((step, win, dim), lambda i: (i, window, 0)),
            pl.BlockSpec((1, dim), lambda i: (0, 0)),
            pl.BlockSpec((dim, 2 * dim), lambda i: (0, 0)),
            pl.BlockSpec((1, 2 * dim), lambda i: (0, 0)),
        ],
        out_specs=[
            pl.BlockSpec((dim // 128, tokens, 128), lambda i: (0, i, 0)),
            pl.BlockSpec((dim, tokens), lambda i: (0, i)),
        ],
        out_shape=[
            jax.ShapeDtypeStruct((dim // 128, win * win, 128), BF),
            jax.ShapeDtypeStruct((dim, win * win), BF),
        ],
        compiler_params=pltpu.CompilerParams(vmem_limit_bytes=24 * 2**20),
        cost_estimate=pl.CostEstimate(
            flops=8 * win * win * dim * dim, bytes_accessed=8 * 2**20, transcendentals=0
        ),
        name="keys_values",
    )(tile_map, gain, weight, bias)


def attention_kernel(slabs, slab_ref, *refs):
    q_refs = refs[:slabs]
    kt_refs, vt_refs = refs[slabs : slabs + 2], refs[slabs + 2 : slabs + 4]
    x_ref, wp_ref, bp_ref = refs[slabs + 4 : slabs + 7]
    out_ref, qa, sb, mb, ot, stage, sems = refs[-7:]
    dim = x_ref.shape[2]
    length = kt_refs[0].shape[1]
    units = HEADS * slabs
    scale = (dim // HEADS) ** (-0.5) * LOG2E
    lane = lax.broadcasted_iota(jnp.int32, (1, 128), 1)
    for slab in range(slabs):
        for group in range(dim // 128):
            q = q_refs[slab][:, 128 * group : 128 * group + 128]
            for part in range(4):
                qa[slab, 4 * group + part] = jnp.where(lane // 32 == part, q, jnp.zeros_like(q))
    ones = jnp.ones((16, KC), BF)

    def score(unit, slot, w, start):
        head = unit // slabs
        s = lax.dot_general(
            kt_refs[w][head // 4, pl.ds(start, KC), :],
            qa[unit % slabs, head],
            (((1,), (1,)), ((), ())),
            preferred_element_type=F32,
        )
        sb[slot, w, pl.ds(start, KC), :] = s
        return jnp.max(s.reshape(KC // 8, 8, QB), axis=0)

    def step(unit, slot, following):
        if unit is not None:
            head = unit // slabs
            rows = pl.ds(pl.multiple_of(head * 32, 32), 32)
        for w in range(2):
            top = total = None
            if unit is not None:
                peak = jnp.max(mb[slot, w], axis=0, keepdims=True)
            for start in range(0, length, KC):
                high = score(following, 1 - slot, w, start)
                top = high if top is None else jnp.maximum(top, high)
                if unit is not None:
                    p = jnp.exp2((sb[slot, w, pl.ds(start, KC), :] - peak) * scale).astype(BF)
                    v = jnp.concatenate([vt_refs[w][rows, pl.ds(start, KC)], ones], axis=0)
                    o = jnp.dot(v, p, preferred_element_type=F32)
                    total = o if total is None else total + o
            mb[1 - slot, w] = top
            if unit is not None:
                ot[unit % slabs, w, rows, :] = (total[:32] / total[32:33]).astype(BF)

    step(None, 1, 0)

    def body(turn, _):
        for j in range(UNROLL):
            unit = UNROLL * turn + j
            step(unit, j % 2, jnp.minimum(unit + 1, units - 1))
        return 0

    lax.fori_loop(0, units // UNROLL, body, 0)

    win = x_ref.shape[1] // 2
    lines = QB // win
    copies = []
    for slab in range(slabs):
        place = pl.ds(pl.multiple_of(slab_ref[slab] * lines, lines), lines)
        for w in range(2):
            cols = slice(w * win, w * win + win)
            y = lax.dot_general(
                ot[slab, w], wp_ref[...], (((0,), (0,)), ((), ())), preferred_element_type=F32
            )
            y = y.reshape(2, 4, lines // 2, win // 4, dim).transpose(0, 2, 1, 3, 4).reshape(lines, win, dim)
            y = x_ref[place, cols, :].astype(F32) + y + bp_ref[...]
            stage[slab, :, cols, :] = y.astype(BF)
        copy = pltpu.make_async_copy(stage.at[slab], out_ref.at[place], sems.at[slab])
        copy.start()
        copies.append(copy)
    for copy in copies:
        copy.wait()


def attention(place, queries, keys, values, tile_map, wp, bp, started=None):
    rows, cols, dim = tile_map.shape
    slabs = len(queries)
    lines = QB * 2 // cols
    more = [] if started is None else [started]
    anywhere = pl.BlockSpec(memory_space=pl.ANY)
    return pl.pallas_call(
        functools.partial(attention_kernel, slabs),
        in_specs=[pl.BlockSpec(memory_space=pltpu.SMEM)] + [VM] * (slabs + 7) + [anywhere] * len(more),
        out_specs=anywhere,
        out_shape=jax.ShapeDtypeStruct(tile_map.shape, BF),
        input_output_aliases={slabs + 8: 0} if more else {},
        scratch_shapes=[
            pltpu.VMEM((slabs, HEADS, QB, 128), BF),
            pltpu.VMEM((2, 2, rows * cols // 2, QB), F32),
            pltpu.VMEM((2, 2, 8, QB), F32),
            pltpu.VMEM((slabs, 2, dim, QB), BF),
            pltpu.VMEM((slabs, lines, cols, dim), BF),
            pltpu.SemaphoreType.DMA((slabs,)),
        ],
        compiler_params=pltpu.CompilerParams(vmem_limit_bytes=40 * 2**20),
        cost_estimate=pl.CostEstimate(
            flops=8 * slabs * QB * 1024 * dim * 8,
            bytes_accessed=12 * 2**20,
            transcendentals=48 * slabs * QB * 1024,
        ),
        name="attention",
    )(place, *queries, *keys, *values, tile_map, wp, bp, *more)


def whole(array):
    return pl.BlockSpec(array.shape, lambda *i: (0,) * len(array.shape), pipeline_mode=pl.Buffered(1))


def wholes(*arrays):
    return [whole(array) for array in arrays]


def at_level(array, level):
    shape = (None,) + array.shape[1:]
    return pl.BlockSpec(shape, lambda *i: (level,) + (0,) * (len(shape) - 1), pipeline_mode=pl.Buffered(1))


POSITION = pl.BlockSpec(memory_space=pltpu.SMEM)


def params(mib):
    return pltpu.CompilerParams(vmem_limit_bytes=mib * 2**20)


def cost(flops, size):
    return pl.CostEstimate(flops=flops, bytes_accessed=size, transcendentals=0)


def round_up(count, unit):
    return -(-count // unit) * unit


def side_pieces_kernel(before, after, left_ref, right_ref, to_right, to_left, keep_r, keep_l):
    high = left_ref.shape[0]
    span = right_ref.shape[1]
    for r in range(high):
        keep_r[r * before : r * before + before, :] = right_ref[r].astype(F32)[span - before :]
        keep_l[r * after : r * after + after, :] = left_ref[r].astype(F32)[:after]
    to_right[...] = keep_r[...].astype(BF)
    to_left[...] = keep_l[...].astype(BF)


def side_pieces(tile, before, after):
    high, wide, dim = tile.shape
    return pl.pallas_call(
        functools.partial(side_pieces_kernel, before, after),
        grid=(1,),
        in_specs=[
            pl.BlockSpec((high, 16, dim), lambda i: (0, 0, 0)),
            pl.BlockSpec((high, 16, dim), lambda i: (0, wide // 16 - 1, 0)),
        ],
        out_shape=[
            jax.ShapeDtypeStruct((high * before, dim), BF),
            jax.ShapeDtypeStruct((high * after, dim), BF),
        ],
        scratch_shapes=[pltpu.VMEM((high * before, dim), F32), pltpu.VMEM((high * after, dim), F32)],
        compiler_params=params(16),
        cost_estimate=cost(0, 2 * 2**20),
        name="side_pieces",
    )(tile, tile)


def line_pieces_kernel(before, after, high, top_ref, low_ref, left_ref, right_ref, to_low, to_up, keep_d, keep_u, side_l, side_r):
    wide = top_ref.shape[1]
    full = before + wide + after
    side_l[...] = left_ref[...].astype(F32)
    side_r[...] = right_ref[...].astype(F32)
    keep_d[...] = jnp.zeros_like(keep_d)
    keep_u[...] = jnp.zeros_like(keep_u)

    def fill(keep, line, r, values):
        base = line * full
        keep[base : base + before, :] = side_l[r * before : r * before + before, :]
        keep[base + before : base + before + wide, :] = values
        keep[base + before + wide : base + full, :] = side_r[r * after : r * after + after, :]

    for line in range(before):
        fill(keep_d, line, high - before + line, low_ref[line].astype(F32))
    for line in range(after):
        fill(keep_u, line, line, top_ref[line].astype(F32))
    to_low[...] = keep_d[...].astype(BF)
    to_up[...] = keep_u[...].astype(BF)


def line_pieces(tile, left, right, before, after):
    high, wide, dim = tile.shape
    full = before + wide + after
    down = round_up(before * full, 16)
    up = round_up(after * full, 16)
    low_size = before if high % before == 0 else 8
    assert high % low_size == 0
    return pl.pallas_call(
        functools.partial(line_low_kernel, low_size, before, after, high),
        grid=(1,),
        in_specs=[
            pl.BlockSpec((after if high % after == 0 else 8, wide, dim), lambda i: (0, 0, 0)),
            pl.BlockSpec((low_size, wide, dim), lambda i: (high // low_size - 1, 0, 0)),
            whole(left),
            whole(right),
        ],
        out_shape=[jax.ShapeDtypeStruct((down, dim), BF), jax.ShapeDtypeStruct((up, dim), BF)],
        scratch_shapes=[
            pltpu.VMEM((down, dim), F32),
            pltpu.VMEM((up, dim), F32),
            pltpu.VMEM(left.shape, F32),
            pltpu.VMEM(right.shape, F32),
        ],
        compiler_params=params(16),
        cost_estimate=cost(0, 2**20),
        name="line_pieces",
    )(tile, tile, left, right)


def line_low_kernel(low_size, before, after, high, top_ref, low_ref, *rest):
    line_pieces_kernel(before, after, high, top_ref, low_ref.at[pl.ds(low_size - before, before)], *rest)


def moved_by(value, rows, cols):
    count = lax.axis_size("tile")
    pairs = []
    for t in range(count):
        r, c = t // TILE_COLS + rows, t % TILE_COLS + cols
        if 0 <= r < count // TILE_COLS and 0 <= c < TILE_COLS:
            pairs.append((t, r * TILE_COLS + c))
    return lax.ppermute(value, "tile", pairs)


def after_these(value, *others):
    return lax.optimization_barrier((value,) + others)[0]


def exchange_rims(tile, pieces, before, after, beside):
    left = moved_by(pieces[0], 0, 1)
    right = moved_by(pieces[1], 0, -1)
    down, up = line_pieces(tile, left, right, before, after)
    above, below = moved_by(down, 1, 0), moved_by(up, -1, 0)
    result = beside(down)
    above, below, *result = lax.optimization_barrier((above, below, *result))
    return (left, right, above, below), result


def erf_gelu(y):
    return 0.5 * y * (1.0 + lax.erf(y * 0.7071067811865476))


def fill_padded(x_ref, rims, before, after, padded, stage):
    high, wide, _ = x_ref.shape
    full = before + wide + after
    left, right, above, below = rims

    def line(r, _):
        padded[r + before, before : before + wide, :] = x_ref[r].astype(F32)
        return 0

    lax.fori_loop(0, high, line, 0)
    stage[: left.shape[0], :] = left[...].astype(F32)
    for r in range(high):
        padded[r + before, 0:before, :] = stage[r * before : r * before + before, :]
    stage[: right.shape[0], :] = right[...].astype(F32)
    for r in range(high):
        padded[r + before, before + wide : full, :] = stage[r * after : r * after + after, :]
    stage[: above.shape[0], :] = above[...].astype(F32)
    for r in range(before):
        padded[r, 0:full, :] = stage[r * full : r * full + full, :]
    stage[: below.shape[0], :] = below[...].astype(F32)
    for r in range(after):
        padded[before + high + r, 0:full, :] = stage[r * full : r * full + full, :]


def conv_gelu(padded, kernel_ref, g_ref, own_rows, own_cols, part_ref):
    rows, cols, dim = g_ref.shape
    column = lax.broadcasted_iota(jnp.int32, (cols, 128), 0)
    mine = (column >= own_cols[0]) & (column < own_cols[1])
    for group in range(dim // 128):
        lanes = slice(128 * group, 128 * group + 128)
        taps = [[kernel_ref[a, b : b + 1, lanes].astype(F32) for b in range(3)] for a in range(3)]

        def line(r, total):
            y = None
            for a in range(3):
                for b in range(3):
                    term = padded[r + a, b : b + cols, lanes] * taps[a][b]
                    y = term if y is None else y + term
            g = erf_gelu(y)
            g_ref[r, :, lanes] = g
            counted = jnp.sum(jnp.where(mine, g, 0.0).reshape(cols // 8, 8, 128), axis=0)
            return total + jnp.where((r >= own_rows[0]) & (r < own_rows[1]), counted, 0.0)

        total = lax.fori_loop(0, rows, line, jnp.zeros((8, 128), F32))
        total = jnp.sum(total, axis=0, keepdims=True)
        part_ref[:, group, :] += jnp.broadcast_to(total, (part_ref.shape[0], 128))


def copy_centre(padded, rest_ref):
    rows, cols, _ = rest_ref.shape

    def line(r, _):
        rest_ref[r] = padded[r + 1, 1 : 1 + cols, :].astype(BF)
        return 0

    lax.fori_loop(0, rows, line, 0)


def thirds(row):
    high = row.astype(BF).astype(F32)
    mid = (row - high).astype(BF).astype(F32)
    low = row - high - mid
    index = lax.broadcasted_iota(jnp.int32, (16, row.shape[1]), 0)
    block = jnp.where(index == 0, high, jnp.where(index == 1, mid, jnp.where(index == 2, low, 0.0)))
    return block.astype(BF)


def gate_row(sums_ref, cells, reduce_ref, expand_ref):
    total = jnp.sum(sums_ref[...], axis=0)
    groups = reduce_ref.shape[0] // 128
    mean = jnp.concatenate([total[group : group + 1] for group in range(groups)], axis=1) / cells
    inner = jnp.sum(jnp.dot(thirds(mean), reduce_ref[...], preferred_element_type=F32), axis=0, keepdims=True)
    inner = erf_gelu(inner)
    outer = jnp.sum(jnp.dot(thirds(inner), expand_ref[...], preferred_element_type=F32), axis=0, keepdims=True)
    return 1.0 / (1.0 + jnp.exp(-outer))


def mix_lines(g_ref, gate, mix_ref, rest_ref, z_ref, first, bounds):
    rows, cols, dim = g_ref.shape
    row_low, row_high, col_low, col_high = bounds
    column = lax.broadcasted_iota(jnp.int32, (cols, 1), 0)
    inside = (column >= col_low) & (column < col_high)
    u = (g_ref[...] * gate).astype(BF).reshape(rows * cols, dim)
    product = jnp.dot(u, mix_ref[...], preferred_element_type=F32).reshape(rows, cols, dim)
    for k in range(rows):
        z = (rest_ref[k].astype(F32) + product[k]).astype(BF).astype(F32)
        keep = inside & (first + k >= row_low) & (first + k < row_high)
        z_ref[first + k] = jnp.where(keep, z, -jnp.inf)


def pooled_line(z_ref, line_ref, i, count):
    most = jnp.maximum(jnp.maximum(z_ref[2 * i], z_ref[2 * i + 1]), z_ref[2 * i + 2])
    groups = []
    for group in range(line_ref.shape[0]):
        line_ref[group] = most[:, 128 * group : 128 * group + 128]
        parts = [line_ref[group, pl.ds(s, count, stride=2), :] for s in range(3)]
        groups.append(jnp.maximum(jnp.maximum(parts[0], parts[1]), parts[2]))
    return jnp.concatenate(groups, axis=1)


def act_kernel(before, after, x_ref, l_ref, r_ref, a_ref, b_ref, kernel_ref, g_ref, rest_ref, part_ref, padded, stage):
    high, wide, _ = x_ref.shape
    step = g_ref.shape[0]
    turn = pl.program_id(0)

    @pl.when(turn == 0)
    def _():
        fill_padded(x_ref, (l_ref, r_ref, a_ref, b_ref), before, after, padded, stage)
        part_ref[...] = jnp.zeros_like(part_ref)

    own = before - 1
    block = padded.at[pl.ds(turn * step, step + 2)]
    copy_centre(block, rest_ref)
    conv_gelu(block, kernel_ref, g_ref, (own - turn * step, own + high - turn * step), (own, own + wide), part_ref)


def activate(tile, rims, kernels, level, before, after, step):
    high, wide, dim = tile.shape
    rows, cols = high + before + after - 2, round_up(wide + before + after - 2, 8)
    stage = max(r.shape[0] for r in rims)
    copies = lax.axis_size("tile")
    block = pl.BlockSpec((step, cols, dim), lambda i: (i, 0, 0))
    return pl.pallas_call(
        functools.partial(act_kernel, before, after),
        grid=(rows // step,),
        in_specs=wholes(tile, *rims) + [at_level(kernels, level)],
        out_specs=[block, block, pl.BlockSpec((copies, 8, 128), lambda i: (0, 0, 0))],
        out_shape=[
            jax.ShapeDtypeStruct((rows, cols, dim), F32),
            jax.ShapeDtypeStruct((rows, cols, dim), BF),
            jax.ShapeDtypeStruct((copies, 8, 128), F32),
        ],
        scratch_shapes=[
            pltpu.VMEM((rows + 2, round_up(cols + 2, 8), dim), F32),
            pltpu.VMEM((stage, dim), F32),
        ],
        compiler_params=params(28),
        cost_estimate=cost(400 * rows * cols * dim, 6 * rows * cols * dim),
        name="activate",
    )(tile, *rims, kernels)


def mix0_kernel(cells, before, after, pos, sums, red, exp, mix, g_ref, rest, x_out, to_right, to_left, gates, z, line, keep_r, keep_l):
    step, cols, dim = g_ref.shape
    high, wide, _ = x_out.shape
    turn = pl.program_id(0)

    @pl.when(turn == 0)
    def _():
        gates[...] = jnp.broadcast_to(gate_row(sums, cells, red, exp), gates.shape)

    bounds = (jnp.where(pos[0] == 0, 1, 0), z.shape[0], jnp.where(pos[1] == 0, 1, 0), cols)
    mix_lines(g_ref, gates[:1, :], mix, rest, z, turn * step, bounds)

    @pl.when(turn == pl.num_programs(0) - 1)
    def _():
        for i in range(high):
            out = pooled_line(z, line, i, wide)
            x_out[i] = out.astype(BF)
            keep_r[i * before : i * before + before, :] = out[wide - before :]
            keep_l[i * after : i * after + after, :] = out[:after]
        to_right[...] = keep_r[...].astype(BF)
        to_left[...] = keep_l[...].astype(BF)


def level_specs(sums, red, exp, mix, level):
    return [POSITION, whole(sums), at_level(red, level), at_level(exp, level), at_level(mix, level)]


def mix0(pos, sums, red, exp, mix, g, rest, cells, high, wide, before, after, step):
    rows, cols, dim = g.shape
    block = pl.BlockSpec((step, cols, dim), lambda i: (i, 0, 0))
    outs = [
        jax.ShapeDtypeStruct((high, wide, dim), BF),
        jax.ShapeDtypeStruct((high * before, dim), BF),
        jax.ShapeDtypeStruct((high * after, dim), BF),
    ]
    return pl.pallas_call(
        functools.partial(mix0_kernel, cells, before, after),
        grid=(rows // step,),
        in_specs=level_specs(sums, red, exp, mix, 0) + [block, block],
        out_specs=wholes(*outs),
        out_shape=outs,
        scratch_shapes=[
            pltpu.VMEM((8, dim), F32),
            pltpu.VMEM((rows, cols, dim), F32),
            pltpu.VMEM((dim // 128, cols, 128), F32),
            pltpu.VMEM((high * before, dim), F32),
            pltpu.VMEM((high * after, dim), F32),
        ],
        compiler_params=params(32),
        cost_estimate=cost(2 * rows * cols * dim * dim, 6 * rows * cols * dim),
        name="mix0",
    )(pos, sums, red, exp, mix, g, rest)


def mix1_kernel(cells, size, before, pos, sums, red, exp, mix, g_ref, rest, kernel, g_out, rest_out, part, z, line, padded):
    rows, cols, dim = g_ref.shape
    side_r, side_c, map_side = size
    gate = gate_row(sums, cells, red, exp)
    shift = before - 1
    row_low = shift - pos[0] * side_r
    col_low = shift - pos[1] * side_c
    mix_lines(g_ref, gate, mix, rest, z, 0, (row_low, row_low + map_side, col_low, col_low + map_side))
    count_r, count_c = padded.shape[0], (cols - 1) // 2
    row_two = 2 - pos[0] * (side_r // 2)
    col_two = 2 - pos[1] * (side_c // 2)
    column = lax.broadcasted_iota(jnp.int32, (count_c, 1), 0)
    inside = (column >= col_two) & (column < col_two + map_side // 2)
    for i in range(count_r):
        out = pooled_line(z, line, i, count_c)
        keep = inside & (i >= row_two) & (i < row_two + map_side // 2)
        padded[i, 0:count_c, :] = jnp.where(keep, out, 0.0)
    copy_centre(padded, rest_out)
    part[...] = jnp.zeros_like(part)
    conv_gelu(padded, kernel, g_out, (1, 1 + side_r // 2), (1, 1 + side_c // 2), part)


def mix1(pos, sums, red, exp, mix, g, rest, kernels, cells, size, before):
    rows, cols, dim = g.shape
    out_rows, out_cols = (rows - 1) // 2 - 2, round_up((cols - 1) // 2 - 2, 8)
    outs = [
        jax.ShapeDtypeStruct((out_rows, out_cols, dim), F32),
        jax.ShapeDtypeStruct((out_rows, out_cols, dim), BF),
        jax.ShapeDtypeStruct(sums.shape, F32),
    ]
    return pl.pallas_call(
        functools.partial(mix1_kernel, cells, size, before),
        grid=(1,),
        in_specs=level_specs(sums, red, exp, mix, 1) + wholes(g, rest) + [at_level(kernels, 2)],
        out_specs=wholes(*outs),
        out_shape=outs,
        scratch_shapes=[
            pltpu.VMEM((rows, cols, dim), F32),
            pltpu.VMEM((dim // 128, cols, 128), F32),
            pltpu.VMEM((out_rows + 2, round_up(out_cols + 2, 8), dim), F32),
        ],
        compiler_params=params(32),
        cost_estimate=cost(2 * rows * cols * dim * dim, 6 * rows * cols * dim),
        name="mix1",
    )(pos, sums, red, exp, mix, g, rest, kernels)


def mix2_kernel(cells, high, wide, pos, sums, red, exp, mix, g_ref, rest, x_out, z, line, keep):
    rows, cols, dim = g_ref.shape
    gate = gate_row(sums, cells, red, exp)
    bounds = (jnp.where(pos[0] == 0, 1, 0), rows, jnp.where(pos[1] == 0, 1, 0), cols)
    mix_lines(g_ref, gate, mix, rest, z, 0, bounds)
    for i in range(high):
        keep[i * wide : i * wide + wide, :] = pooled_line(z, line, i, wide)
    x_out[...] = jnp.broadcast_to(keep[...].astype(BF), x_out.shape)


def mix2(pos, sums, red, exp, mix, g, rest, cells, high, wide, copies):
    rows, cols, dim = g.shape
    out = jax.ShapeDtypeStruct((copies, high * wide, dim), BF)
    return pl.pallas_call(
        functools.partial(mix2_kernel, cells, high, wide),
        grid=(1,),
        in_specs=level_specs(sums, red, exp, mix, 2) + wholes(g, rest),
        out_specs=whole(out),
        out_shape=out,
        scratch_shapes=[
            pltpu.VMEM((rows, cols, dim), F32),
            pltpu.VMEM((dim // 128, cols, 128), F32),
            pltpu.VMEM((high * wide, dim), F32),
        ],
        compiler_params=params(24),
        cost_estimate=cost(2 * rows * cols * dim * dim, 6 * rows * cols * dim),
        name="mix2",
    )(pos, sums, red, exp, mix, g, rest)


def everyones(copies):
    return lax.all_to_all(copies, "tile", 0, 0, tiled=True)


def query_slab(tile_map, pos, dw_kernel, se_reduce, se_expand, mix_weight, keys_of):
    high, wide, dim = tile_map.shape
    tiles = lax.axis_size("tile")
    cells = high * wide * tiles
    group = 2 * TILE_COLS
    rims, first = exchange_rims(tile_map, side_pieces(tile_map, 2, 1), 2, 1, lambda held: keys_of(0, held))
    g, rest, part = activate(tile_map, rims, dw_kernel, 0, 2, 1, 11)
    coarse, to_right, to_left = mix0(
        pos, everyones(part), se_reduce, se_expand, mix_weight, g, rest, cells, high // 2, wide // 2, 6, 3, 11
    )
    rims, second = exchange_rims(coarse, (to_right, to_left), 6, 3, lambda held: keys_of(1, held))
    g, rest, part = activate(coarse, rims, dw_kernel, 1, 6, 3, high // 2 + 7)
    size = (high // 2, wide // 2, high // 2 * (tiles // TILE_COLS))
    g, rest, part = mix1(
        pos, everyones(part), se_reduce, se_expand, mix_weight, g, rest, dw_kernel, cells // 4, size, 6
    )
    query = mix2(
        pos, everyones(part), se_reduce, se_expand, mix_weight, g, rest, cells // 16, high // 8, wide // 8, group
    )
    groups = [list(range(group * x, group * x + group)) for x in range(tiles // group)]
    slab = lax.all_to_all(query, "tile", 0, 0, tiled=True, axis_index_groups=groups)
    return slab.reshape(-1, dim), first, second


def body(
    features,
    dw_kernel,
    se_reduce,
    se_expand,
    mix_weight,
    norm_gain,
    kv_weight,
    kv_bias,
    proj_weight,
    proj_bias,
):
    tile_map = features[0]
    dim = tile_map.shape[-1]
    position = lax.axis_index("tile")
    pos = jnp.stack([position // TILE_COLS, position % TILE_COLS]).astype(jnp.int32)
    gain, kv_row, proj_row = norm_gain.reshape(1, dim), kv_bias.reshape(1, 2 * dim), proj_bias.reshape(1, dim)

    def keys_of(window, held):
        return keys_values(after_these(tile_map, held), gain, kv_weight, kv_row, window)

    slab, (kt0, vt0), (kt1, vt1) = query_slab(
        tile_map, pos, dw_kernel, se_reduce, se_expand, mix_weight, keys_of
    )
    slabs = lax.axis_size("tile") // (2 * TILE_COLS)
    own = position // (2 * TILE_COLS)
    others = []
    for step in range(1, slabs):
        pairs = [(t, t ^ 2 * TILE_COLS * step) for t in range(lax.axis_size("tile"))]
        others.append(lax.ppermute(slab, "tile", pairs))
    keys, values = (kt0, kt1), (vt0, vt1)
    place = jnp.stack([own]).astype(jnp.int32)
    started = attention(place, [slab], keys, values, tile_map, proj_weight, proj_row)
    place = jnp.stack([own ^ step for step in range(1, slabs)]).astype(jnp.int32)
    return attention(place, others, keys, values, tile_map, proj_weight, proj_row, started)[None]


def solution(mesh):
    in_specs = (P(("scene", "tile"), None, None, None), P(), P(), P(), P(), P(), P(), P(), P(), P())
    out_specs = P(("scene", "tile"), None, None, None)
    return jax.shard_map(body, mesh=mesh, in_specs=in_specs, out_specs=out_specs, check_vma=False)
```

```python
import functools

import jax
import jax.numpy as jnp
from jax import lax
from jax.experimental import pallas as pl
from jax.experimental.pallas import tpu as pltpu
from jax.sharding import PartitionSpec as P

HEADS = 24
TILE_COLS = 4
EPSILON = 1e-05
BF = jnp.bfloat16
F32 = jnp.float32
VM = pl.BlockSpec(memory_space=pltpu.VMEM)
LOG2E = 1.4426950408889634
QB = 256
KC = 512
UNROLL = 8


def kv_kernel(x_ref, gain_ref, w_ref, b_ref, kt_ref, vt_ref):
    dim = x_ref.shape[-1]
    tokens = x_ref.shape[0] * x_ref.shape[1]
    x = x_ref[...].reshape(tokens, dim).astype(F32)
    centre = jnp.mean(x, axis=1, keepdims=True)
    moved = x - centre
    spread = jnp.mean(jnp.square(moved), axis=1, keepdims=True)
    normed = (moved * lax.rsqrt(spread + EPSILON) * gain_ref[...].reshape(1, dim)).astype(BF)
    keys = (jnp.dot(normed, w_ref[:, :dim], preferred_element_type=F32) + b_ref[:dim].reshape(1, dim)).astype(BF)
    for group in range(dim // 128):
        kt_ref[group] = keys[:, 128 * group : 128 * group + 128]
    vals = jnp.dot(normed, w_ref[:, dim:], preferred_element_type=F32) + b_ref[dim:].reshape(1, dim)
    vt_ref[...] = vals.T.astype(BF)


def keys_values(tile_map, gain, weight, bias, window):
    win, _, dim = tile_map.shape
    step = 8
    tokens = step * win
    return pl.pallas_call(
        kv_kernel,
        grid=(win // step,),
        in_specs=[
            pl.BlockSpec((step, win, dim), lambda i: (i, window, 0)),
            pl.BlockSpec((dim,), lambda i: (0,)),
            pl.BlockSpec((dim, 2 * dim), lambda i: (0, 0)),
            pl.BlockSpec((2 * dim,), lambda i: (0,)),
        ],
        out_specs=[
            pl.BlockSpec((dim // 128, tokens, 128), lambda i: (0, i, 0)),
            pl.BlockSpec((dim, tokens), lambda i: (0, i)),
        ],
        out_shape=[
            jax.ShapeDtypeStruct((dim // 128, win * win, 128), BF),
            jax.ShapeDtypeStruct((dim, win * win), BF),
        ],
        compiler_params=pltpu.CompilerParams(vmem_limit_bytes=24 * 2**20),
        cost_estimate=pl.CostEstimate(
            flops=8 * win * win * dim * dim, bytes_accessed=8 * 2**20, transcendentals=0
        ),
        name="keys_values",
    )(tile_map, gain, weight, bias)


def attention_kernel(steps, *refs):
    slabs = len(steps)
    q_refs = refs[:slabs]
    kt_refs, vt_refs = refs[slabs : slabs + 2], refs[slabs + 2 : slabs + 4]
    x_ref, wp_ref, bp_ref = refs[slabs + 4 : slabs + 7]
    out_ref, qa, sb, mb, ot, stage, sems = refs[-7:]
    dim = x_ref.shape[2]
    length = kt_refs[0].shape[1]
    units = HEADS * slabs
    scale = (dim // HEADS) ** (-0.5) * LOG2E
    lane = lax.broadcasted_iota(jnp.int32, (1, 128), 1)
    for slab in range(slabs):
        for group in range(dim // 128):
            q = q_refs[slab][:, 128 * group : 128 * group + 128]
            for part in range(4):
                qa[slab, 4 * group + part] = jnp.where(lane // 32 == part, q, jnp.zeros_like(q))
    ones = jnp.ones((16, KC), BF)

    def score(unit, slot, w, start):
        head = unit // slabs
        s = lax.dot_general(
            kt_refs[w][head // 4, pl.ds(start, KC), :],
            qa[unit % slabs, head],
            (((1,), (1,)), ((), ())),
            preferred_element_type=F32,
        )
        sb[slot, w, pl.ds(start, KC), :] = s
        return jnp.max(s.reshape(KC // 8, 8, QB), axis=0)

    def step(unit, slot, following):
        if unit is not None:
            head = unit // slabs
            rows = pl.ds(pl.multiple_of(head * 32, 32), 32)
        for w in range(2):
            top = total = None
            if unit is not None:
                peak = jnp.max(mb[slot, w], axis=0, keepdims=True)
            for start in range(0, length, KC):
                high = score(following, 1 - slot, w, start)
                top = high if top is None else jnp.maximum(top, high)
                if unit is not None:
                    p = jnp.exp2((sb[slot, w, pl.ds(start, KC), :] - peak) * scale).astype(BF)
                    v = jnp.concatenate([vt_refs[w][rows, pl.ds(start, KC)], ones], axis=0)
                    o = jnp.dot(v, p, preferred_element_type=F32)
                    total = o if total is None else total + o
            mb[1 - slot, w] = top
            if unit is not None:
                ot[unit % slabs, w, rows, :] = (total[:32] / total[32:33]).astype(BF)

    step(None, 1, 0)

    def body(turn, _):
        for j in range(UNROLL):
            unit = UNROLL * turn + j
            step(unit, j % 2, jnp.minimum(unit + 1, units - 1))
        return 0

    lax.fori_loop(0, units // UNROLL, body, 0)

    win = x_ref.shape[1] // 2
    lines = QB // win
    copies = []
    for slab in range(slabs):
        own = lax.axis_index("tile") // (2 * TILE_COLS)
        place = pl.ds(pl.multiple_of((own ^ steps[slab]) * lines, lines), lines)
        for w in range(2):
            cols = slice(w * win, w * win + win)
            y = lax.dot_general(
                ot[slab, w], wp_ref[...], (((0,), (0,)), ((), ())), preferred_element_type=F32
            )
            y = y.reshape(2, 4, lines // 2, win // 4, dim).transpose(0, 2, 1, 3, 4).reshape(lines, win, dim)
            y = x_ref[place, cols, :].astype(F32) + y + bp_ref[...].reshape(1, dim)
            stage[slab, :, cols, :] = y.astype(BF)
        copy = pltpu.make_async_copy(stage.at[slab], out_ref.at[place], sems.at[slab])
        copy.start()
        copies.append(copy)
    for copy in copies:
        copy.wait()


def attention(steps, queries, keys, values, tile_map, wp, bp, started=None):
    rows, cols, dim = tile_map.shape
    slabs = len(queries)
    lines = QB * 2 // cols
    more = [] if started is None else [started]
    anywhere = pl.BlockSpec(memory_space=pl.ANY)
    return pl.pallas_call(
        functools.partial(attention_kernel, steps),
        in_specs=[VM] * (slabs + 7) + [anywhere] * len(more),
        out_specs=anywhere,
        out_shape=jax.ShapeDtypeStruct(tile_map.shape, BF),
        input_output_aliases={slabs + 7: 0} if more else {},
        scratch_shapes=[
            pltpu.VMEM((slabs, HEADS, QB, 128), BF),
            pltpu.VMEM((2, 2, rows * cols // 2, QB), F32),
            pltpu.VMEM((2, 2, 8, QB), F32),
            pltpu.VMEM((slabs, 2, dim, QB), BF),
            pltpu.VMEM((slabs, lines, cols, dim), BF),
            pltpu.SemaphoreType.DMA((slabs,)),
        ],
        compiler_params=pltpu.CompilerParams(vmem_limit_bytes=40 * 2**20),
        cost_estimate=pl.CostEstimate(
            flops=8 * slabs * QB * 1024 * dim * 8,
            bytes_accessed=12 * 2**20,
            transcendentals=48 * slabs * QB * 1024,
        ),
        name="attention",
    )(*queries, *keys, *values, tile_map, wp, bp, *more)


def whole(array):
    return pl.BlockSpec(array.shape, lambda *i: (0,) * len(array.shape), pipeline_mode=pl.Buffered(1))


def wholes(*arrays):
    return [whole(array) for array in arrays]


def at_level(array, level):
    shape = (None,) + array.shape[1:]
    return pl.BlockSpec(shape, lambda *i: (level,) + (0,) * (len(shape) - 1), pipeline_mode=pl.Buffered(1))


def position():
    index = lax.axis_index("tile")
    return index // TILE_COLS, index % TILE_COLS


def params(mib):
    return pltpu.CompilerParams(vmem_limit_bytes=mib * 2**20)


def cost(flops, size):
    return pl.CostEstimate(flops=flops, bytes_accessed=size, transcendentals=0)


def round_up(count, unit):
    return -(-count // unit) * unit


def side_pieces_kernel(before, after, left_ref, right_ref, to_right, to_left, keep_r, keep_l):
    high = left_ref.shape[0]
    span = right_ref.shape[1]
    for r in range(high):
        keep_r[r * before : r * before + before, :] = right_ref[r].astype(F32)[span - before :]
        keep_l[r * after : r * after + after, :] = left_ref[r].astype(F32)[:after]
    to_right[...] = keep_r[...].astype(BF)
    to_left[...] = keep_l[...].astype(BF)


def side_pieces(tile, before, after):
    high, wide, dim = tile.shape
    return pl.pallas_call(
        functools.partial(side_pieces_kernel, before, after),
        grid=(1,),
        in_specs=[
            pl.BlockSpec((high, 16, dim), lambda i: (0, 0, 0)),
            pl.BlockSpec((high, 16, dim), lambda i: (0, wide // 16 - 1, 0)),
        ],
        out_shape=[
            jax.ShapeDtypeStruct((high * before, dim), BF),
            jax.ShapeDtypeStruct((high * after, dim), BF),
        ],
        scratch_shapes=[pltpu.VMEM((high * before, dim), F32), pltpu.VMEM((high * after, dim), F32)],
        compiler_params=params(12),
        cost_estimate=cost(0, 2 * 2**20),
        name="side_pieces",
    )(tile, tile)


def line_pieces_kernel(before, after, high, top_ref, low_ref, left_ref, right_ref, to_low, to_up, keep_d, keep_u, side_l, side_r):
    wide = top_ref.shape[1]
    full = before + wide + after
    side_l[...] = left_ref[...].astype(F32)
    side_r[...] = right_ref[...].astype(F32)
    keep_d[...] = jnp.zeros_like(keep_d)
    keep_u[...] = jnp.zeros_like(keep_u)

    def fill(keep, line, r, values):
        base = line * full
        keep[base : base + before, :] = side_l[r * before : r * before + before, :]
        keep[base + before : base + before + wide, :] = values
        keep[base + before + wide : base + full, :] = side_r[r * after : r * after + after, :]

    for line in range(before):
        fill(keep_d, line, high - before + line, low_ref[line].astype(F32))
    for line in range(after):
        fill(keep_u, line, line, top_ref[line].astype(F32))
    to_low[...] = keep_d[...].astype(BF)
    to_up[...] = keep_u[...].astype(BF)


def line_pieces(tile, left, right, before, after):
    high, wide, dim = tile.shape
    full = before + wide + after
    down = round_up(before * full, 16)
    up = round_up(after * full, 16)
    low_size = before if high % before == 0 else 8
    assert high % low_size == 0
    return pl.pallas_call(
        functools.partial(line_low_kernel, low_size, before, after, high),
        grid=(1,),
        in_specs=[
            pl.BlockSpec((after if high % after == 0 else 8, wide, dim), lambda i: (0, 0, 0)),
            pl.BlockSpec((low_size, wide, dim), lambda i: (high // low_size - 1, 0, 0)),
            whole(left),
            whole(right),
        ],
        out_shape=[jax.ShapeDtypeStruct((down, dim), BF), jax.ShapeDtypeStruct((up, dim), BF)],
        scratch_shapes=[
            pltpu.VMEM((down, dim), F32),
            pltpu.VMEM((up, dim), F32),
            pltpu.VMEM(left.shape, F32),
            pltpu.VMEM(right.shape, F32),
        ],
        compiler_params=params(12),
        cost_estimate=cost(0, 2**20),
        name="line_pieces",
    )(tile, tile, left, right)


def line_low_kernel(low_size, before, after, high, top_ref, low_ref, *rest):
    line_pieces_kernel(before, after, high, top_ref, low_ref.at[pl.ds(low_size - before, before)], *rest)


def moved_by(value, rows, cols):
    count = lax.axis_size("tile")
    pairs = []
    for t in range(count):
        r, c = t // TILE_COLS + rows, t % TILE_COLS + cols
        if 0 <= r < count // TILE_COLS and 0 <= c < TILE_COLS:
            pairs.append((t, r * TILE_COLS + c))
    return lax.ppermute(value, "tile", pairs)


def after_these(value, *others):
    return lax.optimization_barrier((value,) + others)[0]


def exchange_rims(tile, pieces, before, after, beside):
    left = moved_by(pieces[0], 0, 1)
    right = moved_by(pieces[1], 0, -1)
    down, up = line_pieces(tile, left, right, before, after)
    above, below = moved_by(down, 1, 0), moved_by(up, -1, 0)
    result = beside(down)
    above, below, *result = lax.optimization_barrier((above, below, *result))
    return (left, right, above, below), result


def erf_gelu(y):
    return 0.5 * y * (1.0 + lax.erf(y * 0.7071067811865476))


def fill_padded(x_ref, rims, before, after, padded, stage):
    high, wide, _ = x_ref.shape
    full = before + wide + after
    left, right, above, below = rims

    def line(r, _):
        padded[r + before, before : before + wide, :] = x_ref[r].astype(F32)
        return 0

    lax.fori_loop(0, high, line, 0)
    stage[: left.shape[0], :] = left[...].astype(F32)
    for r in range(high):
        padded[r + before, 0:before, :] = stage[r * before : r * before + before, :]
    stage[: right.shape[0], :] = right[...].astype(F32)
    for r in range(high):
        padded[r + before, before + wide : full, :] = stage[r * after : r * after + after, :]
    stage[: above.shape[0], :] = above[...].astype(F32)
    for r in range(before):
        padded[r, 0:full, :] = stage[r * full : r * full + full, :]
    stage[: below.shape[0], :] = below[...].astype(F32)
    for r in range(after):
        padded[before + high + r, 0:full, :] = stage[r * full : r * full + full, :]


def conv_gelu(padded, kernel_ref, g_ref, own_rows, own_cols, part_ref):
    rows, cols, dim = g_ref.shape
    column = lax.broadcasted_iota(jnp.int32, (cols, 128), 0)
    mine = (column >= own_cols[0]) & (column < own_cols[1])
    for group in range(dim // 128):
        lanes = slice(128 * group, 128 * group + 128)
        taps = [[kernel_ref[a, b : b + 1, lanes].astype(F32) for b in range(3)] for a in range(3)]

        def line(r, total):
            y = None
            for a in range(3):
                for b in range(3):
                    term = padded[r + a, b : b + cols, lanes] * taps[a][b]
                    y = term if y is None else y + term
            g = erf_gelu(y)
            g_ref[r, :, lanes] = g
            counted = jnp.sum(jnp.where(mine, g, 0.0).reshape(cols // 8, 8, 128), axis=0)
            return total + jnp.where((r >= own_rows[0]) & (r < own_rows[1]), counted, 0.0)

        total = lax.fori_loop(0, rows, line, jnp.zeros((8, 128), F32), unroll=True)
        total = jnp.sum(total, axis=0, keepdims=True)
        part_ref[:, group, :] += jnp.broadcast_to(total, (part_ref.shape[0], 128))


def copy_centre(padded, rest_ref):
    rows, cols, _ = rest_ref.shape

    def line(r, _):
        rest_ref[r] = padded[r + 1, 1 : 1 + cols, :].astype(BF)
        return 0

    lax.fori_loop(0, rows, line, 0)


def thirds(row):
    high = row.astype(BF).astype(F32)
    mid = (row - high).astype(BF).astype(F32)
    low = row - high - mid
    index = lax.broadcasted_iota(jnp.int32, (16, row.shape[1]), 0)
    block = jnp.where(index == 0, high, jnp.where(index == 1, mid, jnp.where(index == 2, low, 0.0)))
    return block.astype(BF)


def gate_row(sums_ref, cells, reduce_ref, expand_ref):
    total = jnp.sum(sums_ref[...], axis=0)
    groups = reduce_ref.shape[1] // 128
    mean = jnp.concatenate([total[group : group + 1] for group in range(groups)], axis=1) / cells
    inner = lax.dot_general(
        thirds(mean), reduce_ref[...], (((1,), (1,)), ((), ())), preferred_element_type=F32
    )
    inner = jnp.sum(inner, axis=0, keepdims=True)
    inner = erf_gelu(inner)
    outer = jnp.sum(jnp.dot(thirds(inner), expand_ref[...], preferred_element_type=F32), axis=0, keepdims=True)
    return 1.0 / (1.0 + jnp.exp(-outer))


def mix_lines(g_ref, gate, mix_ref, rest_ref, z_ref, first, bounds):
    rows, cols, dim = g_ref.shape
    row_low, row_high, col_low, col_high = bounds
    column = lax.broadcasted_iota(jnp.int32, (cols, 1), 0)
    inside = (column >= col_low) & (column < col_high)
    u = (g_ref[...] * gate).astype(BF).reshape(rows * cols, dim)
    product = jnp.dot(u, mix_ref[...], preferred_element_type=F32).reshape(rows, cols, dim)
    for k in range(rows):
        z = (rest_ref[k].astype(F32) + product[k]).astype(BF).astype(F32)
        keep = inside & (first + k >= row_low) & (first + k < row_high)
        z_ref[first + k] = jnp.where(keep, z, -jnp.inf)


def pooled_line(z_ref, line_ref, i, count):
    most = jnp.maximum(jnp.maximum(z_ref[2 * i], z_ref[2 * i + 1]), z_ref[2 * i + 2])
    groups = []
    for group in range(line_ref.shape[0]):
        line_ref[group] = most[:, 128 * group : 128 * group + 128]
        parts = [line_ref[group, pl.ds(s, count, stride=2), :] for s in range(3)]
        groups.append(jnp.maximum(jnp.maximum(parts[0], parts[1]), parts[2]))
    return jnp.concatenate(groups, axis=1)


def act_kernel(before, after, x_ref, l_ref, r_ref, a_ref, b_ref, kernel_ref, g_ref, rest_ref, part_ref, padded, stage):
    high, wide, _ = x_ref.shape
    step = g_ref.shape[0]
    turn = pl.program_id(0)

    @pl.when(turn == 0)
    def _():
        fill_padded(x_ref, (l_ref, r_ref, a_ref, b_ref), before, after, padded, stage)
        part_ref[...] = jnp.zeros_like(part_ref)

    own = before - 1
    block = padded.at[pl.ds(turn * step, step + 2)]
    copy_centre(block, rest_ref)
    conv_gelu(block, kernel_ref, g_ref, (own - turn * step, own + high - turn * step), (own, own + wide), part_ref)


def activate(tile, rims, kernels, level, before, after, step):
    high, wide, dim = tile.shape
    rows, cols = high + before + after - 2, round_up(wide + before + after - 2, 8)
    stage = max(r.shape[0] for r in rims)
    copies = lax.axis_size("tile")
    block = pl.BlockSpec((step, cols, dim), lambda i: (i, 0, 0))
    return pl.pallas_call(
        functools.partial(act_kernel, before, after),
        grid=(rows // step,),
        in_specs=wholes(tile, *rims) + [at_level(kernels, level)],
        out_specs=[block, block, pl.BlockSpec((copies, 8, 128), lambda i: (0, 0, 0))],
        out_shape=[
            jax.ShapeDtypeStruct((rows, cols, dim), F32),
            jax.ShapeDtypeStruct((rows, cols, dim), BF),
            jax.ShapeDtypeStruct((copies, 8, 128), F32),
        ],
        scratch_shapes=[
            pltpu.VMEM((rows + 2, round_up(cols + 2, 8), dim), F32),
            pltpu.VMEM((stage, dim), F32),
        ],
        compiler_params=params(28 if level == 0 else 20),
        cost_estimate=cost(400 * rows * cols * dim, 6 * rows * cols * dim),
        name="activate",
    )(tile, *rims, kernels)


def mix0_kernel(cells, before, after, sums, red, exp, mix, g_ref, rest, x_out, to_right, to_left, gates, z, line, keep_r, keep_l):
    step, cols, dim = g_ref.shape
    high, wide, _ = x_out.shape
    turn = pl.program_id(0)

    @pl.when(turn == 0)
    def _():
        gates[...] = jnp.broadcast_to(gate_row(sums, cells, red, exp), gates.shape)

    pos = position()
    bounds = (jnp.where(pos[0] == 0, 1, 0), z.shape[0], jnp.where(pos[1] == 0, 1, 0), cols)
    mix_lines(g_ref, gates[:1, :], mix, rest, z, turn * step, bounds)

    @pl.when(turn == pl.num_programs(0) - 1)
    def _():
        for i in range(high):
            out = pooled_line(z, line, i, wide)
            x_out[i] = out.astype(BF)
            keep_r[i * before : i * before + before, :] = out[wide - before :]
            keep_l[i * after : i * after + after, :] = out[:after]
        to_right[...] = keep_r[...].astype(BF)
        to_left[...] = keep_l[...].astype(BF)


def level_specs(sums, red, exp, mix, level):
    return [whole(sums), at_level(red, level), at_level(exp, level), at_level(mix, level)]


def mix0(sums, red, exp, mix, g, rest, cells, high, wide, before, after, step):
    rows, cols, dim = g.shape
    block = pl.BlockSpec((step, cols, dim), lambda i: (i, 0, 0))
    outs = [
        jax.ShapeDtypeStruct((high, wide, dim), BF),
        jax.ShapeDtypeStruct((high * before, dim), BF),
        jax.ShapeDtypeStruct((high * after, dim), BF),
    ]
    return pl.pallas_call(
        functools.partial(mix0_kernel, cells, before, after),
        grid=(rows // step,),
        in_specs=level_specs(sums, red, exp, mix, 0) + [block, block],
        out_specs=wholes(*outs),
        out_shape=outs,
        scratch_shapes=[
            pltpu.VMEM((8, dim), F32),
            pltpu.VMEM((rows, cols, dim), F32),
            pltpu.VMEM((dim // 128, cols, 128), F32),
            pltpu.VMEM((high * before, dim), F32),
            pltpu.VMEM((high * after, dim), F32),
        ],
        compiler_params=params(32),
        cost_estimate=cost(2 * rows * cols * dim * dim, 6 * rows * cols * dim),
        name="mix0",
    )(sums, red, exp, mix, g, rest)


def mix1_kernel(cells, size, before, sums, red, exp, mix, g_ref, rest, kernel, g_out, rest_out, part, z, line, padded):
    rows, cols, dim = g_ref.shape
    side_r, side_c, map_side = size
    gate = gate_row(sums, cells, red, exp)
    shift = before - 1
    pos = position()
    row_low = shift - pos[0] * side_r
    col_low = shift - pos[1] * side_c
    mix_lines(g_ref, gate, mix, rest, z, 0, (row_low, row_low + map_side, col_low, col_low + map_side))
    count_r, count_c = padded.shape[0], (cols - 1) // 2
    row_two = 2 - pos[0] * (side_r // 2)
    col_two = 2 - pos[1] * (side_c // 2)
    column = lax.broadcasted_iota(jnp.int32, (count_c, 1), 0)
    inside = (column >= col_two) & (column < col_two + map_side // 2)
    for i in range(count_r):
        out = pooled_line(z, line, i, count_c)
        keep = inside & (i >= row_two) & (i < row_two + map_side // 2)
        padded[i, 0:count_c, :] = jnp.where(keep, out, 0.0)
    copy_centre(padded, rest_out)
    part[...] = jnp.zeros_like(part)
    conv_gelu(padded, kernel, g_out, (1, 1 + side_r // 2), (1, 1 + side_c // 2), part)


def mix1(sums, red, exp, mix, g, rest, kernels, cells, size, before):
    rows, cols, dim = g.shape
    out_rows, out_cols = (rows - 1) // 2 - 2, round_up((cols - 1) // 2 - 2, 8)
    outs = [
        jax.ShapeDtypeStruct((out_rows, out_cols, dim), F32),
        jax.ShapeDtypeStruct((out_rows, out_cols, dim), BF),
        jax.ShapeDtypeStruct(sums.shape, F32),
    ]
    return pl.pallas_call(
        functools.partial(mix1_kernel, cells, size, before),
        grid=(1,),
        in_specs=level_specs(sums, red, exp, mix, 1) + wholes(g, rest) + [at_level(kernels, 2)],
        out_specs=wholes(*outs),
        out_shape=outs,
        scratch_shapes=[
            pltpu.VMEM((rows, cols, dim), F32),
            pltpu.VMEM((dim // 128, cols, 128), F32),
            pltpu.VMEM((out_rows + 2, round_up(out_cols + 2, 8), dim), F32),
        ],
        compiler_params=params(18),
        cost_estimate=cost(2 * rows * cols * dim * dim, 6 * rows * cols * dim),
        name="mix1",
    )(sums, red, exp, mix, g, rest, kernels)


def mix2_kernel(cells, high, wide, sums, red, exp, mix, g_ref, rest, x_out, z, line, keep):
    rows, cols, dim = g_ref.shape
    gate = gate_row(sums, cells, red, exp)
    pos = position()
    bounds = (jnp.where(pos[0] == 0, 1, 0), rows, jnp.where(pos[1] == 0, 1, 0), cols)
    mix_lines(g_ref, gate, mix, rest, z, 0, bounds)
    for i in range(high):
        keep[i * wide : i * wide + wide, :] = pooled_line(z, line, i, wide)
    x_out[...] = jnp.broadcast_to(keep[...].astype(BF), x_out.shape)


def mix2(sums, red, exp, mix, g, rest, cells, high, wide, copies):
    rows, cols, dim = g.shape
    out = jax.ShapeDtypeStruct((copies, high * wide, dim), BF)
    return pl.pallas_call(
        functools.partial(mix2_kernel, cells, high, wide),
        grid=(1,),
        in_specs=level_specs(sums, red, exp, mix, 2) + wholes(g, rest),
        out_specs=whole(out),
        out_shape=out,
        scratch_shapes=[
            pltpu.VMEM((rows, cols, dim), F32),
            pltpu.VMEM((dim // 128, cols, 128), F32),
            pltpu.VMEM((high * wide, dim), F32),
        ],
        compiler_params=params(10),
        cost_estimate=cost(2 * rows * cols * dim * dim, 6 * rows * cols * dim),
        name="mix2",
    )(sums, red, exp, mix, g, rest)


def everyones(copies):
    return lax.all_to_all(copies, "tile", 0, 0, tiled=True)


def query_slab(tile_map, dw_kernel, se_reduce, se_expand, mix_weight, keys_of):
    high, wide, dim = tile_map.shape
    tiles = lax.axis_size("tile")
    cells = high * wide * tiles
    group = 2 * TILE_COLS
    rims, first = exchange_rims(tile_map, side_pieces(tile_map, 2, 1), 2, 1, lambda held: keys_of(0, held))
    g, rest, part = activate(tile_map, rims, dw_kernel, 0, 2, 1, 11)
    coarse, to_right, to_left = mix0(
        everyones(part), se_reduce, se_expand, mix_weight, g, rest, cells, high // 2, wide // 2, 6, 3, 11
    )
    rims, second = exchange_rims(coarse, (to_right, to_left), 6, 3, lambda held: keys_of(1, held))
    g, rest, part = activate(coarse, rims, dw_kernel, 1, 6, 3, high // 2 + 7)
    size = (high // 2, wide // 2, high // 2 * (tiles // TILE_COLS))
    g, rest, part = mix1(
        everyones(part), se_reduce, se_expand, mix_weight, g, rest, dw_kernel, cells // 4, size, 6
    )
    query = mix2(
        everyones(part), se_reduce, se_expand, mix_weight, g, rest, cells // 16, high // 8, wide // 8, group
    )
    groups = [list(range(group * x, group * x + group)) for x in range(tiles // group)]
    slab = lax.all_to_all(query, "tile", 0, 0, tiled=True, axis_index_groups=groups)
    return slab.reshape(-1, dim), first, second


def body(
    features,
    dw_kernel,
    se_reduce,
    se_expand,
    mix_weight,
    norm_gain,
    kv_weight,
    kv_bias,
    proj_weight,
    proj_bias,
):
    tile_map = features[0]
    se_reduce = jnp.swapaxes(se_reduce, 1, 2)

    def keys_of(window, held):
        return keys_values(after_these(tile_map, held), norm_gain, kv_weight, kv_bias, window)

    slab, (kt0, vt0), (kt1, vt1) = query_slab(tile_map, dw_kernel, se_reduce, se_expand, mix_weight, keys_of)
    tiles = lax.axis_size("tile")
    group = 2 * TILE_COLS
    steps = tuple(range(1, tiles // group))
    others = [lax.ppermute(slab, "tile", [(t, t ^ group * step) for t in range(tiles)]) for step in steps]
    rest = ((kt0, kt1), (vt0, vt1), tile_map, proj_weight, proj_bias)
    started = attention((0,), [slab], *rest)
    return attention(steps, others, *rest, started)[None]


def solution(mesh):
    in_specs = (P(("scene", "tile"), None, None, None), P(), P(), P(), P(), P(), P(), P(), P(), P())
    out_specs = P(("scene", "tile"), None, None, None)
    return jax.shard_map(body, mesh=mesh, in_specs=in_specs, out_specs=out_specs, check_vma=False)
```

```python
import functools

import jax
import jax.numpy as jnp
from jax import lax
from jax.experimental import pallas as pl
from jax.experimental.pallas import tpu as pltpu
from jax.sharding import PartitionSpec as P

HEADS = 24
TILE_COLS = 4
EPSILON = 1e-05
BF = jnp.bfloat16
F32 = jnp.float32
VM = pl.BlockSpec(memory_space=pltpu.VMEM)
LOG2E = 1.4426950408889634
QB = 256
KC = 512
UNROLL = 8


def kv_kernel(x_ref, gain_ref, w_ref, b_ref, kt_ref, vt_ref):
    dim = x_ref.shape[-1]
    tokens = x_ref.shape[0] * x_ref.shape[1]
    x = x_ref[...].reshape(tokens, dim).astype(F32)
    centre = jnp.mean(x, axis=1, keepdims=True)
    moved = x - centre
    spread = jnp.mean(jnp.square(moved), axis=1, keepdims=True)
    normed = (moved * lax.rsqrt(spread + EPSILON) * gain_ref[...].reshape(1, dim)).astype(BF)
    keys = (jnp.dot(normed, w_ref[:, :dim], preferred_element_type=F32) + b_ref[:dim].reshape(1, dim)).astype(BF)
    for group in range(dim // 128):
        kt_ref[group] = keys[:, 128 * group : 128 * group + 128]
    vals = jnp.dot(normed, w_ref[:, dim:], preferred_element_type=F32) + b_ref[dim:].reshape(1, dim)
    vt_ref[...] = vals.T.astype(BF)


def keys_values(tile_map, gain, weight, bias, window):
    win, _, dim = tile_map.shape
    step = 8
    tokens = step * win
    return pl.pallas_call(
        kv_kernel,
        grid=(win // step,),
        in_specs=[
            pl.BlockSpec((step, win, dim), lambda i: (i, window, 0)),
            pl.BlockSpec((dim,), lambda i: (0,)),
            pl.BlockSpec((dim, 2 * dim), lambda i: (0, 0)),
            pl.BlockSpec((2 * dim,), lambda i: (0,)),
        ],
        out_specs=[
            pl.BlockSpec((dim // 128, tokens, 128), lambda i: (0, i, 0)),
            pl.BlockSpec((dim, tokens), lambda i: (0, i)),
        ],
        out_shape=[
            jax.ShapeDtypeStruct((dim // 128, win * win, 128), BF),
            jax.ShapeDtypeStruct((dim, win * win), BF),
        ],
        compiler_params=pltpu.CompilerParams(vmem_limit_bytes=24 * 2**20),
        cost_estimate=pl.CostEstimate(
            flops=8 * win * win * dim * dim, bytes_accessed=8 * 2**20, transcendentals=0
        ),
        name="keys_values",
    )(tile_map, gain, weight, bias)


def attention_kernel(steps, *refs):
    slabs = len(steps)
    q_refs = refs[:slabs]
    kt_refs, vt_refs = refs[slabs : slabs + 2], refs[slabs + 2 : slabs + 4]
    x_ref, wp_ref, bp_ref = refs[slabs + 4 : slabs + 7]
    out_ref, qa, sb, mb, ot, stage, sems = refs[-7:]
    dim = x_ref.shape[2]
    length = kt_refs[0].shape[1]
    units = HEADS * slabs
    scale = (dim // HEADS) ** (-0.5) * LOG2E
    lane = lax.broadcasted_iota(jnp.int32, (1, 128), 1)
    for slab in range(slabs):
        for group in range(dim // 128):
            q = q_refs[slab][:, 128 * group : 128 * group + 128]
            for part in range(4):
                qa[slab, 4 * group + part] = jnp.where(lane // 32 == part, q, jnp.zeros_like(q))
    ones = jnp.ones((16, KC), BF)

    def score(unit, slot, w, start):
        head = unit // slabs
        s = lax.dot_general(
            kt_refs[w][head // 4, pl.ds(start, KC), :],
            qa[unit % slabs, head],
            (((1,), (1,)), ((), ())),
            preferred_element_type=F32,
        )
        sb[slot, w, pl.ds(start, KC), :] = s
        return jnp.max(s.reshape(KC // 8, 8, QB), axis=0)

    def step(unit, slot, following):
        if unit is not None:
            head = unit // slabs
            rows = pl.ds(pl.multiple_of(head * 32, 32), 32)
        for w in range(2):
            top = total = None
            if unit is not None:
                peak = jnp.max(mb[slot, w], axis=0, keepdims=True)
            for start in range(0, length, KC):
                high = score(following, 1 - slot, w, start)
                top = high if top is None else jnp.maximum(top, high)
                if unit is not None:
                    p = jnp.exp2((sb[slot, w, pl.ds(start, KC), :] - peak) * scale).astype(BF)
                    v = jnp.concatenate([vt_refs[w][rows, pl.ds(start, KC)], ones], axis=0)
                    o = jnp.dot(v, p, preferred_element_type=F32)
                    total = o if total is None else total + o
            mb[1 - slot, w] = top
            if unit is not None:
                ot[unit % slabs, w, rows, :] = (total[:32] / total[32:33]).astype(BF)

    step(None, 1, 0)

    def body(turn, _):
        for j in range(UNROLL):
            unit = UNROLL * turn + j
            step(unit, j % 2, jnp.minimum(unit + 1, units - 1))
        return 0

    lax.fori_loop(0, units // UNROLL, body, 0)

    win = x_ref.shape[1] // 2
    lines = QB // win
    copies = []
    for slab in range(slabs):
        own = lax.axis_index("tile") // (2 * TILE_COLS)
        place = pl.ds(pl.multiple_of((own ^ steps[slab]) * lines, lines), lines)
        for w in range(2):
            cols = slice(w * win, w * win + win)
            y = lax.dot_general(
                ot[slab, w], wp_ref[...], (((0,), (0,)), ((), ())), preferred_element_type=F32
            )
            y = y.reshape(2, 4, lines // 2, win // 4, dim).transpose(0, 2, 1, 3, 4).reshape(lines, win, dim)
            y = x_ref[place, cols, :].astype(F32) + y + bp_ref[...].reshape(1, dim)
            stage[slab, :, cols, :] = y.astype(BF)
        copy = pltpu.make_async_copy(stage.at[slab], out_ref.at[place], sems.at[slab])
        copy.start()
        copies.append(copy)
    for copy in copies:
        copy.wait()


def attention(steps, queries, keys, values, tile_map, wp, bp, started=None):
    rows, cols, dim = tile_map.shape
    slabs = len(queries)
    lines = QB * 2 // cols
    more = [] if started is None else [started]
    anywhere = pl.BlockSpec(memory_space=pl.ANY)
    return pl.pallas_call(
        functools.partial(attention_kernel, steps),
        in_specs=[VM] * (slabs + 7) + [anywhere] * len(more),
        out_specs=anywhere,
        out_shape=jax.ShapeDtypeStruct(tile_map.shape, BF),
        input_output_aliases={slabs + 7: 0} if more else {},
        scratch_shapes=[
            pltpu.VMEM((slabs, HEADS, QB, 128), BF),
            pltpu.VMEM((2, 2, rows * cols // 2, QB), F32),
            pltpu.VMEM((2, 2, 8, QB), F32),
            pltpu.VMEM((slabs, 2, dim, QB), BF),
            pltpu.VMEM((slabs, lines, cols, dim), BF),
            pltpu.SemaphoreType.DMA((slabs,)),
        ],
        compiler_params=pltpu.CompilerParams(vmem_limit_bytes=40 * 2**20),
        cost_estimate=pl.CostEstimate(
            flops=8 * slabs * QB * 1024 * dim * 8,
            bytes_accessed=12 * 2**20,
            transcendentals=48 * slabs * QB * 1024,
        ),
        name="attention",
    )(*queries, *keys, *values, tile_map, wp, bp, *more)


def whole(array):
    return pl.BlockSpec(array.shape, lambda *i: (0,) * len(array.shape), pipeline_mode=pl.Buffered(1))


def wholes(*arrays):
    return [whole(array) for array in arrays]


def at_level(array, level):
    shape = (None,) + array.shape[1:]
    return pl.BlockSpec(shape, lambda *i: (level,) + (0,) * (len(shape) - 1), pipeline_mode=pl.Buffered(1))


def position():
    index = lax.axis_index("tile")
    return index // TILE_COLS, index % TILE_COLS


def params(mib):
    return pltpu.CompilerParams(vmem_limit_bytes=mib * 2**20)


def cost(flops, size):
    return pl.CostEstimate(flops=flops, bytes_accessed=size, transcendentals=0)


def round_up(count, unit):
    return -(-count // unit) * unit


def side_pieces_kernel(before, after, left_ref, right_ref, to_right, to_left, keep_r, keep_l):
    high = left_ref.shape[0]
    span = right_ref.shape[1]
    for r in range(high):
        keep_r[r * before : r * before + before, :] = right_ref[r].astype(F32)[span - before :]
        keep_l[r * after : r * after + after, :] = left_ref[r].astype(F32)[:after]
    to_right[...] = keep_r[...].astype(BF)
    to_left[...] = keep_l[...].astype(BF)


def side_pieces(tile, before, after):
    high, wide, dim = tile.shape
    return pl.pallas_call(
        functools.partial(side_pieces_kernel, before, after),
        grid=(1,),
        in_specs=[
            pl.BlockSpec((high, 16, dim), lambda i: (0, 0, 0)),
            pl.BlockSpec((high, 16, dim), lambda i: (0, wide // 16 - 1, 0)),
        ],
        out_shape=[
            jax.ShapeDtypeStruct((high * before, dim), BF),
            jax.ShapeDtypeStruct((high * after, dim), BF),
        ],
        scratch_shapes=[pltpu.VMEM((high * before, dim), F32), pltpu.VMEM((high * after, dim), F32)],
        compiler_params=params(12),
        cost_estimate=cost(0, 2 * 2**20),
        name="side_pieces",
    )(tile, tile)


def line_pieces_kernel(before, after, high, top_ref, low_ref, left_ref, right_ref, to_low, to_up, keep_d, keep_u, side_l, side_r):
    wide = top_ref.shape[1]
    full = before + wide + after
    side_l[...] = left_ref[...].astype(F32)
    side_r[...] = right_ref[...].astype(F32)
    keep_d[...] = jnp.zeros_like(keep_d)
    keep_u[...] = jnp.zeros_like(keep_u)

    def fill(keep, line, r, values):
        base = line * full
        keep[base : base + before, :] = side_l[r * before : r * before + before, :]
        keep[base + before : base + before + wide, :] = values
        keep[base + before + wide : base + full, :] = side_r[r * after : r * after + after, :]

    for line in range(before):
        fill(keep_d, line, high - before + line, low_ref[line].astype(F32))
    for line in range(after):
        fill(keep_u, line, line, top_ref[line].astype(F32))
    to_low[...] = keep_d[...].astype(BF)
    to_up[...] = keep_u[...].astype(BF)


def line_pieces(tile, left, right, before, after):
    high, wide, dim = tile.shape
    full = before + wide + after
    down = round_up(before * full, 16)
    up = round_up(after * full, 16)
    low_size = before if high % before == 0 else 8
    assert high % low_size == 0
    return pl.pallas_call(
        functools.partial(line_low_kernel, low_size, before, after, high),
        grid=(1,),
        in_specs=[
            pl.BlockSpec((after if high % after == 0 else 8, wide, dim), lambda i: (0, 0, 0)),
            pl.BlockSpec((low_size, wide, dim), lambda i: (high // low_size - 1, 0, 0)),
            whole(left),
            whole(right),
        ],
        out_shape=[jax.ShapeDtypeStruct((down, dim), BF), jax.ShapeDtypeStruct((up, dim), BF)],
        scratch_shapes=[
            pltpu.VMEM((down, dim), F32),
            pltpu.VMEM((up, dim), F32),
            pltpu.VMEM(left.shape, F32),
            pltpu.VMEM(right.shape, F32),
        ],
        compiler_params=params(12),
        cost_estimate=cost(0, 2**20),
        name="line_pieces",
    )(tile, tile, left, right)


def line_low_kernel(low_size, before, after, high, top_ref, low_ref, *rest):
    line_pieces_kernel(before, after, high, top_ref, low_ref.at[pl.ds(low_size - before, before)], *rest)


def moved_by(value, rows, cols):
    count = lax.axis_size("tile")
    pairs = []
    for t in range(count):
        r, c = t // TILE_COLS + rows, t % TILE_COLS + cols
        if 0 <= r < count // TILE_COLS and 0 <= c < TILE_COLS:
            pairs.append((t, r * TILE_COLS + c))
    return lax.ppermute(value, "tile", pairs)


def after_these(value, *others):
    return lax.optimization_barrier((value,) + others)[0]


def exchange_rims(tile, pieces, before, after, beside):
    left = moved_by(pieces[0], 0, 1)
    right = moved_by(pieces[1], 0, -1)
    down, up = line_pieces(tile, left, right, before, after)
    above, below = moved_by(down, 1, 0), moved_by(up, -1, 0)
    result = beside((left, right), down)
    above, below, *result = lax.optimization_barrier((above, below, *result))
    return (left, right, above, below), result


def erf_gelu(y):
    return 0.5 * y * (1.0 + lax.erf(y * 0.7071067811865476))


def fill_padded(x_ref, rims, before, after, padded, stage):
    high, wide, _ = x_ref.shape
    full = before + wide + after
    left, right, above, below = rims

    def line(r, _):
        padded[r + before, before : before + wide, :] = x_ref[r].astype(F32)
        return 0

    lax.fori_loop(0, high, line, 0)
    stage[: left.shape[0], :] = left[...].astype(F32)
    for r in range(high):
        padded[r + before, 0:before, :] = stage[r * before : r * before + before, :]
    stage[: right.shape[0], :] = right[...].astype(F32)
    for r in range(high):
        padded[r + before, before + wide : full, :] = stage[r * after : r * after + after, :]
    stage[: above.shape[0], :] = above[...].astype(F32)
    for r in range(before):
        padded[r, 0:full, :] = stage[r * full : r * full + full, :]
    stage[: below.shape[0], :] = below[...].astype(F32)
    for r in range(after):
        padded[before + high + r, 0:full, :] = stage[r * full : r * full + full, :]


def conv_gelu(padded, kernel_ref, g_ref, own_rows, own_cols, part_ref):
    rows, cols, dim = g_ref.shape
    column = lax.broadcasted_iota(jnp.int32, (cols, 128), 0)
    mine = (column >= own_cols[0]) & (column < own_cols[1])
    for group in range(dim // 128):
        lanes = slice(128 * group, 128 * group + 128)
        taps = [[kernel_ref[a, b : b + 1, lanes].astype(F32) for b in range(3)] for a in range(3)]

        def line(r, total):
            y = None
            for a in range(3):
                for b in range(3):
                    term = padded[r + a, b : b + cols, lanes] * taps[a][b]
                    y = term if y is None else y + term
            g = erf_gelu(y)
            g_ref[r, :, lanes] = g
            counted = jnp.sum(jnp.where(mine, g, 0.0).reshape(cols // 8, 8, 128), axis=0)
            return total + jnp.where((r >= own_rows[0]) & (r < own_rows[1]), counted, 0.0)

        total = lax.fori_loop(0, rows, line, jnp.zeros((8, 128), F32), unroll=True)
        total = jnp.sum(total, axis=0, keepdims=True)
        part_ref[:, group, :] += jnp.broadcast_to(total, (part_ref.shape[0], 128))


def copy_centre(padded, rest_ref):
    rows, cols, _ = rest_ref.shape

    def line(r, _):
        rest_ref[r] = padded[r + 1, 1 : 1 + cols, :].astype(BF)
        return 0

    lax.fori_loop(0, rows, line, 0)


def thirds(row):
    high = row.astype(BF).astype(F32)
    mid = (row - high).astype(BF).astype(F32)
    low = row - high - mid
    index = lax.broadcasted_iota(jnp.int32, (16, row.shape[1]), 0)
    block = jnp.where(index == 0, high, jnp.where(index == 1, mid, jnp.where(index == 2, low, 0.0)))
    return block.astype(BF)


def gate_row(sums_ref, cells, reduce_ref, expand_ref):
    total = jnp.sum(sums_ref[...], axis=0)
    groups = reduce_ref.shape[1] // 128
    mean = jnp.concatenate([total[group : group + 1] for group in range(groups)], axis=1) / cells
    inner = lax.dot_general(
        thirds(mean), reduce_ref[...], (((1,), (1,)), ((), ())), preferred_element_type=F32
    )
    inner = jnp.sum(inner, axis=0, keepdims=True)
    inner = erf_gelu(inner)
    outer = jnp.sum(jnp.dot(thirds(inner), expand_ref[...], preferred_element_type=F32), axis=0, keepdims=True)
    return 1.0 / (1.0 + jnp.exp(-outer))


def mix_lines(g_ref, gate, mix_ref, rest_ref, z_ref, lines, bounds):
    rows, cols, dim = g_ref.shape
    row_low, row_high, col_low, col_high = bounds
    column = lax.broadcasted_iota(jnp.int32, (cols, 1), 0)
    inside = (column >= col_low) & (column < col_high)
    u = (g_ref[...] * gate).astype(BF).reshape(rows * cols, dim)
    product = jnp.dot(u, mix_ref[...], preferred_element_type=F32).reshape(rows, cols, dim)
    for k in range(rows):
        z = (rest_ref[k].astype(F32) + product[k]).astype(BF).astype(F32)
        keep = inside & (lines[k] >= row_low) & (lines[k] < row_high)
        z_ref[lines[k]] = jnp.where(keep, z, -jnp.inf)


def pooled_line(z_ref, line_ref, i, count):
    most = jnp.maximum(jnp.maximum(z_ref[2 * i], z_ref[2 * i + 1]), z_ref[2 * i + 2])
    groups = []
    for group in range(line_ref.shape[0]):
        line_ref[group] = most[:, 128 * group : 128 * group + 128]
        parts = [line_ref[group, pl.ds(s, count, stride=2), :] for s in range(3)]
        groups.append(jnp.maximum(jnp.maximum(parts[0], parts[1]), parts[2]))
    return jnp.concatenate(groups, axis=1)


def act_kernel(before, after, x_ref, l_ref, r_ref, a_ref, b_ref, kernel_ref, g_ref, rest_ref, part_ref, padded, stage):
    high, wide, _ = x_ref.shape
    step = g_ref.shape[0]
    turn = pl.program_id(0)

    @pl.when(turn == 0)
    def _():
        fill_padded(x_ref, (l_ref, r_ref, a_ref, b_ref), before, after, padded, stage)
        part_ref[...] = jnp.zeros_like(part_ref)

    own = before - 1
    block = padded.at[pl.ds(turn * step, step + 2)]
    copy_centre(block, rest_ref)
    conv_gelu(block, kernel_ref, g_ref, (own - turn * step, own + high - turn * step), (own, own + wide), part_ref)


def activate(tile, rims, kernels, level, before, after, step):
    high, wide, dim = tile.shape
    rows, cols = high + before + after - 2, round_up(wide + before + after - 2, 8)
    stage = max(r.shape[0] for r in rims)
    copies = lax.axis_size("tile")
    block = pl.BlockSpec((step, cols, dim), lambda i: (i, 0, 0))
    return pl.pallas_call(
        functools.partial(act_kernel, before, after),
        grid=(rows // step,),
        in_specs=wholes(tile, *rims) + [at_level(kernels, level)],
        out_specs=[block, block, pl.BlockSpec((copies, 8, 128), lambda i: (0, 0, 0))],
        out_shape=[
            jax.ShapeDtypeStruct((rows, cols, dim), F32),
            jax.ShapeDtypeStruct((rows, cols, dim), BF),
            jax.ShapeDtypeStruct((copies, 8, 128), F32),
        ],
        scratch_shapes=[
            pltpu.VMEM((rows + 2, round_up(cols + 2, 8), dim), F32),
            pltpu.VMEM((stage, dim), F32),
        ],
        compiler_params=params(28 if level == 0 else 20),
        cost_estimate=cost(400 * rows * cols * dim, 6 * rows * cols * dim),
        name="activate",
    )(tile, *rims, kernels)


def fill_sides(x_ref, left_ref, right_ref, before, after, padded, stage):
    high, wide, _ = x_ref.shape
    full = before + wide + after

    def line(r, _):
        padded[r, before : before + wide, :] = x_ref[r].astype(F32)
        return 0

    lax.fori_loop(0, high, line, 0)
    stage[: left_ref.shape[0], :] = left_ref[...].astype(F32)
    for r in range(high):
        padded[r, 0:before, :] = stage[r * before : r * before + before, :]
    stage[: right_ref.shape[0], :] = right_ref[...].astype(F32)
    for r in range(high):
        padded[r, before + wide : full, :] = stage[r * after : r * after + after, :]


def inner_kernel(before, after, x_ref, l_ref, r_ref, kernel_ref, g_ref, rest_ref, part_ref, padded, stage):
    _, wide, _ = x_ref.shape
    step = g_ref.shape[0]
    turn = pl.program_id(0)

    @pl.when(turn == 0)
    def _():
        fill_sides(x_ref, l_ref, r_ref, before, after, padded, stage)
        part_ref[...] = jnp.zeros_like(part_ref)

    block = padded.at[pl.ds(turn * step, step + 2)]
    copy_centre(block, rest_ref)
    conv_gelu(block, kernel_ref, g_ref, (0, step), (before - 1, before - 1 + wide), part_ref)


def activate_inner(tile, left, right, kernels, before, after, step):
    high, wide, dim = tile.shape
    rows, cols = high - 2, round_up(wide + before + after - 2, 8)
    copies = lax.axis_size("tile")
    block = pl.BlockSpec((step, cols, dim), lambda i: (i, 0, 0))
    return pl.pallas_call(
        functools.partial(inner_kernel, before, after),
        grid=(rows // step,),
        in_specs=wholes(tile, left, right) + [at_level(kernels, 0)],
        out_specs=[block, block, pl.BlockSpec((copies, 8, 128), lambda i: (0, 0, 0))],
        out_shape=[
            jax.ShapeDtypeStruct((rows, cols, dim), F32),
            jax.ShapeDtypeStruct((rows, cols, dim), BF),
            jax.ShapeDtypeStruct((copies, 8, 128), F32),
        ],
        scratch_shapes=[
            pltpu.VMEM((high, round_up(cols + 2, 8), dim), F32),
            pltpu.VMEM((max(left.shape[0], right.shape[0]), dim), F32),
        ],
        compiler_params=params(28),
        cost_estimate=cost(400 * rows * cols * dim, 6 * rows * cols * dim),
        name="activate_inner",
    )(tile, left, right, kernels)


def edge_kernel(high, top_ref, low_ref, l_ref, r_ref, a_ref, b_ref, kernel_ref, sum_ref, g_ref, rest_ref, part_ref, upper, lower, side_l, side_r, stage):
    wide = top_ref.shape[1]
    full = wide + 3
    own = (1, 1 + wide)
    side_l[...] = l_ref[...].astype(F32)
    side_r[...] = r_ref[...].astype(F32)

    def fill(padded, at, r, values):
        padded[at, 0:2, :] = side_l[2 * r : 2 * r + 2, :]
        padded[at, 2 : 2 + wide, :] = values.astype(F32)
        padded[at, 2 + wide : full, :] = side_r[r : r + 1, :]

    for k in range(2):
        fill(upper, 2 + k, k, top_ref[k])
        fill(lower, k, high - 2 + k, low_ref[k])
    stage[: a_ref.shape[0], :] = a_ref[...].astype(F32)
    for k in range(2):
        upper[k, 0:full, :] = stage[k * full : k * full + full, :]
    stage[: b_ref.shape[0], :] = b_ref[...].astype(F32)
    lower[2, 0:full, :] = stage[0:full, :]
    part_ref[...] = sum_ref[...]
    copy_centre(upper, rest_ref.at[pl.ds(0, 2)])
    copy_centre(lower, rest_ref.at[pl.ds(2, 1)])
    conv_gelu(upper, kernel_ref, g_ref.at[pl.ds(0, 2)], (1, 2), own, part_ref)
    conv_gelu(lower, kernel_ref, g_ref.at[pl.ds(2, 1)], (0, 1), own, part_ref)


def activate_edge(tile, rims, kernels, part):
    high, wide, dim = tile.shape
    cols = round_up(wide + 1, 8)
    padded = round_up(cols + 2, 8)
    stage = max(r.shape[0] for r in rims)
    left, right, above, below = rims
    outs = [
        jax.ShapeDtypeStruct((3, cols, dim), F32),
        jax.ShapeDtypeStruct((3, cols, dim), BF),
        jax.ShapeDtypeStruct(part.shape, F32),
    ]
    return pl.pallas_call(
        functools.partial(edge_kernel, high),
        grid=(1,),
        in_specs=[
            pl.BlockSpec((2, wide, dim), lambda i: (0, 0, 0)),
            pl.BlockSpec((2, wide, dim), lambda i: (high // 2 - 1, 0, 0)),
        ]
        + wholes(*rims)
        + [at_level(kernels, 0), whole(part)],
        out_specs=wholes(*outs),
        out_shape=outs,
        scratch_shapes=[
            pltpu.VMEM((4, padded, dim), F32),
            pltpu.VMEM((3, padded, dim), F32),
            pltpu.VMEM(left.shape, F32),
            pltpu.VMEM(right.shape, F32),
            pltpu.VMEM((stage, dim), F32),
        ],
        compiler_params=params(12),
        cost_estimate=cost(400 * 3 * cols * dim, 6 * 3 * cols * dim),
        name="activate_edge",
    )(tile, tile, *rims, kernels, part)


def mix0_kernel(cells, before, after, sums, red, exp, mix, g_ref, rest, g_edge, rest_edge, x_out, to_right, to_left, gates, z, line, keep_r, keep_l):
    step, cols, dim = g_ref.shape
    high, wide, _ = x_out.shape
    turn = pl.program_id(0)

    pos = position()
    bounds = (jnp.where(pos[0] == 0, 1, 0), z.shape[0], jnp.where(pos[1] == 0, 1, 0), cols)

    @pl.when(turn == 0)
    def _():
        gates[...] = jnp.broadcast_to(gate_row(sums, cells, red, exp), gates.shape)
        mix_lines(g_edge, gates[:1, :], mix, rest_edge, z, (0, 1, z.shape[0] - 1), bounds)

    mix_lines(g_ref, gates[:1, :], mix, rest, z, [2 + turn * step + k for k in range(step)], bounds)

    @pl.when(turn == pl.num_programs(0) - 1)
    def _():
        for i in range(high):
            out = pooled_line(z, line, i, wide)
            x_out[i] = out.astype(BF)
            keep_r[i * before : i * before + before, :] = out[wide - before :]
            keep_l[i * after : i * after + after, :] = out[:after]
        to_right[...] = keep_r[...].astype(BF)
        to_left[...] = keep_l[...].astype(BF)


def level_specs(sums, red, exp, mix, level):
    return [whole(sums), at_level(red, level), at_level(exp, level), at_level(mix, level)]


def mix0(sums, red, exp, mix, g, rest, edges, cells, high, wide, before, after, step):
    rows, cols, dim = g.shape
    block = pl.BlockSpec((step, cols, dim), lambda i: (i, 0, 0))
    outs = [
        jax.ShapeDtypeStruct((high, wide, dim), BF),
        jax.ShapeDtypeStruct((high * before, dim), BF),
        jax.ShapeDtypeStruct((high * after, dim), BF),
    ]
    return pl.pallas_call(
        functools.partial(mix0_kernel, cells, before, after),
        grid=(rows // step,),
        in_specs=level_specs(sums, red, exp, mix, 0) + [block, block] + wholes(*edges),
        out_specs=wholes(*outs),
        out_shape=outs,
        scratch_shapes=[
            pltpu.VMEM((8, dim), F32),
            pltpu.VMEM((rows + 3, cols, dim), F32),
            pltpu.VMEM((dim // 128, cols, 128), F32),
            pltpu.VMEM((high * before, dim), F32),
            pltpu.VMEM((high * after, dim), F32),
        ],
        compiler_params=params(32),
        cost_estimate=cost(2 * rows * cols * dim * dim, 6 * rows * cols * dim),
        name="mix0",
    )(sums, red, exp, mix, g, rest, *edges)


def mix1_kernel(cells, size, before, sums, red, exp, mix, g_ref, rest, kernel, g_out, rest_out, part, z, line, padded):
    rows, cols, dim = g_ref.shape
    side_r, side_c, map_side = size
    gate = gate_row(sums, cells, red, exp)
    shift = before - 1
    pos = position()
    row_low = shift - pos[0] * side_r
    col_low = shift - pos[1] * side_c
    mix_lines(g_ref, gate, mix, rest, z, range(rows), (row_low, row_low + map_side, col_low, col_low + map_side))
    count_r, count_c = padded.shape[0], (cols - 1) // 2
    row_two = 2 - pos[0] * (side_r // 2)
    col_two = 2 - pos[1] * (side_c // 2)
    column = lax.broadcasted_iota(jnp.int32, (count_c, 1), 0)
    inside = (column >= col_two) & (column < col_two + map_side // 2)
    for i in range(count_r):
        out = pooled_line(z, line, i, count_c)
        keep = inside & (i >= row_two) & (i < row_two + map_side // 2)
        padded[i, 0:count_c, :] = jnp.where(keep, out, 0.0)
    copy_centre(padded, rest_out)
    part[...] = jnp.zeros_like(part)
    conv_gelu(padded, kernel, g_out, (1, 1 + side_r // 2), (1, 1 + side_c // 2), part)


def mix1(sums, red, exp, mix, g, rest, kernels, cells, size, before):
    rows, cols, dim = g.shape
    out_rows, out_cols = (rows - 1) // 2 - 2, round_up((cols - 1) // 2 - 2, 8)
    outs = [
        jax.ShapeDtypeStruct((out_rows, out_cols, dim), F32),
        jax.ShapeDtypeStruct((out_rows, out_cols, dim), BF),
        jax.ShapeDtypeStruct(sums.shape, F32),
    ]
    return pl.pallas_call(
        functools.partial(mix1_kernel, cells, size, before),
        grid=(1,),
        in_specs=level_specs(sums, red, exp, mix, 1) + wholes(g, rest) + [at_level(kernels, 2)],
        out_specs=wholes(*outs),
        out_shape=outs,
        scratch_shapes=[
            pltpu.VMEM((rows, cols, dim), F32),
            pltpu.VMEM((dim // 128, cols, 128), F32),
            pltpu.VMEM((out_rows + 2, round_up(out_cols + 2, 8), dim), F32),
        ],
        compiler_params=params(18),
        cost_estimate=cost(2 * rows * cols * dim * dim, 6 * rows * cols * dim),
        name="mix1",
    )(sums, red, exp, mix, g, rest, kernels)


def mix2_kernel(cells, high, wide, sums, red, exp, mix, g_ref, rest, x_out, z, line, keep):
    rows, cols, dim = g_ref.shape
    gate = gate_row(sums, cells, red, exp)
    pos = position()
    bounds = (jnp.where(pos[0] == 0, 1, 0), rows, jnp.where(pos[1] == 0, 1, 0), cols)
    mix_lines(g_ref, gate, mix, rest, z, range(rows), bounds)
    for i in range(high):
        keep[i * wide : i * wide + wide, :] = pooled_line(z, line, i, wide)
    x_out[...] = jnp.broadcast_to(keep[...].astype(BF), x_out.shape)


def mix2(sums, red, exp, mix, g, rest, cells, high, wide, copies):
    rows, cols, dim = g.shape
    out = jax.ShapeDtypeStruct((copies, high * wide, dim), BF)
    return pl.pallas_call(
        functools.partial(mix2_kernel, cells, high, wide),
        grid=(1,),
        in_specs=level_specs(sums, red, exp, mix, 2) + wholes(g, rest),
        out_specs=whole(out),
        out_shape=out,
        scratch_shapes=[
            pltpu.VMEM((rows, cols, dim), F32),
            pltpu.VMEM((dim // 128, cols, 128), F32),
            pltpu.VMEM((high * wide, dim), F32),
        ],
        compiler_params=params(10),
        cost_estimate=cost(2 * rows * cols * dim * dim, 6 * rows * cols * dim),
        name="mix2",
    )(sums, red, exp, mix, g, rest)


def everyones(copies):
    return lax.all_to_all(copies, "tile", 0, 0, tiled=True)


def query_slab(tile_map, dw_kernel, se_reduce, se_expand, mix_weight, keys_of):
    high, wide, dim = tile_map.shape
    tiles = lax.axis_size("tile")
    cells = high * wide * tiles
    group = 2 * TILE_COLS
    inner = lambda sides, held: activate_inner(after_these(tile_map, held), *sides, dw_kernel, 2, 1, 10)
    rims, (g, rest, part) = exchange_rims(tile_map, side_pieces(tile_map, 2, 1), 2, 1, inner)
    g_edge, rest_edge, part = activate_edge(tile_map, rims, dw_kernel, part)
    coarse, to_right, to_left = mix0(
        everyones(part), se_reduce, se_expand, mix_weight, g, rest, (g_edge, rest_edge), cells, high // 2, wide // 2, 6, 3, 10
    )
    both = lambda sides, held: keys_of(0, held) + keys_of(1, held)
    rims, (kt0, vt0, kt1, vt1) = exchange_rims(coarse, (to_right, to_left), 6, 3, both)
    g, rest, part = activate(coarse, rims, dw_kernel, 1, 6, 3, high // 2 + 7)
    size = (high // 2, wide // 2, high // 2 * (tiles // TILE_COLS))
    g, rest, part = mix1(
        everyones(part), se_reduce, se_expand, mix_weight, g, rest, dw_kernel, cells // 4, size, 6
    )
    query = mix2(
        everyones(part), se_reduce, se_expand, mix_weight, g, rest, cells // 16, high // 8, wide // 8, group
    )
    groups = [list(range(group * x, group * x + group)) for x in range(tiles // group)]
    slab = lax.all_to_all(query, "tile", 0, 0, tiled=True, axis_index_groups=groups)
    return slab.reshape(-1, dim), (kt0, kt1), (vt0, vt1)


def body(
    features,
    dw_kernel,
    se_reduce,
    se_expand,
    mix_weight,
    norm_gain,
    kv_weight,
    kv_bias,
    proj_weight,
    proj_bias,
):
    tile_map = features[0]
    se_reduce = jnp.swapaxes(se_reduce, 1, 2)

    def keys_of(window, held):
        return keys_values(after_these(tile_map, held), norm_gain, kv_weight, kv_bias, window)

    slab, keys, values = query_slab(tile_map, dw_kernel, se_reduce, se_expand, mix_weight, keys_of)
    tiles = lax.axis_size("tile")
    group = 2 * TILE_COLS
    steps = tuple(range(1, tiles // group))
    others = [lax.ppermute(slab, "tile", [(t, t ^ group * step) for t in range(tiles)]) for step in steps]
    rest = (keys, values, tile_map, proj_weight, proj_bias)
    started = attention((0,), [slab], *rest)
    return attention(steps, others, *rest, started)[None]


def solution(mesh):
    in_specs = (P(("scene", "tile"), None, None, None), P(), P(), P(), P(), P(), P(), P(), P(), P())
    out_specs = P(("scene", "tile"), None, None, None)
    return jax.shard_map(body, mesh=mesh, in_specs=in_specs, out_specs=out_specs, check_vma=False)
```

```python
import functools

import jax
import jax.numpy as jnp
from jax import lax
from jax.experimental import pallas as pl
from jax.experimental.pallas import tpu as pltpu
from jax.sharding import PartitionSpec as P

HEADS = 24
TILE_COLS = 4
EPSILON = 1e-05
BF = jnp.bfloat16
F32 = jnp.float32
VM = pl.BlockSpec(memory_space=pltpu.VMEM)
LOG2E = 1.4426950408889634
QB = 256
KC = 512
UNROLL = 12


def kv_kernel(x_ref, gain_ref, w_ref, b_ref, kt_ref, vt_ref):
    dim = x_ref.shape[-1]
    tokens = x_ref.shape[0] * x_ref.shape[1]
    x = x_ref[...].reshape(tokens, dim).astype(F32)
    centre = jnp.mean(x, axis=1, keepdims=True)
    moved = x - centre
    spread = jnp.mean(jnp.square(moved), axis=1, keepdims=True)
    normed = (moved * lax.rsqrt(spread + EPSILON) * gain_ref[...].reshape(1, dim)).astype(BF)
    keys = (jnp.dot(normed, w_ref[:, :dim], preferred_element_type=F32) + b_ref[:dim].reshape(1, dim)).astype(BF)
    for group in range(dim // 128):
        kt_ref[group] = keys[:, 128 * group : 128 * group + 128]
    vals = jnp.dot(normed, w_ref[:, dim:], preferred_element_type=F32) + b_ref[dim:].reshape(1, dim)
    vt_ref[...] = vals.T.astype(BF)


def keys_values(tile_map, gain, weight, bias, window):
    win, _, dim = tile_map.shape
    step = 8
    tokens = step * win
    return pl.pallas_call(
        kv_kernel,
        grid=(win // step,),
        in_specs=[
            pl.BlockSpec((step, win, dim), lambda i: (i, window, 0)),
            pl.BlockSpec((dim,), lambda i: (0,)),
            pl.BlockSpec((dim, 2 * dim), lambda i: (0, 0)),
            pl.BlockSpec((2 * dim,), lambda i: (0,)),
        ],
        out_specs=[
            pl.BlockSpec((dim // 128, tokens, 128), lambda i: (0, i, 0)),
            pl.BlockSpec((dim, tokens), lambda i: (0, i)),
        ],
        out_shape=[
            jax.ShapeDtypeStruct((dim // 128, win * win, 128), BF),
            jax.ShapeDtypeStruct((dim, win * win), BF),
        ],
        compiler_params=pltpu.CompilerParams(vmem_limit_bytes=24 * 2**20),
        cost_estimate=pl.CostEstimate(
            flops=8 * win * win * dim * dim, bytes_accessed=8 * 2**20, transcendentals=0
        ),
        name="keys_values",
    )(tile_map, gain, weight, bias)


def attention_kernel(steps, *refs):
    slabs = len(steps)
    q_refs = refs[:slabs]
    kt_refs, vt_refs = refs[slabs : slabs + 2], refs[slabs + 2 : slabs + 4]
    x_ref, wp_ref, bp_ref = refs[slabs + 4 : slabs + 7]
    out_ref, qa, sb, mb, ot, stage, sems = refs[-7:]
    dim = x_ref.shape[2]
    length = kt_refs[0].shape[1]
    units = HEADS * slabs
    scale = (dim // HEADS) ** (-0.5) * LOG2E
    lane = lax.broadcasted_iota(jnp.int32, (1, 128), 1)
    for slab in range(slabs):
        for group in range(dim // 128):
            q = q_refs[slab][:, 128 * group : 128 * group + 128]
            for part in range(4):
                qa[slab, 4 * group + part] = jnp.where(lane // 32 == part, q, jnp.zeros_like(q))
    ones = jnp.ones((16, KC), BF)

    def score(unit, slot, w, start):
        head = unit // slabs
        s = lax.dot_general(
            kt_refs[w][head // 4, pl.ds(start, KC), :],
            qa[unit % slabs, head],
            (((1,), (1,)), ((), ())),
            preferred_element_type=F32,
        )
        sb[slot, w, pl.ds(start, KC), :] = s
        return jnp.max(s.reshape(KC // 8, 8, QB), axis=0)

    def step(unit, slot, following):
        if unit is not None:
            head = unit // slabs
            rows = pl.ds(pl.multiple_of(head * 32, 32), 32)
        for w in range(2):
            top = total = None
            if unit is not None:
                peak = jnp.max(mb[slot, w], axis=0, keepdims=True)
            for start in range(0, length, KC):
                high = score(following, 1 - slot, w, start)
                top = high if top is None else jnp.maximum(top, high)
                if unit is not None:
                    p = jnp.exp2((sb[slot, w, pl.ds(start, KC), :] - peak) * scale).astype(BF)
                    v = jnp.concatenate([vt_refs[w][rows, pl.ds(start, KC)], ones], axis=0)
                    o = jnp.dot(v, p, preferred_element_type=F32)
                    total = o if total is None else total + o
            mb[1 - slot, w] = top
            if unit is not None:
                ot[unit % slabs, w, rows, :] = (total[:32] / total[32:33]).astype(BF)

    step(None, 1, 0)

    def body(turn, _):
        for j in range(UNROLL):
            unit = UNROLL * turn + j
            step(unit, j % 2, jnp.minimum(unit + 1, units - 1))
        return 0

    lax.fori_loop(0, units // UNROLL, body, 0)

    win = x_ref.shape[1] // 2
    lines = QB // win
    copies = []
    for slab in range(slabs):
        own = lax.axis_index("tile") // (2 * TILE_COLS)
        place = pl.ds(pl.multiple_of((own ^ steps[slab]) * lines, lines), lines)
        for w in range(2):
            cols = slice(w * win, w * win + win)
            y = lax.dot_general(
                ot[slab, w], wp_ref[...], (((0,), (0,)), ((), ())), preferred_element_type=F32
            )
            y = y.reshape(2, 4, lines // 2, win // 4, dim).transpose(0, 2, 1, 3, 4).reshape(lines, win, dim)
            y = x_ref[place, cols, :].astype(F32) + y + bp_ref[...].reshape(1, dim)
            stage[slab, :, cols, :] = y.astype(BF)
        copy = pltpu.make_async_copy(stage.at[slab], out_ref.at[place], sems.at[slab])
        copy.start()
        copies.append(copy)
    for copy in copies:
        copy.wait()


def attention(steps, queries, keys, values, tile_map, wp, bp, started=None):
    rows, cols, dim = tile_map.shape
    slabs = len(queries)
    lines = QB * 2 // cols
    more = [] if started is None else [started]
    anywhere = pl.BlockSpec(memory_space=pl.ANY)
    return pl.pallas_call(
        functools.partial(attention_kernel, steps),
        in_specs=[VM] * (slabs + 7) + [anywhere] * len(more),
        out_specs=anywhere,
        out_shape=jax.ShapeDtypeStruct(tile_map.shape, BF),
        input_output_aliases={slabs + 7: 0} if more else {},
        scratch_shapes=[
            pltpu.VMEM((slabs, HEADS, QB, 128), BF),
            pltpu.VMEM((2, 2, rows * cols // 2, QB), F32),
            pltpu.VMEM((2, 2, 8, QB), F32),
            pltpu.VMEM((slabs, 2, dim, QB), BF),
            pltpu.VMEM((slabs, lines, cols, dim), BF),
            pltpu.SemaphoreType.DMA((slabs,)),
        ],
        compiler_params=pltpu.CompilerParams(vmem_limit_bytes=40 * 2**20),
        cost_estimate=pl.CostEstimate(
            flops=8 * slabs * QB * 1024 * dim * 8,
            bytes_accessed=12 * 2**20,
            transcendentals=48 * slabs * QB * 1024,
        ),
        name="attention",
    )(*queries, *keys, *values, tile_map, wp, bp, *more)


def whole(array):
    return pl.BlockSpec(array.shape, lambda *i: (0,) * len(array.shape), pipeline_mode=pl.Buffered(1))


def wholes(*arrays):
    return [whole(array) for array in arrays]


def at_level(array, level):
    shape = (None,) + array.shape[1:]
    return pl.BlockSpec(shape, lambda *i: (level,) + (0,) * (len(shape) - 1), pipeline_mode=pl.Buffered(1))


def position():
    index = lax.axis_index("tile")
    return index // TILE_COLS, index % TILE_COLS


def params(mib):
    return pltpu.CompilerParams(vmem_limit_bytes=mib * 2**20)


def cost(flops, size):
    return pl.CostEstimate(flops=flops, bytes_accessed=size, transcendentals=0)


def round_up(count, unit):
    return -(-count // unit) * unit


def odd_column():
    return position()[1] % 2 == 1


def give_sides(keep_r, keep_l, to_partner, to_cross):
    odd = odd_column()
    to_partner[...] = jnp.where(odd, keep_l[...], keep_r[...]).astype(BF)
    to_cross[...] = jnp.where(odd, keep_r[...], keep_l[...]).astype(BF)


def take_sides(partner_ref, cross_ref):
    odd = odd_column()
    partner, cross = partner_ref[...].astype(F32), cross_ref[...].astype(F32)
    return jnp.where(odd, partner, cross), jnp.where(odd, cross, partner)


def side_pieces_kernel(before, after, left_ref, right_ref, to_partner, to_cross, keep_r, keep_l):
    high = left_ref.shape[0]
    span = right_ref.shape[1]
    keep_l[...] = jnp.zeros_like(keep_l)
    for r in range(high):
        keep_r[r * before : r * before + before, :] = right_ref[r].astype(F32)[span - before :]
        keep_l[r * before : r * before + after, :] = left_ref[r].astype(F32)[:after]
    give_sides(keep_r, keep_l, to_partner, to_cross)


def side_pieces(tile, before, after):
    high, wide, dim = tile.shape
    return pl.pallas_call(
        functools.partial(side_pieces_kernel, before, after),
        grid=(1,),
        in_specs=[
            pl.BlockSpec((high, 16, dim), lambda i: (0, 0, 0)),
            pl.BlockSpec((high, 16, dim), lambda i: (0, wide // 16 - 1, 0)),
        ],
        out_shape=[jax.ShapeDtypeStruct((high * before, dim), BF)] * 2,
        scratch_shapes=[pltpu.VMEM((high * before, dim), F32)] * 2,
        compiler_params=params(12),
        cost_estimate=cost(0, 2 * 2**20),
        name="side_pieces",
    )(tile, tile)


def line_pieces_kernel(before, after, high, top_ref, low_ref, left_ref, right_ref, to_low, to_up, keep_d, keep_u, side_l, side_r):
    wide = top_ref.shape[1]
    full = before + wide + after
    side_l[...], side_r[...] = take_sides(left_ref, right_ref)
    keep_d[...] = jnp.zeros_like(keep_d)
    keep_u[...] = jnp.zeros_like(keep_u)

    def fill(keep, line, r, values):
        base = line * full
        keep[base : base + before, :] = side_l[r * before : r * before + before, :]
        keep[base + before : base + before + wide, :] = values
        keep[base + before + wide : base + full, :] = side_r[r * before : r * before + after, :]

    for line in range(before):
        fill(keep_d, line, high - before + line, low_ref[line].astype(F32))
    for line in range(after):
        fill(keep_u, line, line, top_ref[line].astype(F32))
    to_low[...] = keep_d[...].astype(BF)
    to_up[...] = keep_u[...].astype(BF)


def line_pieces(tile, left, right, before, after):
    high, wide, dim = tile.shape
    full = before + wide + after
    down = round_up(before * full, 16)
    up = round_up(after * full, 16)
    low_size = before if high % before == 0 else 8
    assert high % low_size == 0
    return pl.pallas_call(
        functools.partial(line_low_kernel, low_size, before, after, high),
        grid=(1,),
        in_specs=[
            pl.BlockSpec((after if high % after == 0 else 8, wide, dim), lambda i: (0, 0, 0)),
            pl.BlockSpec((low_size, wide, dim), lambda i: (high // low_size - 1, 0, 0)),
            whole(left),
            whole(right),
        ],
        out_shape=[jax.ShapeDtypeStruct((down, dim), BF), jax.ShapeDtypeStruct((up, dim), BF)],
        scratch_shapes=[
            pltpu.VMEM((down, dim), F32),
            pltpu.VMEM((up, dim), F32),
            pltpu.VMEM(left.shape, F32),
            pltpu.VMEM(right.shape, F32),
        ],
        compiler_params=params(12),
        cost_estimate=cost(0, 2**20),
        name="line_pieces",
    )(tile, tile, left, right)


def line_low_kernel(low_size, before, after, high, top_ref, low_ref, *rest):
    line_pieces_kernel(before, after, high, top_ref, low_ref.at[pl.ds(low_size - before, before)], *rest)


def moved_by(value, rows, cols):
    count = lax.axis_size("tile")
    pairs = []
    for t in range(count):
        r, c = t // TILE_COLS + rows, t % TILE_COLS + cols
        if 0 <= r < count // TILE_COLS and 0 <= c < TILE_COLS:
            pairs.append((t, r * TILE_COLS + c))
    return lax.ppermute(value, "tile", pairs)


def after_these(value, *others):
    return lax.optimization_barrier((value,) + others)[0]


def exchange_rims(tile, pieces, before, after, early, beside):
    tiles = range(lax.axis_size("tile"))
    left = lax.ppermute(pieces[0], "tile", [(t, t ^ 1) for t in tiles])
    between = [(t, t + 1) for t in tiles if t % 2 == 1 and (t + 1) % TILE_COLS]
    right = lax.ppermute(pieces[1], "tile", between + [(b, a) for a, b in between])
    left, right, *first = lax.optimization_barrier((left, right, *early(pieces[0])))
    down, up = line_pieces(tile, left, right, before, after)
    above, below = moved_by(down, 1, 0), moved_by(up, -1, 0)
    result = beside((left, right), down)
    above, below, *result = lax.optimization_barrier((above, below, *result))
    return (left, right, above, below), first, result


def erf_gelu(y):
    return 0.5 * y * (1.0 + lax.erf(y * 0.7071067811865476))


def conv_gelu(padded, kernel_ref, g_ref, own_rows, own_cols, part_ref):
    rows, cols, dim = g_ref.shape
    column = lax.broadcasted_iota(jnp.int32, (cols, 128), 0)
    mine = (column >= own_cols[0]) & (column < own_cols[1])
    for group in range(dim // 128):
        lanes = slice(128 * group, 128 * group + 128)
        taps = [[kernel_ref[a, b : b + 1, lanes].astype(F32) for b in range(3)] for a in range(3)]

        def line(r, total):
            y = None
            for a in range(3):
                for b in range(3):
                    term = padded[r + a, b : b + cols, lanes] * taps[a][b]
                    y = term if y is None else y + term
            g = erf_gelu(y)
            g_ref[r, :, lanes] = g
            counted = jnp.sum(jnp.where(mine, g, 0.0).reshape(cols // 8, 8, 128), axis=0)
            return total + jnp.where((r >= own_rows[0]) & (r < own_rows[1]), counted, 0.0)

        total = lax.fori_loop(0, rows, line, jnp.zeros((8, 128), F32), unroll=True)
        total = jnp.sum(total, axis=0, keepdims=True)
        part_ref[:, group, :] += jnp.broadcast_to(total, (part_ref.shape[0], 128))


def copy_centre(padded, rest_ref):
    rows, cols, _ = rest_ref.shape

    def line(r, _):
        rest_ref[r] = padded[r + 1, 1 : 1 + cols, :].astype(BF)
        return 0

    lax.fori_loop(0, rows, line, 0)


def thirds(row):
    high = row.astype(BF).astype(F32)
    mid = (row - high).astype(BF).astype(F32)
    low = row - high - mid
    index = lax.broadcasted_iota(jnp.int32, (16, row.shape[1]), 0)
    block = jnp.where(index == 0, high, jnp.where(index == 1, mid, jnp.where(index == 2, low, 0.0)))
    return block.astype(BF)


def gate_row(sums_ref, cells, reduce_ref, expand_ref):
    total = jnp.sum(sums_ref[...], axis=0)
    groups = reduce_ref.shape[1] // 128
    mean = jnp.concatenate([total[group : group + 1] for group in range(groups)], axis=1) / cells
    inner = lax.dot_general(
        thirds(mean), reduce_ref[...], (((1,), (1,)), ((), ())), preferred_element_type=F32
    )
    inner = jnp.sum(inner, axis=0, keepdims=True)
    inner = erf_gelu(inner)
    outer = jnp.sum(jnp.dot(thirds(inner), expand_ref[...], preferred_element_type=F32), axis=0, keepdims=True)
    return 1.0 / (1.0 + jnp.exp(-outer))


def mix_lines(g_ref, gate, mix_ref, rest_ref, z_ref, lines, bounds):
    rows, cols, dim = g_ref.shape
    row_low, row_high, col_low, col_high = bounds
    column = lax.broadcasted_iota(jnp.int32, (cols, 1), 0)
    inside = (column >= col_low) & (column < col_high)
    u = (g_ref[...] * gate).astype(BF).reshape(rows * cols, dim)
    product = jnp.dot(u, mix_ref[...], preferred_element_type=F32).reshape(rows, cols, dim)
    for k in range(rows):
        z = (rest_ref[k].astype(F32) + product[k]).astype(BF).astype(F32)
        keep = inside & (lines[k] >= row_low) & (lines[k] < row_high)
        z_ref[lines[k]] = jnp.where(keep, z, -jnp.inf)


def pooled_line(z_ref, line_ref, i, count):
    most = jnp.maximum(jnp.maximum(z_ref[2 * i], z_ref[2 * i + 1]), z_ref[2 * i + 2])
    groups = []
    for group in range(line_ref.shape[0]):
        line_ref[group] = most[:, 128 * group : 128 * group + 128]
        parts = [line_ref[group, pl.ds(s, count, stride=2), :] for s in range(3)]
        groups.append(jnp.maximum(jnp.maximum(parts[0], parts[1]), parts[2]))
    return jnp.concatenate(groups, axis=1)


def fill_sides(x_ref, left_ref, right_ref, before, after, padded, stage):
    high, wide, _ = x_ref.shape
    full = before + wide + after

    def line(r, _):
        padded[r, before : before + wide, :] = x_ref[r].astype(F32)
        return 0

    lax.fori_loop(0, high, line, 0)
    left, right = take_sides(left_ref, right_ref)
    stage[...] = left
    for r in range(high):
        padded[r, 0:before, :] = stage[r * before : r * before + before, :]
    stage[...] = right
    for r in range(high):
        padded[r, before + wide : full, :] = stage[r * before : r * before + after, :]


def inner_kernel(before, after, x_ref, l_ref, r_ref, kernel_ref, g_ref, rest_ref, part_ref, padded, stage):
    _, wide, _ = x_ref.shape
    step = g_ref.shape[0]
    turn = pl.program_id(0)

    @pl.when(turn == 0)
    def _():
        fill_sides(x_ref, l_ref, r_ref, before, after, padded, stage)
        part_ref[...] = jnp.zeros_like(part_ref)

    block = padded.at[pl.ds(turn * step, step + 2)]
    copy_centre(block, rest_ref)
    conv_gelu(block, kernel_ref, g_ref, (0, step), (before - 1, before - 1 + wide), part_ref)


def activate_inner(tile, left, right, kernels, level, before, after, step):
    high, wide, dim = tile.shape
    rows, cols = high - 2, round_up(wide + before + after - 2, 8)
    copies = lax.axis_size("tile")
    block = pl.BlockSpec((step, cols, dim), lambda i: (i, 0, 0))
    return pl.pallas_call(
        functools.partial(inner_kernel, before, after),
        grid=(rows // step,),
        in_specs=wholes(tile, left, right) + [at_level(kernels, level)],
        out_specs=[block, block, pl.BlockSpec((copies, 8, 128), lambda i: (0, 0, 0))],
        out_shape=[
            jax.ShapeDtypeStruct((rows, cols, dim), F32),
            jax.ShapeDtypeStruct((rows, cols, dim), BF),
            jax.ShapeDtypeStruct((copies, 8, 128), F32),
        ],
        scratch_shapes=[
            pltpu.VMEM((high, round_up(cols + 2, 8), dim), F32),
            pltpu.VMEM((max(left.shape[0], right.shape[0]), dim), F32),
        ],
        compiler_params=params(28 if level == 0 else 20),
        cost_estimate=cost(400 * rows * cols * dim, 6 * rows * cols * dim),
        name="activate_inner",
    )(tile, left, right, kernels)


def edge_kernel(high, before, after, top_ref, low_ref, l_ref, r_ref, a_ref, b_ref, kernel_ref, sum_ref, g_ref, rest_ref, part_ref, upper, lower, side_l, side_r, stage):
    wide = top_ref.shape[1]
    full = before + wide + after
    own = (before - 1, before - 1 + wide)
    side_l[...], side_r[...] = take_sides(l_ref, r_ref)

    def fill(padded, at, r, values):
        padded[at, 0:before, :] = side_l[r * before : r * before + before, :]
        padded[at, before : before + wide, :] = values.astype(F32)
        padded[at, before + wide : full, :] = side_r[r * before : r * before + after, :]

    for k in range(2):
        fill(upper, before + k, k, top_ref[k])
        fill(lower, k, high - 2 + k, low_ref[k])
    stage[: a_ref.shape[0], :] = a_ref[...].astype(F32)
    for k in range(before):
        upper[k, 0:full, :] = stage[k * full : k * full + full, :]
    stage[: b_ref.shape[0], :] = b_ref[...].astype(F32)
    for k in range(after):
        lower[2 + k, 0:full, :] = stage[k * full : k * full + full, :]
    part_ref[...] = sum_ref[...]
    up, low = pl.ds(0, before), pl.ds(before, after)
    copy_centre(upper, rest_ref.at[up])
    copy_centre(lower, rest_ref.at[low])
    conv_gelu(upper, kernel_ref, g_ref.at[up], (before - 1, before), own, part_ref)
    conv_gelu(lower, kernel_ref, g_ref.at[low], (0, 1), own, part_ref)


def activate_edge(tile, rims, kernels, part, level, before, after):
    high, wide, dim = tile.shape
    cols = round_up(wide + before + after - 2, 8)
    padded = round_up(cols + 2, 8)
    stage = max(r.shape[0] for r in rims)
    left, right, above, below = rims
    lines = before + after
    outs = [
        jax.ShapeDtypeStruct((lines, cols, dim), F32),
        jax.ShapeDtypeStruct((lines, cols, dim), BF),
        jax.ShapeDtypeStruct(part.shape, F32),
    ]
    return pl.pallas_call(
        functools.partial(edge_kernel, high, before, after),
        grid=(1,),
        in_specs=[
            pl.BlockSpec((2, wide, dim), lambda i: (0, 0, 0)),
            pl.BlockSpec((2, wide, dim), lambda i: (high // 2 - 1, 0, 0)),
        ]
        + wholes(*rims)
        + [at_level(kernels, level), whole(part)],
        out_specs=wholes(*outs),
        out_shape=outs,
        scratch_shapes=[
            pltpu.VMEM((before + 2, padded, dim), F32),
            pltpu.VMEM((after + 2, padded, dim), F32),
            pltpu.VMEM(left.shape, F32),
            pltpu.VMEM(right.shape, F32),
            pltpu.VMEM((stage, dim), F32),
        ],
        compiler_params=params(16),
        cost_estimate=cost(400 * lines * cols * dim, 6 * lines * cols * dim),
        name="activate_edge",
    )(tile, tile, *rims, kernels, part)


def mix0_kernel(cells, before, after, sums, red, exp, mix, g_ref, rest, g_edge, rest_edge, x_out, to_partner, to_cross, gates, z, line, keep_r, keep_l):
    step, cols, dim = g_ref.shape
    high, wide, _ = x_out.shape
    turn = pl.program_id(0)

    pos = position()
    bounds = (jnp.where(pos[0] == 0, 1, 0), z.shape[0], jnp.where(pos[1] == 0, 1, 0), cols)

    @pl.when(turn == 0)
    def _():
        gates[...] = jnp.broadcast_to(gate_row(sums, cells, red, exp), gates.shape)
        keep_l[...] = jnp.zeros_like(keep_l)
        mix_lines(g_edge, gates[:1, :], mix, rest_edge, z, (0, 1, z.shape[0] - 1), bounds)

    mix_lines(g_ref, gates[:1, :], mix, rest, z, [2 + turn * step + k for k in range(step)], bounds)

    @pl.when(turn == pl.num_programs(0) - 1)
    def _():
        for i in range(high):
            out = pooled_line(z, line, i, wide)
            x_out[i] = out.astype(BF)
            keep_r[i * before : i * before + before, :] = out[wide - before :]
            keep_l[i * before : i * before + after, :] = out[:after]
        give_sides(keep_r, keep_l, to_partner, to_cross)


def level_specs(sums, red, exp, mix, level):
    return [whole(sums), at_level(red, level), at_level(exp, level), at_level(mix, level)]


def mix0(sums, red, exp, mix, g, rest, edges, cells, high, wide, before, after, step):
    rows, cols, dim = g.shape
    block = pl.BlockSpec((step, cols, dim), lambda i: (i, 0, 0))
    outs = [
        jax.ShapeDtypeStruct((high, wide, dim), BF),
        jax.ShapeDtypeStruct((high * before, dim), BF),
        jax.ShapeDtypeStruct((high * before, dim), BF),
    ]
    return pl.pallas_call(
        functools.partial(mix0_kernel, cells, before, after),
        grid=(rows // step,),
        in_specs=level_specs(sums, red, exp, mix, 0) + [block, block] + wholes(*edges),
        out_specs=wholes(*outs),
        out_shape=outs,
        scratch_shapes=[
            pltpu.VMEM((8, dim), F32),
            pltpu.VMEM((rows + 3, cols, dim), F32),
            pltpu.VMEM((dim // 128, cols, 128), F32),
            pltpu.VMEM((high * before, dim), F32),
            pltpu.VMEM((high * before, dim), F32),
        ],
        compiler_params=params(32),
        cost_estimate=cost(2 * rows * cols * dim * dim, 6 * rows * cols * dim),
        name="mix0",
    )(sums, red, exp, mix, g, rest, *edges)


def mix1_kernel(cells, size, before, sums, red, exp, mix, g_ref, rest, g_edge, rest_edge, kernel, g_out, rest_out, part, z, line, padded):
    rows, cols, dim = g_ref.shape
    side_r, side_c, map_side = size
    gate = gate_row(sums, cells, red, exp)
    shift = before - 1
    pos = position()
    row_low = shift - pos[0] * side_r
    col_low = shift - pos[1] * side_c
    bounds = (row_low, row_low + map_side, col_low, col_low + map_side)
    inner = range(before, before + rows)
    mix_lines(g_ref, gate, mix, rest, z, inner, bounds)
    mix_lines(g_edge, gate, mix, rest_edge, z, [k for k in range(z.shape[0]) if k not in inner], bounds)
    count_r, count_c = padded.shape[0], (cols - 1) // 2
    row_two = 2 - pos[0] * (side_r // 2)
    col_two = 2 - pos[1] * (side_c // 2)
    column = lax.broadcasted_iota(jnp.int32, (count_c, 1), 0)
    inside = (column >= col_two) & (column < col_two + map_side // 2)
    for i in range(count_r):
        out = pooled_line(z, line, i, count_c)
        keep = inside & (i >= row_two) & (i < row_two + map_side // 2)
        padded[i, 0:count_c, :] = jnp.where(keep, out, 0.0)
    copy_centre(padded, rest_out)
    part[...] = jnp.zeros_like(part)
    conv_gelu(padded, kernel, g_out, (1, 1 + side_r // 2), (1, 1 + side_c // 2), part)


def mix1(sums, red, exp, mix, g, rest, edges, kernels, cells, size, before):
    rows, cols, dim = g.shape
    rows += edges[0].shape[0]
    out_rows, out_cols = (rows - 1) // 2 - 2, round_up((cols - 1) // 2 - 2, 8)
    outs = [
        jax.ShapeDtypeStruct((out_rows, out_cols, dim), F32),
        jax.ShapeDtypeStruct((out_rows, out_cols, dim), BF),
        jax.ShapeDtypeStruct(sums.shape, F32),
    ]
    return pl.pallas_call(
        functools.partial(mix1_kernel, cells, size, before),
        grid=(1,),
        in_specs=level_specs(sums, red, exp, mix, 1) + wholes(g, rest, *edges) + [at_level(kernels, 2)],
        out_specs=wholes(*outs),
        out_shape=outs,
        scratch_shapes=[
            pltpu.VMEM((rows, cols, dim), F32),
            pltpu.VMEM((dim // 128, cols, 128), F32),
            pltpu.VMEM((out_rows + 2, round_up(out_cols + 2, 8), dim), F32),
        ],
        compiler_params=params(18),
        cost_estimate=cost(2 * rows * cols * dim * dim, 6 * rows * cols * dim),
        name="mix1",
    )(sums, red, exp, mix, g, rest, *edges, kernels)


def mix2_kernel(cells, high, wide, sums, red, exp, mix, g_ref, rest, x_out, z, line, keep):
    rows, cols, dim = g_ref.shape
    gate = gate_row(sums, cells, red, exp)
    pos = position()
    bounds = (jnp.where(pos[0] == 0, 1, 0), rows, jnp.where(pos[1] == 0, 1, 0), cols)
    mix_lines(g_ref, gate, mix, rest, z, range(rows), bounds)
    for i in range(high):
        keep[i * wide : i * wide + wide, :] = pooled_line(z, line, i, wide)
    x_out[...] = jnp.broadcast_to(keep[...].astype(BF), x_out.shape)


def mix2(sums, red, exp, mix, g, rest, cells, high, wide, copies):
    rows, cols, dim = g.shape
    out = jax.ShapeDtypeStruct((copies, high * wide, dim), BF)
    return pl.pallas_call(
        functools.partial(mix2_kernel, cells, high, wide),
        grid=(1,),
        in_specs=level_specs(sums, red, exp, mix, 2) + wholes(g, rest),
        out_specs=whole(out),
        out_shape=out,
        scratch_shapes=[
            pltpu.VMEM((rows, cols, dim), F32),
            pltpu.VMEM((dim // 128, cols, 128), F32),
            pltpu.VMEM((high * wide, dim), F32),
        ],
        compiler_params=params(10),
        cost_estimate=cost(2 * rows * cols * dim * dim, 6 * rows * cols * dim),
        name="mix2",
    )(sums, red, exp, mix, g, rest)


def everyones(copies):
    return lax.all_to_all(copies, "tile", 0, 0, tiled=True)


def query_slab(tile_map, dw_kernel, se_reduce, se_expand, mix_weight, keys_of):
    high, wide, dim = tile_map.shape
    tiles = lax.axis_size("tile")
    cells = high * wide * tiles
    group = 2 * TILE_COLS
    def inner(tile, level, sides, held, *halos):
        return activate_inner(after_these(tile, held), *sides, dw_kernel, level, *halos)

    rims, (kt0, vt0), (g, rest, part) = exchange_rims(
        tile_map,
        side_pieces(tile_map, 2, 1),
        2,
        1,
        lambda held: keys_of(0, held),
        lambda sides, held: inner(tile_map, 0, sides, held, 2, 1, 10),
    )
    *edges, part = activate_edge(tile_map, rims, dw_kernel, part, 0, 2, 1)
    coarse, *sides = mix0(
        everyones(part), se_reduce, se_expand, mix_weight, g, rest, edges, cells, high // 2, wide // 2, 6, 3, 10
    )

    rims, (kt1, vt1), (g, rest, part) = exchange_rims(
        coarse,
        sides,
        6,
        3,
        lambda held: keys_of(1, held),
        lambda sides, held: inner(coarse, 1, sides, held, 6, 3, high // 2 - 2),
    )
    *edges, part = activate_edge(coarse, rims, dw_kernel, part, 1, 6, 3)
    size = (high // 2, wide // 2, high // 2 * (tiles // TILE_COLS))
    g, rest, part = mix1(
        everyones(part), se_reduce, se_expand, mix_weight, g, rest, edges, dw_kernel, cells // 4, size, 6
    )
    query = mix2(
        everyones(part), se_reduce, se_expand, mix_weight, g, rest, cells // 16, high // 8, wide // 8, group
    )
    groups = [list(range(group * x, group * x + group)) for x in range(tiles // group)]
    slab = lax.all_to_all(query, "tile", 0, 0, tiled=True, axis_index_groups=groups)
    return slab.reshape(-1, dim), (kt0, kt1), (vt0, vt1)


def body(
    features,
    dw_kernel,
    se_reduce,
    se_expand,
    mix_weight,
    norm_gain,
    kv_weight,
    kv_bias,
    proj_weight,
    proj_bias,
):
    tile_map = features[0]
    se_reduce = jnp.swapaxes(se_reduce, 1, 2)

    def keys_of(window, held):
        return keys_values(after_these(tile_map, held), norm_gain, kv_weight, kv_bias, window)

    slab, keys, values = query_slab(tile_map, dw_kernel, se_reduce, se_expand, mix_weight, keys_of)
    tiles = lax.axis_size("tile")
    group = 2 * TILE_COLS
    def from_x(value, step):
        return lax.ppermute(value, "tile", [(t, t ^ group * step) for t in range(tiles)])

    near = [from_x(slab, 1), from_x(slab, 3)]
    rest = (keys, values, tile_map, proj_weight, proj_bias)
    out = attention((0,), [slab], *rest)
    far, out = lax.optimization_barrier((slab, out))
    far = from_x(far, 2)
    out = attention((1, 3), near, *rest, out)
    return attention((2,), [far], *rest, out)[None]


def solution(mesh):
    in_specs = (P(("scene", "tile"), None, None, None), P(), P(), P(), P(), P(), P(), P(), P(), P())
    out_specs = P(("scene", "tile"), None, None, None)
    return jax.shard_map(body, mesh=mesh, in_specs=in_specs, out_specs=out_specs, check_vma=False)
```

```python
import functools

import jax
import jax.numpy as jnp
from jax import lax
from jax.experimental import pallas as pl
from jax.experimental.pallas import tpu as pltpu
from jax.sharding import PartitionSpec as P

HEADS = 24
TILE_COLS = 4
EPSILON = 1e-05
BF = jnp.bfloat16
F32 = jnp.float32
VM = pl.BlockSpec(memory_space=pltpu.VMEM)
LOG2E = 1.4426950408889634
QB = 256
KC = 512
UNROLL = {1: 4, 2: 8, 3: 8}


def kv_kernel(x_ref, gain_ref, w_ref, b_ref, kt_ref, vt_ref):
    dim = x_ref.shape[-1]
    tokens = x_ref.shape[0] * x_ref.shape[1]
    x = x_ref[...].reshape(tokens, dim).astype(F32)
    centre = jnp.mean(x, axis=1, keepdims=True)
    moved = x - centre
    spread = jnp.mean(jnp.square(moved), axis=1, keepdims=True)
    normed = (moved * lax.rsqrt(spread + EPSILON) * gain_ref[...].reshape(1, dim)).astype(BF)
    keys = (jnp.dot(normed, w_ref[:, :dim], preferred_element_type=F32) + b_ref[:dim].reshape(1, dim)).astype(BF)
    for group in range(dim // 128):
        kt_ref[group] = keys[:, 128 * group : 128 * group + 128]
    vals = jnp.dot(normed, w_ref[:, dim:], preferred_element_type=F32) + b_ref[dim:].reshape(1, dim)
    vt_ref[...] = vals.T.astype(BF)


def keys_values(tile_map, gain, weight, bias, window):
    win, _, dim = tile_map.shape
    step = 8
    tokens = step * win
    return pl.pallas_call(
        kv_kernel,
        grid=(win // step,),
        in_specs=[
            pl.BlockSpec((step, win, dim), lambda i: (i, window, 0)),
            pl.BlockSpec((dim,), lambda i: (0,)),
            pl.BlockSpec((dim, 2 * dim), lambda i: (0, 0)),
            pl.BlockSpec((2 * dim,), lambda i: (0,)),
        ],
        out_specs=[
            pl.BlockSpec((dim // 128, tokens, 128), lambda i: (0, i, 0)),
            pl.BlockSpec((dim, tokens), lambda i: (0, i)),
        ],
        out_shape=[
            jax.ShapeDtypeStruct((dim // 128, win * win, 128), BF),
            jax.ShapeDtypeStruct((dim, win * win), BF),
        ],
        compiler_params=pltpu.CompilerParams(vmem_limit_bytes=24 * 2**20),
        cost_estimate=pl.CostEstimate(
            flops=8 * win * win * dim * dim, bytes_accessed=8 * 2**20, transcendentals=0
        ),
        name="keys_values",
    )(tile_map, gain, weight, bias)


def attention_kernel(steps, *refs):
    slabs = len(steps)
    q_refs = refs[:slabs]
    kt_refs, vt_refs = refs[slabs : slabs + 2], refs[slabs + 2 : slabs + 4]
    x_ref, wp_ref, bp_ref = refs[slabs + 4 : slabs + 7]
    out_ref, qa, sb, mb, ot, stage, sems = refs[-7:]
    dim = x_ref.shape[2]
    length = kt_refs[0].shape[1]
    units = HEADS * slabs
    unroll = UNROLL[slabs]
    scale = (dim // HEADS) ** (-0.5) * LOG2E
    lane = lax.broadcasted_iota(jnp.int32, (1, 128), 1)
    for slab in range(slabs):
        for group in range(dim // 128):
            q = q_refs[slab][:, 128 * group : 128 * group + 128]
            for part in range(4):
                qa[slab, 4 * group + part] = jnp.where(lane // 32 == part, q, jnp.zeros_like(q))
    ones = jnp.ones((16, KC), BF)

    def score(unit, slot, w, start):
        head = unit // slabs
        s = lax.dot_general(
            kt_refs[w][head // 4, pl.ds(start, KC), :],
            qa[unit % slabs, head],
            (((1,), (1,)), ((), ())),
            preferred_element_type=F32,
        )
        sb[slot, w, pl.ds(start, KC), :] = s
        return jnp.max(s.reshape(KC // 8, 8, QB), axis=0)

    def step(unit, slot, following):
        if unit is not None:
            head = unit // slabs
            rows = pl.ds(pl.multiple_of(head * 32, 32), 32)
        for w in range(2):
            top = total = None
            if unit is not None:
                peak = jnp.max(mb[slot, w], axis=0, keepdims=True)
            for start in range(0, length, KC):
                high = score(following, 1 - slot, w, start)
                top = high if top is None else jnp.maximum(top, high)
                if unit is not None:
                    p = jnp.exp2((sb[slot, w, pl.ds(start, KC), :] - peak) * scale).astype(BF)
                    v = jnp.concatenate([vt_refs[w][rows, pl.ds(start, KC)], ones], axis=0)
                    o = jnp.dot(v, p, preferred_element_type=F32)
                    total = o if total is None else total + o
            mb[1 - slot, w] = top
            if unit is not None:
                ot[unit % slabs, w, rows, :] = (total[:32] / total[32:33]).astype(BF)

    step(None, 1, 0)

    def body(turn, _):
        for j in range(unroll):
            unit = unroll * turn + j
            step(unit, j % 2, jnp.minimum(unit + 1, units - 1))
        return 0

    lax.fori_loop(0, units // unroll, body, 0)

    win = x_ref.shape[1] // 2
    lines = QB // win
    copies = []
    for slab in range(slabs):
        own = lax.axis_index("tile") // (2 * TILE_COLS)
        place = pl.ds(pl.multiple_of((own ^ steps[slab]) * lines, lines), lines)
        for w in range(2):
            cols = slice(w * win, w * win + win)
            y = lax.dot_general(
                ot[slab, w], wp_ref[...], (((0,), (0,)), ((), ())), preferred_element_type=F32
            )
            y = y.reshape(2, 4, lines // 2, win // 4, dim).transpose(0, 2, 1, 3, 4).reshape(lines, win, dim)
            y = x_ref[place, cols, :].astype(F32) + y + bp_ref[...].reshape(1, dim)
            stage[slab, :, cols, :] = y.astype(BF)
        copy = pltpu.make_async_copy(stage.at[slab], out_ref.at[place], sems.at[slab])
        copy.start()
        copies.append(copy)
    for copy in copies:
        copy.wait()


def attention(steps, queries, keys, values, tile_map, wp, bp, started=None):
    rows, cols, dim = tile_map.shape
    slabs = len(queries)
    lines = QB * 2 // cols
    more = [] if started is None else [started]
    anywhere = pl.BlockSpec(memory_space=pl.ANY)
    return pl.pallas_call(
        functools.partial(attention_kernel, steps),
        in_specs=[VM] * (slabs + 7) + [anywhere] * len(more),
        out_specs=anywhere,
        out_shape=jax.ShapeDtypeStruct(tile_map.shape, BF),
        input_output_aliases={slabs + 7: 0} if more else {},
        scratch_shapes=[
            pltpu.VMEM((slabs, HEADS, QB, 128), BF),
            pltpu.VMEM((2, 2, rows * cols // 2, QB), F32),
            pltpu.VMEM((2, 2, 8, QB), F32),
            pltpu.VMEM((slabs, 2, dim, QB), BF),
            pltpu.VMEM((slabs, lines, cols, dim), BF),
            pltpu.SemaphoreType.DMA((slabs,)),
        ],
        compiler_params=pltpu.CompilerParams(vmem_limit_bytes=40 * 2**20),
        cost_estimate=pl.CostEstimate(
            flops=8 * slabs * QB * 1024 * dim * 8,
            bytes_accessed=12 * 2**20,
            transcendentals=48 * slabs * QB * 1024,
        ),
        name="attention",
    )(*queries, *keys, *values, tile_map, wp, bp, *more)


def whole(array):
    return pl.BlockSpec(array.shape, lambda *i: (0,) * len(array.shape), pipeline_mode=pl.Buffered(1))


def wholes(*arrays):
    return [whole(array) for array in arrays]


def at_level(array, level):
    shape = (None,) + array.shape[1:]
    return pl.BlockSpec(shape, lambda *i: (level,) + (0,) * (len(shape) - 1), pipeline_mode=pl.Buffered(1))


def position():
    index = lax.axis_index("tile")
    return index // TILE_COLS, index % TILE_COLS


def params(mib):
    return pltpu.CompilerParams(vmem_limit_bytes=mib * 2**20)


def cost(flops, size):
    return pl.CostEstimate(flops=flops, bytes_accessed=size, transcendentals=0)


def round_up(count, unit):
    return -(-count // unit) * unit


def odd_column():
    return position()[1] % 2 == 1


def give_sides(keep_r, keep_l, to_partner, to_cross):
    odd = odd_column()
    to_partner[...] = jnp.where(odd, keep_l[...], keep_r[...]).astype(BF)
    to_cross[...] = jnp.where(odd, keep_r[...], keep_l[...]).astype(BF)


def take_sides(partner_ref, cross_ref):
    odd = odd_column()
    partner, cross = partner_ref[...].astype(F32), cross_ref[...].astype(F32)
    return jnp.where(odd, partner, cross), jnp.where(odd, cross, partner)


def side_pieces_kernel(before, after, left_ref, right_ref, to_partner, to_cross, keep_r, keep_l):
    high = left_ref.shape[0]
    span = right_ref.shape[1]
    keep_l[...] = jnp.zeros_like(keep_l)
    for r in range(high):
        keep_r[r * before : r * before + before, :] = right_ref[r].astype(F32)[span - before :]
        keep_l[r * before : r * before + after, :] = left_ref[r].astype(F32)[:after]
    give_sides(keep_r, keep_l, to_partner, to_cross)


def side_pieces(tile, before, after):
    high, wide, dim = tile.shape
    return pl.pallas_call(
        functools.partial(side_pieces_kernel, before, after),
        grid=(1,),
        in_specs=[
            pl.BlockSpec((high, 16, dim), lambda i: (0, 0, 0)),
            pl.BlockSpec((high, 16, dim), lambda i: (0, wide // 16 - 1, 0)),
        ],
        out_shape=[jax.ShapeDtypeStruct((high * before, dim), BF)] * 2,
        scratch_shapes=[pltpu.VMEM((high * before, dim), F32)] * 2,
        compiler_params=params(12),
        cost_estimate=cost(0, 2 * 2**20),
        name="side_pieces",
    )(tile, tile)


def line_pieces_kernel(before, after, high, top_ref, low_ref, left_ref, right_ref, to_low, to_up, keep_d, keep_u, side_l, side_r):
    wide = top_ref.shape[1]
    full = before + wide + after
    side_l[...], side_r[...] = take_sides(left_ref, right_ref)
    keep_d[...] = jnp.zeros_like(keep_d)
    keep_u[...] = jnp.zeros_like(keep_u)

    def fill(keep, line, r, values):
        base = line * full
        keep[base : base + before, :] = side_l[r * before : r * before + before, :]
        keep[base + before : base + before + wide, :] = values
        keep[base + before + wide : base + full, :] = side_r[r * before : r * before + after, :]

    for line in range(before):
        fill(keep_d, line, high - before + line, low_ref[line].astype(F32))
    for line in range(after):
        fill(keep_u, line, line, top_ref[line].astype(F32))
    to_low[...] = keep_d[...].astype(BF)
    to_up[...] = keep_u[...].astype(BF)


def line_pieces(tile, left, right, before, after):
    high, wide, dim = tile.shape
    full = before + wide + after
    down = round_up(before * full, 16)
    up = round_up(after * full, 16)
    low_size = before if high % before == 0 else 8
    assert high % low_size == 0
    return pl.pallas_call(
        functools.partial(line_low_kernel, low_size, before, after, high),
        grid=(1,),
        in_specs=[
            pl.BlockSpec((after if high % after == 0 else 8, wide, dim), lambda i: (0, 0, 0)),
            pl.BlockSpec((low_size, wide, dim), lambda i: (high // low_size - 1, 0, 0)),
            whole(left),
            whole(right),
        ],
        out_shape=[jax.ShapeDtypeStruct((down, dim), BF), jax.ShapeDtypeStruct((up, dim), BF)],
        scratch_shapes=[
            pltpu.VMEM((down, dim), F32),
            pltpu.VMEM((up, dim), F32),
            pltpu.VMEM(left.shape, F32),
            pltpu.VMEM(right.shape, F32),
        ],
        compiler_params=params(12),
        cost_estimate=cost(0, 2**20),
        name="line_pieces",
    )(tile, tile, left, right)


def line_low_kernel(low_size, before, after, high, top_ref, low_ref, *rest):
    line_pieces_kernel(before, after, high, top_ref, low_ref.at[pl.ds(low_size - before, before)], *rest)


def moved_by(value, rows, cols):
    count = lax.axis_size("tile")
    pairs = []
    for t in range(count):
        r, c = t // TILE_COLS + rows, t % TILE_COLS + cols
        if 0 <= r < count // TILE_COLS and 0 <= c < TILE_COLS:
            pairs.append((t, r * TILE_COLS + c))
    return lax.ppermute(value, "tile", pairs)


def after_these(value, *others):
    return lax.optimization_barrier((value,) + others)[0]


def exchange_rims(tile, pieces, before, after, early, beside):
    tiles = range(lax.axis_size("tile"))
    left = lax.ppermute(pieces[0], "tile", [(t, t ^ 1) for t in tiles])
    between = [(t, t + 1) for t in tiles if t % 2 == 1 and (t + 1) % TILE_COLS]
    right = lax.ppermute(pieces[1], "tile", between + [(b, a) for a, b in between])
    left, right, *first = lax.optimization_barrier((left, right, *early(pieces[0])))
    down, up = line_pieces(tile, left, right, before, after)
    above, below = moved_by(down, 1, 0), moved_by(up, -1, 0)
    result = beside((left, right), down)
    above, below, *result = lax.optimization_barrier((above, below, *result))
    return (left, right, above, below), first, result


def erf_gelu(y):
    return 0.5 * y * (1.0 + lax.erf(y * 0.7071067811865476))


def conv_gelu(padded, kernel_ref, g_ref, own_rows, own_cols, part_ref):
    rows, cols, dim = g_ref.shape
    column = lax.broadcasted_iota(jnp.int32, (cols, 128), 0)
    mine = (column >= own_cols[0]) & (column < own_cols[1])
    for group in range(dim // 128):
        lanes = slice(128 * group, 128 * group + 128)
        taps = [[kernel_ref[a, b : b + 1, lanes].astype(F32) for b in range(3)] for a in range(3)]

        def line(r, total):
            y = None
            for a in range(3):
                for b in range(3):
                    term = padded[r + a, b : b + cols, lanes] * taps[a][b]
                    y = term if y is None else y + term
            g = erf_gelu(y)
            g_ref[r, :, lanes] = g
            counted = jnp.sum(jnp.where(mine, g, 0.0).reshape(cols // 8, 8, 128), axis=0)
            return total + jnp.where((r >= own_rows[0]) & (r < own_rows[1]), counted, 0.0)

        total = lax.fori_loop(0, rows, line, jnp.zeros((8, 128), F32), unroll=True)
        total = jnp.sum(total, axis=0, keepdims=True)
        part_ref[:, group, :] += jnp.broadcast_to(total, (part_ref.shape[0], 128))


def copy_centre(padded, rest_ref):
    rows, cols, _ = rest_ref.shape

    def line(r, _):
        rest_ref[r] = padded[r + 1, 1 : 1 + cols, :].astype(BF)
        return 0

    lax.fori_loop(0, rows, line, 0)


def thirds(row):
    high = row.astype(BF).astype(F32)
    mid = (row - high).astype(BF).astype(F32)
    low = row - high - mid
    index = lax.broadcasted_iota(jnp.int32, (16, row.shape[1]), 0)
    block = jnp.where(index == 0, high, jnp.where(index == 1, mid, jnp.where(index == 2, low, 0.0)))
    return block.astype(BF)


def gate_row(sums_ref, cells, reduce_ref, expand_ref):
    total = jnp.sum(sums_ref[...], axis=0)
    groups = reduce_ref.shape[1] // 128
    mean = jnp.concatenate([total[group : group + 1] for group in range(groups)], axis=1) / cells
    inner = lax.dot_general(
        thirds(mean), reduce_ref[...], (((1,), (1,)), ((), ())), preferred_element_type=F32
    )
    inner = jnp.sum(inner, axis=0, keepdims=True)
    inner = erf_gelu(inner)
    outer = jnp.sum(jnp.dot(thirds(inner), expand_ref[...], preferred_element_type=F32), axis=0, keepdims=True)
    return 1.0 / (1.0 + jnp.exp(-outer))


def mix_lines(g_ref, gate, mix_ref, rest_ref, z_ref, lines, bounds):
    rows, cols, dim = g_ref.shape
    row_low, row_high, col_low, col_high = bounds
    column = lax.broadcasted_iota(jnp.int32, (cols, 1), 0)
    inside = (column >= col_low) & (column < col_high)
    u = (g_ref[...] * gate).astype(BF).reshape(rows * cols, dim)
    product = jnp.dot(u, mix_ref[...], preferred_element_type=F32).reshape(rows, cols, dim)
    for k in range(rows):
        z = (rest_ref[k].astype(F32) + product[k]).astype(BF).astype(F32)
        keep = inside & (lines[k] >= row_low) & (lines[k] < row_high)
        z_ref[lines[k]] = jnp.where(keep, z, -jnp.inf)


def pooled_line(z_ref, line_ref, i, count):
    most = jnp.maximum(jnp.maximum(z_ref[2 * i], z_ref[2 * i + 1]), z_ref[2 * i + 2])
    groups = []
    for group in range(line_ref.shape[0]):
        line_ref[group] = most[:, 128 * group : 128 * group + 128]
        parts = [line_ref[group, pl.ds(s, count, stride=2), :] for s in range(3)]
        groups.append(jnp.maximum(jnp.maximum(parts[0], parts[1]), parts[2]))
    return jnp.concatenate(groups, axis=1)


def fill_sides(x_ref, left_ref, right_ref, before, after, padded, stage):
    high, wide, _ = x_ref.shape
    full = before + wide + after

    def line(r, _):
        padded[r, before : before + wide, :] = x_ref[r].astype(F32)
        return 0

    lax.fori_loop(0, high, line, 0)
    left, right = take_sides(left_ref, right_ref)
    stage[...] = left
    for r in range(high):
        padded[r, 0:before, :] = stage[r * before : r * before + before, :]
    stage[...] = right
    for r in range(high):
        padded[r, before + wide : full, :] = stage[r * before : r * before + after, :]


def inner_kernel(before, after, x_ref, l_ref, r_ref, kernel_ref, g_ref, rest_ref, part_ref, padded, stage):
    _, wide, _ = x_ref.shape
    step = g_ref.shape[0]
    turn = pl.program_id(0)

    @pl.when(turn == 0)
    def _():
        fill_sides(x_ref, l_ref, r_ref, before, after, padded, stage)
        part_ref[...] = jnp.zeros_like(part_ref)

    block = padded.at[pl.ds(turn * step, step + 2)]
    copy_centre(block, rest_ref)
    conv_gelu(block, kernel_ref, g_ref, (0, step), (before - 1, before - 1 + wide), part_ref)


def activate_inner(tile, left, right, kernels, level, before, after, step):
    high, wide, dim = tile.shape
    rows, cols = high - 2, round_up(wide + before + after - 2, 8)
    copies = lax.axis_size("tile")
    block = pl.BlockSpec((step, cols, dim), lambda i: (i, 0, 0))
    return pl.pallas_call(
        functools.partial(inner_kernel, before, after),
        grid=(rows // step,),
        in_specs=wholes(tile, left, right) + [at_level(kernels, level)],
        out_specs=[block, block, pl.BlockSpec((copies, 8, 128), lambda i: (0, 0, 0))],
        out_shape=[
            jax.ShapeDtypeStruct((rows, cols, dim), F32),
            jax.ShapeDtypeStruct((rows, cols, dim), BF),
            jax.ShapeDtypeStruct((copies, 8, 128), F32),
        ],
        scratch_shapes=[
            pltpu.VMEM((high, round_up(cols + 2, 8), dim), F32),
            pltpu.VMEM((max(left.shape[0], right.shape[0]), dim), F32),
        ],
        compiler_params=params(28 if level == 0 else 20),
        cost_estimate=cost(400 * rows * cols * dim, 6 * rows * cols * dim),
        name="activate_inner",
    )(tile, left, right, kernels)


def edge_kernel(high, before, after, top_ref, low_ref, l_ref, r_ref, a_ref, b_ref, kernel_ref, sum_ref, g_ref, rest_ref, part_ref, upper, lower, side_l, side_r, stage):
    wide = top_ref.shape[1]
    full = before + wide + after
    own = (before - 1, before - 1 + wide)
    side_l[...], side_r[...] = take_sides(l_ref, r_ref)

    def fill(padded, at, r, values):
        padded[at, 0:before, :] = side_l[r * before : r * before + before, :]
        padded[at, before : before + wide, :] = values.astype(F32)
        padded[at, before + wide : full, :] = side_r[r * before : r * before + after, :]

    for k in range(2):
        fill(upper, before + k, k, top_ref[k])
        fill(lower, k, high - 2 + k, low_ref[k])
    stage[: a_ref.shape[0], :] = a_ref[...].astype(F32)
    for k in range(before):
        upper[k, 0:full, :] = stage[k * full : k * full + full, :]
    stage[: b_ref.shape[0], :] = b_ref[...].astype(F32)
    for k in range(after):
        lower[2 + k, 0:full, :] = stage[k * full : k * full + full, :]
    part_ref[...] = sum_ref[...]
    up, low = pl.ds(0, before), pl.ds(before, after)
    copy_centre(upper, rest_ref.at[up])
    copy_centre(lower, rest_ref.at[low])
    conv_gelu(upper, kernel_ref, g_ref.at[up], (before - 1, before), own, part_ref)
    conv_gelu(lower, kernel_ref, g_ref.at[low], (0, 1), own, part_ref)


def activate_edge(tile, rims, kernels, part, level, before, after):
    high, wide, dim = tile.shape
    cols = round_up(wide + before + after - 2, 8)
    padded = round_up(cols + 2, 8)
    stage = max(r.shape[0] for r in rims)
    left, right, above, below = rims
    lines = before + after
    outs = [
        jax.ShapeDtypeStruct((lines, cols, dim), F32),
        jax.ShapeDtypeStruct((lines, cols, dim), BF),
        jax.ShapeDtypeStruct(part.shape, F32),
    ]
    return pl.pallas_call(
        functools.partial(edge_kernel, high, before, after),
        grid=(1,),
        in_specs=[
            pl.BlockSpec((2, wide, dim), lambda i: (0, 0, 0)),
            pl.BlockSpec((2, wide, dim), lambda i: (high // 2 - 1, 0, 0)),
        ]
        + wholes(*rims)
        + [at_level(kernels, level), whole(part)],
        out_specs=wholes(*outs),
        out_shape=outs,
        scratch_shapes=[
            pltpu.VMEM((before + 2, padded, dim), F32),
            pltpu.VMEM((after + 2, padded, dim), F32),
            pltpu.VMEM(left.shape, F32),
            pltpu.VMEM(right.shape, F32),
            pltpu.VMEM((stage, dim), F32),
        ],
        compiler_params=params(16),
        cost_estimate=cost(400 * lines * cols * dim, 6 * lines * cols * dim),
        name="activate_edge",
    )(tile, tile, *rims, kernels, part)


def mix0_kernel(cells, before, after, sums, red, exp, mix, g_ref, rest, g_edge, rest_edge, x_out, to_partner, to_cross, gates, z, line, keep_r, keep_l):
    step, cols, dim = g_ref.shape
    high, wide, _ = x_out.shape
    turn = pl.program_id(0)

    pos = position()
    bounds = (jnp.where(pos[0] == 0, 1, 0), z.shape[0], jnp.where(pos[1] == 0, 1, 0), cols)

    @pl.when(turn == 0)
    def _():
        gates[...] = jnp.broadcast_to(gate_row(sums, cells, red, exp), gates.shape)
        keep_l[...] = jnp.zeros_like(keep_l)
        mix_lines(g_edge, gates[:1, :], mix, rest_edge, z, (0, 1, z.shape[0] - 1), bounds)

    mix_lines(g_ref, gates[:1, :], mix, rest, z, [2 + turn * step + k for k in range(step)], bounds)

    @pl.when(turn == pl.num_programs(0) - 1)
    def _():
        for i in range(high):
            out = pooled_line(z, line, i, wide)
            x_out[i] = out.astype(BF)
            keep_r[i * before : i * before + before, :] = out[wide - before :]
            keep_l[i * before : i * before + after, :] = out[:after]
        give_sides(keep_r, keep_l, to_partner, to_cross)


def level_specs(sums, red, exp, mix, level):
    return [whole(sums), at_level(red, level), at_level(exp, level), at_level(mix, level)]


def mix0(sums, red, exp, mix, g, rest, edges, cells, high, wide, before, after, step):
    rows, cols, dim = g.shape
    block = pl.BlockSpec((step, cols, dim), lambda i: (i, 0, 0))
    outs = [
        jax.ShapeDtypeStruct((high, wide, dim), BF),
        jax.ShapeDtypeStruct((high * before, dim), BF),
        jax.ShapeDtypeStruct((high * before, dim), BF),
    ]
    return pl.pallas_call(
        functools.partial(mix0_kernel, cells, before, after),
        grid=(rows // step,),
        in_specs=level_specs(sums, red, exp, mix, 0) + [block, block] + wholes(*edges),
        out_specs=wholes(*outs),
        out_shape=outs,
        scratch_shapes=[
            pltpu.VMEM((8, dim), F32),
            pltpu.VMEM((rows + 3, cols, dim), F32),
            pltpu.VMEM((dim // 128, cols, 128), F32),
            pltpu.VMEM((high * before, dim), F32),
            pltpu.VMEM((high * before, dim), F32),
        ],
        compiler_params=params(32),
        cost_estimate=cost(2 * rows * cols * dim * dim, 6 * rows * cols * dim),
        name="mix0",
    )(sums, red, exp, mix, g, rest, *edges)


def mix1_kernel(cells, size, before, sums, red, exp, mix, g_ref, rest, g_edge, rest_edge, kernel, g_out, rest_out, part, z, line, padded):
    rows, cols, dim = g_ref.shape
    side_r, side_c, map_side = size
    gate = gate_row(sums, cells, red, exp)
    shift = before - 1
    pos = position()
    row_low = shift - pos[0] * side_r
    col_low = shift - pos[1] * side_c
    bounds = (row_low, row_low + map_side, col_low, col_low + map_side)
    inner = range(before, before + rows)
    mix_lines(g_ref, gate, mix, rest, z, inner, bounds)
    mix_lines(g_edge, gate, mix, rest_edge, z, [k for k in range(z.shape[0]) if k not in inner], bounds)
    count_r, count_c = padded.shape[0], (cols - 1) // 2
    row_two = 2 - pos[0] * (side_r // 2)
    col_two = 2 - pos[1] * (side_c // 2)
    column = lax.broadcasted_iota(jnp.int32, (count_c, 1), 0)
    inside = (column >= col_two) & (column < col_two + map_side // 2)
    for i in range(count_r):
        out = pooled_line(z, line, i, count_c)
        keep = inside & (i >= row_two) & (i < row_two + map_side // 2)
        padded[i, 0:count_c, :] = jnp.where(keep, out, 0.0)
    copy_centre(padded, rest_out)
    part[...] = jnp.zeros_like(part)
    conv_gelu(padded, kernel, g_out, (1, 1 + side_r // 2), (1, 1 + side_c // 2), part)


def mix1(sums, red, exp, mix, g, rest, edges, kernels, cells, size, before):
    rows, cols, dim = g.shape
    rows += edges[0].shape[0]
    out_rows, out_cols = (rows - 1) // 2 - 2, round_up((cols - 1) // 2 - 2, 8)
    outs = [
        jax.ShapeDtypeStruct((out_rows, out_cols, dim), F32),
        jax.ShapeDtypeStruct((out_rows, out_cols, dim), BF),
        jax.ShapeDtypeStruct(sums.shape, F32),
    ]
    return pl.pallas_call(
        functools.partial(mix1_kernel, cells, size, before),
        grid=(1,),
        in_specs=level_specs(sums, red, exp, mix, 1) + wholes(g, rest, *edges) + [at_level(kernels, 2)],
        out_specs=wholes(*outs),
        out_shape=outs,
        scratch_shapes=[
            pltpu.VMEM((rows, cols, dim), F32),
            pltpu.VMEM((dim // 128, cols, 128), F32),
            pltpu.VMEM((out_rows + 2, round_up(out_cols + 2, 8), dim), F32),
        ],
        compiler_params=params(18),
        cost_estimate=cost(2 * rows * cols * dim * dim, 6 * rows * cols * dim),
        name="mix1",
    )(sums, red, exp, mix, g, rest, *edges, kernels)


def mix2_kernel(cells, high, wide, sums, red, exp, mix, g_ref, rest, x_out, z, line, keep):
    rows, cols, dim = g_ref.shape
    gate = gate_row(sums, cells, red, exp)
    pos = position()
    bounds = (jnp.where(pos[0] == 0, 1, 0), rows, jnp.where(pos[1] == 0, 1, 0), cols)
    mix_lines(g_ref, gate, mix, rest, z, range(rows), bounds)
    for i in range(high):
        keep[i * wide : i * wide + wide, :] = pooled_line(z, line, i, wide)
    x_out[...] = jnp.broadcast_to(keep[...].astype(BF), x_out.shape)


def mix2(sums, red, exp, mix, g, rest, cells, high, wide, copies):
    rows, cols, dim = g.shape
    out = jax.ShapeDtypeStruct((copies, high * wide, dim), BF)
    return pl.pallas_call(
        functools.partial(mix2_kernel, cells, high, wide),
        grid=(1,),
        in_specs=level_specs(sums, red, exp, mix, 2) + wholes(g, rest),
        out_specs=whole(out),
        out_shape=out,
        scratch_shapes=[
            pltpu.VMEM((rows, cols, dim), F32),
            pltpu.VMEM((dim // 128, cols, 128), F32),
            pltpu.VMEM((high * wide, dim), F32),
        ],
        compiler_params=params(10),
        cost_estimate=cost(2 * rows * cols * dim * dim, 6 * rows * cols * dim),
        name="mix2",
    )(sums, red, exp, mix, g, rest)


def everyones(copies):
    return lax.all_to_all(copies, "tile", 0, 0, tiled=True)


def query_slab(tile_map, dw_kernel, se_reduce, se_expand, mix_weight, keys_of):
    high, wide, dim = tile_map.shape
    tiles = lax.axis_size("tile")
    cells = high * wide * tiles
    group = 2 * TILE_COLS
    def inner(tile, level, sides, held, *halos):
        return activate_inner(after_these(tile, held), *sides, dw_kernel, level, *halos)

    rims, (kt0, vt0), (g, rest, part) = exchange_rims(
        tile_map,
        side_pieces(tile_map, 2, 1),
        2,
        1,
        lambda held: keys_of(0, held),
        lambda sides, held: inner(tile_map, 0, sides, held, 2, 1, 10),
    )
    *edges, part = activate_edge(tile_map, rims, dw_kernel, part, 0, 2, 1)
    coarse, *sides = mix0(
        everyones(part), se_reduce, se_expand, mix_weight, g, rest, edges, cells, high // 2, wide // 2, 6, 3, 10
    )

    rims, (kt1, vt1), (g, rest, part) = exchange_rims(
        coarse,
        sides,
        6,
        3,
        lambda held: keys_of(1, held),
        lambda sides, held: inner(coarse, 1, sides, held, 6, 3, high // 2 - 2),
    )
    *edges, part = activate_edge(coarse, rims, dw_kernel, part, 1, 6, 3)
    size = (high // 2, wide // 2, high // 2 * (tiles // TILE_COLS))
    g, rest, part = mix1(
        everyones(part), se_reduce, se_expand, mix_weight, g, rest, edges, dw_kernel, cells // 4, size, 6
    )
    query = mix2(
        everyones(part), se_reduce, se_expand, mix_weight, g, rest, cells // 16, high // 8, wide // 8, group
    )
    groups = [list(range(group * x, group * x + group)) for x in range(tiles // group)]
    slab = lax.all_to_all(query, "tile", 0, 0, tiled=True, axis_index_groups=groups)
    return slab.reshape(-1, dim), (kt0, kt1), (vt0, vt1)


def body(
    features,
    dw_kernel,
    se_reduce,
    se_expand,
    mix_weight,
    norm_gain,
    kv_weight,
    kv_bias,
    proj_weight,
    proj_bias,
):
    tile_map = features[0]
    se_reduce = jnp.swapaxes(se_reduce, 1, 2)

    def keys_of(window, held):
        return keys_values(after_these(tile_map, held), norm_gain, kv_weight, kv_bias, window)

    slab, keys, values = query_slab(tile_map, dw_kernel, se_reduce, se_expand, mix_weight, keys_of)
    tiles = lax.axis_size("tile")
    group = 2 * TILE_COLS
    def from_x(value, step):
        return lax.ppermute(value, "tile", [(t, t ^ group * step) for t in range(tiles)])

    near = [from_x(slab, 1), from_x(slab, 3)]
    rest = (keys, values, tile_map, proj_weight, proj_bias)
    out = attention((0,), [slab], *rest)
    far, out = lax.optimization_barrier((slab, out))
    far = from_x(far, 2)
    out = attention((1, 3), near, *rest, out)
    return attention((2,), [far], *rest, out)[None]


def solution(mesh):
    in_specs = (P(("scene", "tile"), None, None, None), P(), P(), P(), P(), P(), P(), P(), P(), P())
    out_specs = P(("scene", "tile"), None, None, None)
    return jax.shard_map(body, mesh=mesh, in_specs=in_specs, out_specs=out_specs, check_vma=False)
```

```python
import functools

import jax
import jax.numpy as jnp
from jax import lax
from jax.experimental import pallas as pl
from jax.experimental.pallas import tpu as pltpu
from jax.sharding import PartitionSpec as P

HEADS = 24
TILE_COLS = 4
EPSILON = 1e-05
BF = jnp.bfloat16
F32 = jnp.float32
VM = pl.BlockSpec(memory_space=pltpu.VMEM)
LOG2E = 1.4426950408889634
QB = 256
KC = 512
UNROLL = {1: 8, 2: 8}


def kv_kernel(x_ref, gain_ref, w_ref, b_ref, kt_ref, vt_ref):
    dim = x_ref.shape[-1]
    tokens = x_ref.shape[0] * x_ref.shape[1]
    x = x_ref[...].reshape(tokens, dim).astype(F32)
    centre = jnp.mean(x, axis=1, keepdims=True)
    moved = x - centre
    spread = jnp.mean(jnp.square(moved), axis=1, keepdims=True)
    normed = (moved * lax.rsqrt(spread + EPSILON) * gain_ref[...].reshape(1, dim)).astype(BF)
    keys = (jnp.dot(normed, w_ref[:, :dim], preferred_element_type=F32) + b_ref[:dim].reshape(1, dim)).astype(BF)
    for group in range(dim // 128):
        kt_ref[group] = keys[:, 128 * group : 128 * group + 128]
    vals = jnp.dot(normed, w_ref[:, dim:], preferred_element_type=F32) + b_ref[dim:].reshape(1, dim)
    vt_ref[...] = vals.T.astype(BF)


def keys_values(tile_map, gain, weight, bias, window):
    win, _, dim = tile_map.shape
    step = 8
    tokens = step * win
    return pl.pallas_call(
        kv_kernel,
        grid=(win // step,),
        in_specs=[
            pl.BlockSpec((step, win, dim), lambda i: (i, window, 0)),
            pl.BlockSpec((dim,), lambda i: (0,)),
            pl.BlockSpec((dim, 2 * dim), lambda i: (0, 0)),
            pl.BlockSpec((2 * dim,), lambda i: (0,)),
        ],
        out_specs=[
            pl.BlockSpec((dim // 128, tokens, 128), lambda i: (0, i, 0)),
            pl.BlockSpec((dim, tokens), lambda i: (0, i)),
        ],
        out_shape=[
            jax.ShapeDtypeStruct((dim // 128, win * win, 128), BF),
            jax.ShapeDtypeStruct((dim, win * win), BF),
        ],
        compiler_params=pltpu.CompilerParams(vmem_limit_bytes=24 * 2**20),
        cost_estimate=pl.CostEstimate(
            flops=8 * win * win * dim * dim, bytes_accessed=8 * 2**20, transcendentals=0
        ),
        name="keys_values",
    )(tile_map, gain, weight, bias)


def attention_kernel(steps, *refs):
    slabs = len(steps)
    q_refs = refs[:slabs]
    kt_refs, vt_refs = refs[slabs : slabs + 2], refs[slabs + 2 : slabs + 4]
    x_ref, wp_ref, bp_ref = refs[slabs + 4 : slabs + 7]
    out_ref, qa, sb, mb, ot, stage, sems = refs[-7:]
    dim = x_ref.shape[2]
    length = kt_refs[0].shape[1]
    units = HEADS * slabs
    unroll = UNROLL[slabs]
    scale = (dim // HEADS) ** (-0.5) * LOG2E
    lane = lax.broadcasted_iota(jnp.int32, (1, 128), 1)
    for slab in range(slabs):
        for group in range(dim // 128):
            q = q_refs[slab][:, 128 * group : 128 * group + 128]
            for part in range(4):
                qa[slab, 4 * group + part] = jnp.where(lane // 32 == part, q, jnp.zeros_like(q))
    ones = jnp.ones((16, KC), BF)

    def score(unit, slot, w, start):
        head = unit // slabs
        s = lax.dot_general(
            kt_refs[w][head // 4, pl.ds(start, KC), :],
            qa[unit % slabs, head],
            (((1,), (1,)), ((), ())),
            preferred_element_type=F32,
        )
        sb[slot, w, pl.ds(start, KC), :] = s
        return jnp.max(s.reshape(KC // 8, 8, QB), axis=0)

    def step(unit, slot, following):
        if unit is not None:
            head = unit // slabs
            rows = pl.ds(pl.multiple_of(head * 32, 32), 32)
        for w in range(2):
            top = total = None
            if unit is not None:
                peak = jnp.max(mb[slot, w], axis=0, keepdims=True)
            for start in range(0, length, KC):
                high = score(following, 1 - slot, w, start)
                top = high if top is None else jnp.maximum(top, high)
                if unit is not None:
                    p = jnp.exp2((sb[slot, w, pl.ds(start, KC), :] - peak) * scale).astype(BF)
                    v = jnp.concatenate([vt_refs[w][rows, pl.ds(start, KC)], ones], axis=0)
                    o = jnp.dot(v, p, preferred_element_type=F32)
                    total = o if total is None else total + o
            mb[1 - slot, w] = top
            if unit is not None:
                ot[unit % slabs, w, rows, :] = (total[:32] / total[32:33]).astype(BF)

    step(None, 1, 0)

    def body(turn, _):
        for j in range(unroll):
            unit = unroll * turn + j
            step(unit, j % 2, jnp.minimum(unit + 1, units - 1))
        return 0

    lax.fori_loop(0, units // unroll, body, 0)

    win = x_ref.shape[1] // 2
    lines = QB // win
    copies = []
    for slab in range(slabs):
        own = lax.axis_index("tile") // (2 * TILE_COLS)
        place = pl.ds(pl.multiple_of((own ^ steps[slab]) * lines, lines), lines)
        for w in range(2):
            cols = slice(w * win, w * win + win)
            y = lax.dot_general(
                ot[slab, w], wp_ref[...], (((0,), (0,)), ((), ())), preferred_element_type=F32
            )
            y = y.reshape(2, 4, lines // 2, win // 4, dim).transpose(0, 2, 1, 3, 4).reshape(lines, win, dim)
            y = x_ref[place, cols, :].astype(F32) + y + bp_ref[...].reshape(1, dim)
            stage[slab, :, cols, :] = y.astype(BF)
        copy = pltpu.make_async_copy(stage.at[slab], out_ref.at[place], sems.at[slab])
        copy.start()
        copies.append(copy)
    for copy in copies:
        copy.wait()


def attention(steps, queries, keys, values, tile_map, wp, bp, started=None):
    rows, cols, dim = tile_map.shape
    slabs = len(queries)
    lines = QB * 2 // cols
    more = [] if started is None else [started]
    anywhere = pl.BlockSpec(memory_space=pl.ANY)
    return pl.pallas_call(
        functools.partial(attention_kernel, steps),
        in_specs=[VM] * (slabs + 7) + [anywhere] * len(more),
        out_specs=anywhere,
        out_shape=jax.ShapeDtypeStruct(tile_map.shape, BF),
        input_output_aliases={slabs + 7: 0} if more else {},
        scratch_shapes=[
            pltpu.VMEM((slabs, HEADS, QB, 128), BF),
            pltpu.VMEM((2, 2, rows * cols // 2, QB), F32),
            pltpu.VMEM((2, 2, 8, QB), F32),
            pltpu.VMEM((slabs, 2, dim, QB), BF),
            pltpu.VMEM((slabs, lines, cols, dim), BF),
            pltpu.SemaphoreType.DMA((slabs,)),
        ],
        compiler_params=pltpu.CompilerParams(vmem_limit_bytes=40 * 2**20),
        cost_estimate=pl.CostEstimate(
            flops=8 * slabs * QB * 1024 * dim * 8,
            bytes_accessed=12 * 2**20,
            transcendentals=48 * slabs * QB * 1024,
        ),
        name="attention",
    )(*queries, *keys, *values, tile_map, wp, bp, *more)


def whole(array):
    return pl.BlockSpec(array.shape, lambda *i: (0,) * len(array.shape), pipeline_mode=pl.Buffered(1))


def wholes(*arrays):
    return [whole(array) for array in arrays]


def at_level(array, level):
    shape = (None,) + array.shape[1:]
    return pl.BlockSpec(shape, lambda *i: (level,) + (0,) * (len(shape) - 1), pipeline_mode=pl.Buffered(1))


def position():
    index = lax.axis_index("tile")
    return index // TILE_COLS, index % TILE_COLS


def params(mib):
    return pltpu.CompilerParams(vmem_limit_bytes=mib * 2**20)


def cost(flops, size):
    return pl.CostEstimate(flops=flops, bytes_accessed=size, transcendentals=0)


def round_up(count, unit):
    return -(-count // unit) * unit


def odd_column():
    return position()[1] % 2 == 1


def give_sides(keep_r, keep_l, to_partner, to_cross):
    odd = odd_column()
    to_partner[...] = jnp.where(odd, keep_l[...], keep_r[...]).astype(BF)
    to_cross[...] = jnp.where(odd, keep_r[...], keep_l[...]).astype(BF)


def take_sides(partner_ref, cross_ref):
    odd = odd_column()
    partner, cross = partner_ref[...].astype(F32), cross_ref[...].astype(F32)
    return jnp.where(odd, partner, cross), jnp.where(odd, cross, partner)


def side_pieces_kernel(before, after, left_ref, right_ref, to_partner, to_cross, keep_r, keep_l):
    high = left_ref.shape[0]
    span = right_ref.shape[1]
    keep_l[...] = jnp.zeros_like(keep_l)
    for r in range(high):
        keep_r[r * before : r * before + before, :] = right_ref[r].astype(F32)[span - before :]
        keep_l[r * before : r * before + after, :] = left_ref[r].astype(F32)[:after]
    give_sides(keep_r, keep_l, to_partner, to_cross)


def side_pieces(tile, before, after):
    high, wide, dim = tile.shape
    return pl.pallas_call(
        functools.partial(side_pieces_kernel, before, after),
        grid=(1,),
        in_specs=[
            pl.BlockSpec((high, 16, dim), lambda i: (0, 0, 0)),
            pl.BlockSpec((high, 16, dim), lambda i: (0, wide // 16 - 1, 0)),
        ],
        out_shape=[jax.ShapeDtypeStruct((high * before, dim), BF)] * 2,
        scratch_shapes=[pltpu.VMEM((high * before, dim), F32)] * 2,
        compiler_params=params(12),
        cost_estimate=cost(0, 2 * 2**20),
        name="side_pieces",
    )(tile, tile)


def line_pieces_kernel(before, after, high, top_ref, low_ref, left_ref, right_ref, to_low, to_up, keep_d, keep_u, side_l, side_r):
    wide = top_ref.shape[1]
    full = before + wide + after
    side_l[...], side_r[...] = take_sides(left_ref, right_ref)
    keep_d[...] = jnp.zeros_like(keep_d)
    keep_u[...] = jnp.zeros_like(keep_u)

    def fill(keep, line, r, values):
        base = line * full
        keep[base : base + before, :] = side_l[r * before : r * before + before, :]
        keep[base + before : base + before + wide, :] = values
        keep[base + before + wide : base + full, :] = side_r[r * before : r * before + after, :]

    for line in range(before):
        fill(keep_d, line, high - before + line, low_ref[line].astype(F32))
    for line in range(after):
        fill(keep_u, line, line, top_ref[line].astype(F32))
    to_low[...] = keep_d[...].astype(BF)
    to_up[...] = keep_u[...].astype(BF)


def line_pieces(tile, left, right, before, after):
    high, wide, dim = tile.shape
    full = before + wide + after
    down = round_up(before * full, 16)
    up = round_up(after * full, 16)
    low_size = before if high % before == 0 else 8
    assert high % low_size == 0
    return pl.pallas_call(
        functools.partial(line_low_kernel, low_size, before, after, high),
        grid=(1,),
        in_specs=[
            pl.BlockSpec((after if high % after == 0 else 8, wide, dim), lambda i: (0, 0, 0)),
            pl.BlockSpec((low_size, wide, dim), lambda i: (high // low_size - 1, 0, 0)),
            whole(left),
            whole(right),
        ],
        out_shape=[jax.ShapeDtypeStruct((down, dim), BF), jax.ShapeDtypeStruct((up, dim), BF)],
        scratch_shapes=[
            pltpu.VMEM((down, dim), F32),
            pltpu.VMEM((up, dim), F32),
            pltpu.VMEM(left.shape, F32),
            pltpu.VMEM(right.shape, F32),
        ],
        compiler_params=params(12),
        cost_estimate=cost(0, 2**20),
        name="line_pieces",
    )(tile, tile, left, right)


def line_low_kernel(low_size, before, after, high, top_ref, low_ref, *rest):
    line_pieces_kernel(before, after, high, top_ref, low_ref.at[pl.ds(low_size - before, before)], *rest)


def moved_by(value, rows, cols):
    count = lax.axis_size("tile")
    pairs = []
    for t in range(count):
        r, c = t // TILE_COLS + rows, t % TILE_COLS + cols
        if 0 <= r < count // TILE_COLS and 0 <= c < TILE_COLS:
            pairs.append((t, r * TILE_COLS + c))
    return lax.ppermute(value, "tile", pairs)


def after_these(value, *others):
    return lax.optimization_barrier((value,) + others)[0]


def exchange_rims(tile, pieces, before, after, early, beside):
    tiles = range(lax.axis_size("tile"))
    left = lax.ppermute(pieces[0], "tile", [(t, t ^ 1) for t in tiles])
    between = [(t, t + 1) for t in tiles if t % 2 == 1 and (t + 1) % TILE_COLS]
    right = lax.ppermute(pieces[1], "tile", between + [(b, a) for a, b in between])
    left, right, *first = lax.optimization_barrier((left, right, *early(pieces[0])))
    down, up = line_pieces(tile, left, right, before, after)
    above, below = moved_by(down, 1, 0), moved_by(up, -1, 0)
    result = beside((left, right), down)
    above, below, *result = lax.optimization_barrier((above, below, *result))
    return (left, right, above, below), first, result


def erf_gelu(y):
    return 0.5 * y * (1.0 + lax.erf(y * 0.7071067811865476))


def conv_gelu(padded, kernel_ref, g_ref, own_rows, own_cols, part_ref):
    rows, cols, dim = g_ref.shape
    column = lax.broadcasted_iota(jnp.int32, (cols, 128), 0)
    mine = (column >= own_cols[0]) & (column < own_cols[1])
    for group in range(dim // 128):
        lanes = slice(128 * group, 128 * group + 128)
        taps = [[kernel_ref[a, b : b + 1, lanes].astype(F32) for b in range(3)] for a in range(3)]

        def line(r, total):
            y = None
            for a in range(3):
                for b in range(3):
                    term = padded[r + a, b : b + cols, lanes] * taps[a][b]
                    y = term if y is None else y + term
            g = erf_gelu(y)
            g_ref[r, :, lanes] = g
            counted = jnp.sum(jnp.where(mine, g, 0.0).reshape(cols // 8, 8, 128), axis=0)
            return total + jnp.where((r >= own_rows[0]) & (r < own_rows[1]), counted, 0.0)

        total = lax.fori_loop(0, rows, line, jnp.zeros((8, 128), F32), unroll=5)
        total = jnp.sum(total, axis=0, keepdims=True)
        part_ref[:, group, :] += jnp.broadcast_to(total, (part_ref.shape[0], 128))


def copy_centre(padded, rest_ref):
    rows, cols, _ = rest_ref.shape

    def line(r, _):
        rest_ref[r] = padded[r + 1, 1 : 1 + cols, :].astype(BF)
        return 0

    lax.fori_loop(0, rows, line, 0)


def thirds(row):
    high = row.astype(BF).astype(F32)
    mid = (row - high).astype(BF).astype(F32)
    low = row - high - mid
    index = lax.broadcasted_iota(jnp.int32, (16, row.shape[1]), 0)
    block = jnp.where(index == 0, high, jnp.where(index == 1, mid, jnp.where(index == 2, low, 0.0)))
    return block.astype(BF)


def gate_row(sums_ref, cells, reduce_ref, expand_ref):
    total = jnp.sum(sums_ref[...], axis=0)
    groups = reduce_ref.shape[1] // 128
    mean = jnp.concatenate([total[group : group + 1] for group in range(groups)], axis=1) / cells
    inner = lax.dot_general(
        thirds(mean), reduce_ref[...], (((1,), (1,)), ((), ())), preferred_element_type=F32
    )
    inner = jnp.sum(inner, axis=0, keepdims=True)
    inner = erf_gelu(inner)
    outer = jnp.sum(jnp.dot(thirds(inner), expand_ref[...], preferred_element_type=F32), axis=0, keepdims=True)
    return 1.0 / (1.0 + jnp.exp(-outer))


def mix_lines(g_ref, gate, mix_ref, rest_ref, z_ref, lines, bounds):
    rows, cols, dim = g_ref.shape
    row_low, row_high, col_low, col_high = bounds
    column = lax.broadcasted_iota(jnp.int32, (cols, 1), 0)
    inside = (column >= col_low) & (column < col_high)
    u = (g_ref[...] * gate).astype(BF).reshape(rows * cols, dim)
    product = jnp.dot(u, mix_ref[...], preferred_element_type=F32).reshape(rows, cols, dim)
    for k in range(rows):
        z = (rest_ref[k].astype(F32) + product[k]).astype(BF).astype(F32)
        keep = inside & (lines[k] >= row_low) & (lines[k] < row_high)
        z_ref[lines[k]] = jnp.where(keep, z, -jnp.inf)


def pooled_line(z_ref, line_ref, i, count):
    most = jnp.maximum(jnp.maximum(z_ref[2 * i], z_ref[2 * i + 1]), z_ref[2 * i + 2])
    groups = []
    for group in range(line_ref.shape[0]):
        line_ref[group] = most[:, 128 * group : 128 * group + 128]
        parts = [line_ref[group, pl.ds(s, count, stride=2), :] for s in range(3)]
        groups.append(jnp.maximum(jnp.maximum(parts[0], parts[1]), parts[2]))
    return jnp.concatenate(groups, axis=1)


def fill_sides(x_ref, left_ref, right_ref, before, after, padded, stage):
    high, wide, _ = x_ref.shape
    full = before + wide + after

    def line(r, _):
        padded[r, before : before + wide, :] = x_ref[r].astype(F32)
        return 0

    lax.fori_loop(0, high, line, 0)
    left, right = take_sides(left_ref, right_ref)
    stage[...] = left
    for r in range(high):
        padded[r, 0:before, :] = stage[r * before : r * before + before, :]
    stage[...] = right
    for r in range(high):
        padded[r, before + wide : full, :] = stage[r * before : r * before + after, :]


def inner_kernel(before, after, x_ref, l_ref, r_ref, kernel_ref, g_ref, rest_ref, part_ref, padded, stage):
    _, wide, _ = x_ref.shape
    step = g_ref.shape[0]
    turn = pl.program_id(0)

    @pl.when(turn == 0)
    def _():
        fill_sides(x_ref, l_ref, r_ref, before, after, padded, stage)
        part_ref[...] = jnp.zeros_like(part_ref)

    block = padded.at[pl.ds(turn * step, step + 2)]
    copy_centre(block, rest_ref)
    conv_gelu(block, kernel_ref, g_ref, (0, step), (before - 1, before - 1 + wide), part_ref)


def activate_inner(tile, left, right, kernels, level, before, after, step):
    high, wide, dim = tile.shape
    rows, cols = high - 2, round_up(wide + before + after - 2, 8)
    copies = lax.axis_size("tile")
    block = pl.BlockSpec((step, cols, dim), lambda i: (i, 0, 0))
    return pl.pallas_call(
        functools.partial(inner_kernel, before, after),
        grid=(rows // step,),
        in_specs=wholes(tile, left, right) + [at_level(kernels, level)],
        out_specs=[block, block, pl.BlockSpec((copies, 8, 128), lambda i: (0, 0, 0))],
        out_shape=[
            jax.ShapeDtypeStruct((rows, cols, dim), F32),
            jax.ShapeDtypeStruct((rows, cols, dim), BF),
            jax.ShapeDtypeStruct((copies, 8, 128), F32),
        ],
        scratch_shapes=[
            pltpu.VMEM((high, round_up(cols + 2, 8), dim), F32),
            pltpu.VMEM((max(left.shape[0], right.shape[0]), dim), F32),
        ],
        compiler_params=params(28 if level == 0 else 20),
        cost_estimate=cost(400 * rows * cols * dim, 6 * rows * cols * dim),
        name="activate_inner",
    )(tile, left, right, kernels)


def edge_kernel(high, before, after, top_ref, low_ref, l_ref, r_ref, a_ref, b_ref, kernel_ref, sum_ref, g_ref, rest_ref, part_ref, upper, lower, side_l, side_r, stage):
    wide = top_ref.shape[1]
    full = before + wide + after
    own = (before - 1, before - 1 + wide)
    side_l[...], side_r[...] = take_sides(l_ref, r_ref)

    def fill(padded, at, r, values):
        padded[at, 0:before, :] = side_l[r * before : r * before + before, :]
        padded[at, before : before + wide, :] = values.astype(F32)
        padded[at, before + wide : full, :] = side_r[r * before : r * before + after, :]

    for k in range(2):
        fill(upper, before + k, k, top_ref[k])
        fill(lower, k, high - 2 + k, low_ref[k])
    stage[: a_ref.shape[0], :] = a_ref[...].astype(F32)
    for k in range(before):
        upper[k, 0:full, :] = stage[k * full : k * full + full, :]
    stage[: b_ref.shape[0], :] = b_ref[...].astype(F32)
    for k in range(after):
        lower[2 + k, 0:full, :] = stage[k * full : k * full + full, :]
    part_ref[...] = sum_ref[...]
    up, low = pl.ds(0, before), pl.ds(before, after)
    copy_centre(upper, rest_ref.at[up])
    copy_centre(lower, rest_ref.at[low])
    conv_gelu(upper, kernel_ref, g_ref.at[up], (before - 1, before), own, part_ref)
    conv_gelu(lower, kernel_ref, g_ref.at[low], (0, 1), own, part_ref)


def activate_edge(tile, rims, kernels, part, level, before, after):
    high, wide, dim = tile.shape
    cols = round_up(wide + before + after - 2, 8)
    padded = round_up(cols + 2, 8)
    stage = max(r.shape[0] for r in rims)
    left, right, above, below = rims
    lines = before + after
    outs = [
        jax.ShapeDtypeStruct((lines, cols, dim), F32),
        jax.ShapeDtypeStruct((lines, cols, dim), BF),
        jax.ShapeDtypeStruct(part.shape, F32),
    ]
    return pl.pallas_call(
        functools.partial(edge_kernel, high, before, after),
        grid=(1,),
        in_specs=[
            pl.BlockSpec((2, wide, dim), lambda i: (0, 0, 0)),
            pl.BlockSpec((2, wide, dim), lambda i: (high // 2 - 1, 0, 0)),
        ]
        + wholes(*rims)
        + [at_level(kernels, level), whole(part)],
        out_specs=wholes(*outs),
        out_shape=outs,
        scratch_shapes=[
            pltpu.VMEM((before + 2, padded, dim), F32),
            pltpu.VMEM((after + 2, padded, dim), F32),
            pltpu.VMEM(left.shape, F32),
            pltpu.VMEM(right.shape, F32),
            pltpu.VMEM((stage, dim), F32),
        ],
        compiler_params=params(16),
        cost_estimate=cost(400 * lines * cols * dim, 6 * lines * cols * dim),
        name="activate_edge",
    )(tile, tile, *rims, kernels, part)


def mix0_kernel(cells, before, after, sums, red, exp, mix, g_ref, rest, g_edge, rest_edge, x_out, to_partner, to_cross, gates, z, line, keep_r, keep_l):
    step, cols, dim = g_ref.shape
    high, wide, _ = x_out.shape
    turn = pl.program_id(0)

    pos = position()
    bounds = (jnp.where(pos[0] == 0, 1, 0), z.shape[0], jnp.where(pos[1] == 0, 1, 0), cols)

    @pl.when(turn == 0)
    def _():
        gates[...] = jnp.broadcast_to(gate_row(sums, cells, red, exp), gates.shape)
        keep_l[...] = jnp.zeros_like(keep_l)
        mix_lines(g_edge, gates[:1, :], mix, rest_edge, z, (0, 1, z.shape[0] - 1), bounds)

    mix_lines(g_ref, gates[:1, :], mix, rest, z, [2 + turn * step + k for k in range(step)], bounds)

    @pl.when(turn == pl.num_programs(0) - 1)
    def _():
        for i in range(high):
            out = pooled_line(z, line, i, wide)
            x_out[i] = out.astype(BF)
            keep_r[i * before : i * before + before, :] = out[wide - before :]
            keep_l[i * before : i * before + after, :] = out[:after]
        give_sides(keep_r, keep_l, to_partner, to_cross)


def level_specs(sums, red, exp, mix, level):
    return [whole(sums), at_level(red, level), at_level(exp, level), at_level(mix, level)]


def mix0(sums, red, exp, mix, g, rest, edges, cells, high, wide, before, after, step):
    rows, cols, dim = g.shape
    block = pl.BlockSpec((step, cols, dim), lambda i: (i, 0, 0))
    outs = [
        jax.ShapeDtypeStruct((high, wide, dim), BF),
        jax.ShapeDtypeStruct((high * before, dim), BF),
        jax.ShapeDtypeStruct((high * before, dim), BF),
    ]
    return pl.pallas_call(
        functools.partial(mix0_kernel, cells, before, after),
        grid=(rows // step,),
        in_specs=level_specs(sums, red, exp, mix, 0) + [block, block] + wholes(*edges),
        out_specs=wholes(*outs),
        out_shape=outs,
        scratch_shapes=[
            pltpu.VMEM((8, dim), F32),
            pltpu.VMEM((rows + 3, cols, dim), F32),
            pltpu.VMEM((dim // 128, cols, 128), F32),
            pltpu.VMEM((high * before, dim), F32),
            pltpu.VMEM((high * before, dim), F32),
        ],
        compiler_params=params(32),
        cost_estimate=cost(2 * rows * cols * dim * dim, 6 * rows * cols * dim),
        name="mix0",
    )(sums, red, exp, mix, g, rest, *edges)


def mix1_kernel(cells, size, before, sums, red, exp, mix, g_ref, rest, g_edge, rest_edge, kernel, g_out, rest_out, part, z, line, padded):
    rows, cols, dim = g_ref.shape
    side_r, side_c, map_side = size
    gate = gate_row(sums, cells, red, exp)
    shift = before - 1
    pos = position()
    row_low = shift - pos[0] * side_r
    col_low = shift - pos[1] * side_c
    bounds = (row_low, row_low + map_side, col_low, col_low + map_side)
    inner = range(before, before + rows)
    mix_lines(g_ref, gate, mix, rest, z, inner, bounds)
    mix_lines(g_edge, gate, mix, rest_edge, z, [k for k in range(z.shape[0]) if k not in inner], bounds)
    count_r, count_c = padded.shape[0], (cols - 1) // 2
    row_two = 2 - pos[0] * (side_r // 2)
    col_two = 2 - pos[1] * (side_c // 2)
    column = lax.broadcasted_iota(jnp.int32, (count_c, 1), 0)
    inside = (column >= col_two) & (column < col_two + map_side // 2)
    for i in range(count_r):
        out = pooled_line(z, line, i, count_c)
        keep = inside & (i >= row_two) & (i < row_two + map_side // 2)
        padded[i, 0:count_c, :] = jnp.where(keep, out, 0.0)
    copy_centre(padded, rest_out)
    part[...] = jnp.zeros_like(part)
    conv_gelu(padded, kernel, g_out, (1, 1 + side_r // 2), (1, 1 + side_c // 2), part)


def mix1(sums, red, exp, mix, g, rest, edges, kernels, cells, size, before):
    rows, cols, dim = g.shape
    rows += edges[0].shape[0]
    out_rows, out_cols = (rows - 1) // 2 - 2, round_up((cols - 1) // 2 - 2, 8)
    outs = [
        jax.ShapeDtypeStruct((out_rows, out_cols, dim), F32),
        jax.ShapeDtypeStruct((out_rows, out_cols, dim), BF),
        jax.ShapeDtypeStruct(sums.shape, F32),
    ]
    return pl.pallas_call(
        functools.partial(mix1_kernel, cells, size, before),
        grid=(1,),
        in_specs=level_specs(sums, red, exp, mix, 1) + wholes(g, rest, *edges) + [at_level(kernels, 2)],
        out_specs=wholes(*outs),
        out_shape=outs,
        scratch_shapes=[
            pltpu.VMEM((rows, cols, dim), F32),
            pltpu.VMEM((dim // 128, cols, 128), F32),
            pltpu.VMEM((out_rows + 2, round_up(out_cols + 2, 8), dim), F32),
        ],
        compiler_params=params(18),
        cost_estimate=cost(2 * rows * cols * dim * dim, 6 * rows * cols * dim),
        name="mix1",
    )(sums, red, exp, mix, g, rest, *edges, kernels)


def mix2_kernel(cells, high, wide, sums, red, exp, mix, g_ref, rest, x_out, z, line, keep):
    rows, cols, dim = g_ref.shape
    gate = gate_row(sums, cells, red, exp)
    pos = position()
    bounds = (jnp.where(pos[0] == 0, 1, 0), rows, jnp.where(pos[1] == 0, 1, 0), cols)
    mix_lines(g_ref, gate, mix, rest, z, range(rows), bounds)
    for i in range(high):
        keep[i * wide : i * wide + wide, :] = pooled_line(z, line, i, wide)
    x_out[...] = jnp.broadcast_to(keep[...].astype(BF), x_out.shape)


def mix2(sums, red, exp, mix, g, rest, cells, high, wide, copies):
    rows, cols, dim = g.shape
    out = jax.ShapeDtypeStruct((copies, high * wide, dim), BF)
    return pl.pallas_call(
        functools.partial(mix2_kernel, cells, high, wide),
        grid=(1,),
        in_specs=level_specs(sums, red, exp, mix, 2) + wholes(g, rest),
        out_specs=whole(out),
        out_shape=out,
        scratch_shapes=[
            pltpu.VMEM((rows, cols, dim), F32),
            pltpu.VMEM((dim // 128, cols, 128), F32),
            pltpu.VMEM((high * wide, dim), F32),
        ],
        compiler_params=params(10),
        cost_estimate=cost(2 * rows * cols * dim * dim, 6 * rows * cols * dim),
        name="mix2",
    )(sums, red, exp, mix, g, rest)


def everyones(copies):
    return lax.all_to_all(copies, "tile", 0, 0, tiled=True)


def query_slab(tile_map, dw_kernel, se_reduce, se_expand, mix_weight, keys_of):
    high, wide, dim = tile_map.shape
    tiles = lax.axis_size("tile")
    cells = high * wide * tiles
    group = 2 * TILE_COLS
    def inner(tile, level, sides, held, *halos):
        return activate_inner(after_these(tile, held), *sides, dw_kernel, level, *halos)

    rims, (kt0, vt0), (g, rest, part) = exchange_rims(
        tile_map,
        side_pieces(tile_map, 2, 1),
        2,
        1,
        lambda held: keys_of(0, held),
        lambda sides, held: inner(tile_map, 0, sides, held, 2, 1, 10),
    )
    *edges, part = activate_edge(tile_map, rims, dw_kernel, part, 0, 2, 1)
    coarse, *sides = mix0(
        everyones(part), se_reduce, se_expand, mix_weight, g, rest, edges, cells, high // 2, wide // 2, 6, 3, 10
    )

    rims, (kt1, vt1), (g, rest, part) = exchange_rims(
        coarse,
        sides,
        6,
        3,
        lambda held: keys_of(1, held),
        lambda sides, held: inner(coarse, 1, sides, held, 6, 3, high // 2 - 2),
    )
    *edges, part = activate_edge(coarse, rims, dw_kernel, part, 1, 6, 3)
    size = (high // 2, wide // 2, high // 2 * (tiles // TILE_COLS))
    g, rest, part = mix1(
        everyones(part), se_reduce, se_expand, mix_weight, g, rest, edges, dw_kernel, cells // 4, size, 6
    )
    query = mix2(
        everyones(part), se_reduce, se_expand, mix_weight, g, rest, cells // 16, high // 8, wide // 8, group
    )
    groups = [list(range(group * x, group * x + group)) for x in range(tiles // group)]
    slab = lax.all_to_all(query, "tile", 0, 0, tiled=True, axis_index_groups=groups)
    return slab.reshape(-1, dim), (kt0, kt1), (vt0, vt1)


def body(
    features,
    dw_kernel,
    se_reduce,
    se_expand,
    mix_weight,
    norm_gain,
    kv_weight,
    kv_bias,
    proj_weight,
    proj_bias,
):
    tile_map = features[0]
    se_reduce = jnp.swapaxes(se_reduce, 1, 2)

    def keys_of(window, held):
        return keys_values(after_these(tile_map, held), norm_gain, kv_weight, kv_bias, window)

    slab, keys, values = query_slab(tile_map, dw_kernel, se_reduce, se_expand, mix_weight, keys_of)
    tiles = lax.axis_size("tile")
    group = 2 * TILE_COLS
    def from_x(value, step):
        return lax.ppermute(value, "tile", [(t, t ^ group * step) for t in range(tiles)])

    near = [from_x(slab, 1), from_x(slab, 3)]
    rest = (keys, values, tile_map, proj_weight, proj_bias)
    out = attention((0,), [slab], *rest)
    far, out = lax.optimization_barrier((slab, out))
    far = from_x(far, 2)
    out = attention((1, 3), near, *rest, out)
    return attention((2,), [far], *rest, out)[None]


def solution(mesh):
    in_specs = (P(("scene", "tile"), None, None, None), P(), P(), P(), P(), P(), P(), P(), P(), P())
    out_specs = P(("scene", "tile"), None, None, None)
    return jax.shard_map(body, mesh=mesh, in_specs=in_specs, out_specs=out_specs, check_vma=False)
```
